32 devices in a mesh: cells: 8 (over z, y), seq: 4 (over x, core).
Axes of the slice: x: 2, y: 2, z: 4, core: 2. Of those that a mesh axis runs over, the one named last changes fastest.
Arguments:
- tokens: bfloat16 [16, 1024, 1120], P('cells', 'seq'), may hold values from -6 to 6
- first_gain: float32 [1120], replicated, may hold values from 0.1 to 1.9
- first_shift: float32 [1120], replicated, may hold values from -1.8 to 1.8
- mix_weight: bfloat16 [1120, 3360], replicated, may hold values from -0.1875 to 0.1875
- query_bias: float32 [1120], replicated, may hold values from -1.8 to 1.8
- value_bias: float32 [1120], replicated, may hold values from -1.8 to 1.8
- out_weight: bfloat16 [1120, 1120], replicated, may hold values from -1.5 to 1.5
- out_bias: float32 [1120], replicated, may hold values from -1.8 to 1.8
- second_gain: float32 [1120], replicated, may hold values from 0.1 to 1.9
- second_shift: float32 [1120], replicated, may hold values from -1.8 to 1.8
- up_weight: bfloat16 [1120, 4480], replicated, may hold values from -0.1875 to 0.1875
- up_bias: float32 [4480], replicated, may hold values from -1.8 to 1.8
- down_weight: bfloat16 [4480, 1120], replicated, may hold values from -0.09375 to 0.09375
- down_bias: float32 [1120], replicated, may hold values from -1.8 to 1.8
- cotangent: bfloat16 [16, 1024, 1120], P('cells', 'seq'), may hold values from -6 to 6
- prefix_lengths: int32 [16], P('cells'), may hold values from 1 to 8, as said below
- gene_counts: int32 [16], P('cells'), may hold values from 200 to 1023, as said below
- key_mask: int32 [16, 1024], P('cells', 'seq'), may hold values 0 or 1
Outputs:
- block_out: bfloat16 [16, 1024, 1120], P('cells', 'seq')
- tokens_gradient: bfloat16 [16, 1024, 1120], P('cells', 'seq')
- first_gain_gradient: float32 [1120], P('cells')
- first_shift_gradient: float32 [1120], P('cells')
- mix_weight_gradient: float32 [1120, 3360], P('cells', 'seq')
- query_bias_gradient: float32 [1120], P('cells')
- value_bias_gradient: float32 [1120], P('cells')
- out_weight_gradient: float32 [1120, 1120], P('cells', 'seq')
- out_bias_gradient: float32 [1120], P('cells')
- second_gain_gradient: float32 [1120], P('cells')
- second_shift_gradient: float32 [1120], P('cells')
- up_weight_gradient: float32 [1120, 4480], P('cells', 'seq')
- up_bias_gradient: float32 [4480], P('cells')
- down_weight_gradient: float32 [4480, 1120], P('cells', 'seq')
- down_bias_gradient: float32 [1120], P('cells')
The draws below stay inside these ranges and needn't reach their ends.
Inputs may be any that keep to these rules, and one draw needn't show every extreme that they name: `prefix_lengths`: at most 8; cell 0 has 8. `gene_counts`: prefix plus genes is at most 1024; among cells k * 2 to (k+1) * 2 - 1, for every k, one cell's prefix plus genes exceeds 1024 - 1024 // 4; in the last such group that cell fills all 1024 positions.
All inputs are finite; a program needn't handle non-finite values. No bound on the sum of `key_mask` on one device may be relied on, other than what follows from the above.
Results may differ from the reference program's by a relative error of at most 0.025.
Values may be sent and summed in bfloat16 or wider, within the bound.
No kernel may reach another device: no remote copies, remote signals or barrier semaphores. Data moves between devices by JAX's collectives and lax.ppermute only.
A program may use at most 320 MiB of HBM per device.

```python
import math
import jax
import jax.numpy as jnp
from jax import lax

D = 1120
HEADS = 20
HD = 56
FF = 4480
LEN = 1024
CELLS_DEV = 2
PMAX = 8
GMIN = 200
NCELLS = 16
N_SEQ = 4


def cell_lengths(key):
    prefix = jax.random.randint(jax.random.fold_in(key, 11), (NCELLS,), 1, PMAX + 1)
    spread = jax.random.randint(jax.random.fold_in(key, 12), (NCELLS,), 0, 256)
    pick = jax.random.randint(jax.random.fold_in(key, 13), (NCELLS // CELLS_DEV,), 0, CELLS_DEV)
    reach = jax.random.randint(jax.random.fold_in(key, 14), (NCELLS,), LEN - LEN // N_SEQ + 1, LEN + 1)
    places = jnp.arange(NCELLS)
    owner = places // CELLS_DEV
    slot = places % CELLS_DEV
    full = slot == pick[owner]
    last_full = full & (owner == NCELLS // CELLS_DEV - 1)
    prefix = jnp.where(last_full, 1, prefix)
    prefix = prefix.at[0].set(PMAX)
    reach = jnp.where(last_full, LEN, reach)
    tail = spread * spread // 256
    tail = tail * spread // 256
    room = LEN - prefix - GMIN
    genes = GMIN + tail * room // 256
    genes = jnp.where(full, reach - prefix, genes)
    return (prefix.astype(jnp.int32), genes.astype(jnp.int32))


def draw_prefix_lengths(key, part):
    return cell_lengths(key)[0]


def draw_gene_counts(key, part):
    return cell_lengths(key)[1]


def set_ends(values, own_key, least, largest):
    shape = values.shape
    index_at = [jax.random.randint(jax.random.fold_in(own_key, axis), (), 0, shape[axis]) for axis in range(len(shape))]
    values = values.at[tuple(index_at)].set(least)
    longest = shape.index(max(shape))
    index_at[longest] = (index_at[longest] + 1) % shape[longest]
    return values.at[tuple(index_at)].set(largest)


def steps_of(key, shape, split, low, largest):
    level, own = 1.0, jax.random.fold_in(key, 6)
    for position, shards_of in split:
        heights = jnp.exp(jax.random.uniform(jax.random.fold_in(own, position), (shards_of,), jnp.float32, low / len(split), largest / len(split)))
        level = level * jnp.repeat(heights, shape[position] // shards_of).reshape([-1 if axis == position else 1 for axis in range(len(shape))])
    return level


def bell_draw(key, dims, width, bound, shards=(), kind=jnp.bfloat16):
    values = width * jax.random.normal(key, dims, jnp.float32)
    if shards:
        values = values * steps_of(key, dims, shards, -0.22, 0.18)
    return jnp.clip(values, -bound, bound).astype(kind)


def setup_inputs(seed: int = 0) -> dict:
    key_of = jax.random.split(jax.random.key(seed), 19)
    return {
        "tokens": bell_draw(key_of[0], (NCELLS, LEN, D), 1.0, 6.0, ((0, 8), (1, 4))),
        "first_gain": jnp.clip(1.0 + 0.18 * jax.random.normal(key_of[1], (D,), jnp.float32), 0.1, 1.9),
        "first_shift": bell_draw(key_of[2], (D,), 0.3, 1.8, (), jnp.float32),
        "mix_weight": bell_draw(key_of[3], (D, 3 * D), D ** -0.5, 0.1875),
        "query_bias": bell_draw(key_of[4], (D,), 0.3, 1.8, (), jnp.float32),
        "value_bias": bell_draw(key_of[5], (D,), 0.3, 1.8, (), jnp.float32),
        "out_weight": bell_draw(key_of[6], (D, D), (max(D // 64, 1)) ** -0.5, 1.5),
        "out_bias": bell_draw(key_of[7], (D,), 0.3, 1.8, (), jnp.float32),
        "second_gain": jnp.clip(1.0 + 0.18 * jax.random.normal(key_of[8], (D,), jnp.float32), 0.1, 1.9),
        "second_shift": bell_draw(key_of[9], (D,), 0.3, 1.8, (), jnp.float32),
        "up_weight": bell_draw(key_of[10], (D, FF), D ** -0.5, 0.1875),
        "up_bias": bell_draw(key_of[11], (FF,), 0.3, 1.8, (), jnp.float32),
        "down_weight": bell_draw(key_of[12], (FF, D), FF ** -0.5, 0.09375),
        "down_bias": bell_draw(key_of[13], (D,), 0.3, 1.8, (), jnp.float32),
        "cotangent": bell_draw(key_of[14], (NCELLS, LEN, D), 1.0, 6.0, ((0, 8), (1, 4))),
        "prefix_lengths": draw_prefix_lengths(jax.random.fold_in(key_of[18], 71), 0),
        "gene_counts": draw_gene_counts(jax.random.fold_in(key_of[18], 71), 0),
        "key_mask": set_ends((jax.random.randint(key_of[17], (NCELLS, LEN), 0, 8) < 7).astype(jnp.int32), jax.random.fold_in(key_of[17], 1), 0, 1),
    }


@jax.custom_vjp
def low(v):
    return lax.optimization_barrier(v.astype(jnp.bfloat16)).astype(jnp.float32)

@jax.custom_vjp
def low_back(v):
    return v

def low_keep(v):
    return (low(v), None)

def low_pass(kept, grad):
    return (grad,)

def back_keep(v):
    return (v, None)

def back_low(kept, grad):
    return (low(grad),)
low.defvjp(low_keep, low_pass)
low_back.defvjp(back_keep, back_low)

def layer_norm(values, gain, shift):
    centre = lax.optimization_barrier(jnp.mean(values, axis=-1, keepdims=True))
    centred = values - centre
    spread = lax.optimization_barrier(jnp.mean(centred * centred, axis=-1, keepdims=True))
    return centred * lax.rsqrt(spread + 1e-05) * gain + shift

def attend_cell(block):
    queries, keys, values, prefix, total, keeps = block
    scale = 1.0 / math.sqrt(HD)
    raw = jnp.einsum('qhe,khe->hqk', queries, keys, precision=lax.Precision.HIGHEST) * scale
    places = jnp.arange(LEN)
    rows = places[:, None]
    cols = places[None, :]
    open_key = (cols < total) & (keeps[None, :] == 1) & ((cols <= rows) | (cols < prefix))
    seen = open_key | (cols == rows)
    scores = low_back(jnp.where(seen[None], raw, -1e+30))
    top = lax.optimization_barrier(jnp.max(scores, axis=-1, keepdims=True))
    raised = jnp.exp(scores - top)
    probs = low(raised / lax.optimization_barrier(jnp.sum(raised, axis=-1, keepdims=True)))
    return jnp.einsum('hqk,khe->qhe', probs, values, precision=lax.Precision.HIGHEST)

def forward(params, inputs, prefixes, totals, keeps):
    first_gain, first_shift, mix_weight, query_bias, value_bias, out_weight, out_bias, second_gain, second_shift, up_weight, up_bias, down_weight, down_bias = params
    high = lax.Precision.HIGHEST
    normed = low(layer_norm(inputs, first_gain, first_shift))
    mixed = jnp.einsum('gtd,de->gte', normed, mix_weight, precision=high)
    queries = low_back(low(mixed[..., :D] + query_bias))
    keys = low_back(low(mixed[..., D:2 * D]))
    values = low_back(low(mixed[..., 2 * D:] + value_bias))
    shape = (inputs.shape[0], LEN, HEADS, HD)
    attended = lax.map(jax.checkpoint(attend_cell), (queries.reshape(shape), keys.reshape(shape), values.reshape(shape), prefixes, totals, keeps))
    attended = low_back(low(attended.reshape(inputs.shape)))
    branch = low_back(jnp.einsum('gtd,de->gte', attended, out_weight, precision=high) + out_bias)
    middle = inputs + branch
    second = low(layer_norm(middle, second_gain, second_shift))
    upper = low_back(jnp.einsum('gtd,df->gtf', second, up_weight, precision=high) + up_bias)
    active = low(jax.nn.gelu(upper, approximate=True))
    return middle + jnp.einsum('gtf,fd->gtd', active, down_weight, precision=high) + down_bias

def reference(tokens, first_gain, first_shift, mix_weight, query_bias, value_bias, out_weight, out_bias, second_gain, second_shift, up_weight, up_bias, down_weight, down_bias, cotangent, prefix_lengths, gene_counts, key_mask):
    params = tuple((item.astype(jnp.float32) for item in (first_gain, first_shift, mix_weight, query_bias, value_bias, out_weight, out_bias, second_gain, second_shift, up_weight, up_bias, down_weight, down_bias)))
    group = math.gcd(NCELLS, 4)
    rounds = NCELLS // group

    def one_round(sums, block):
        inputs, back_out, prefixes, genes, keeps = block

        def run(params_in, inputs_in):
            return forward(params_in, inputs_in, prefixes, prefixes + genes, keeps)
        result, pull = jax.vjp(run, params, inputs.astype(jnp.float32))
        grads, back_inputs = pull(back_out.astype(jnp.float32))
        sums = jax.tree.map(lambda left, right: left + right, sums, grads)
        return (sums, (result.astype(jnp.bfloat16), back_inputs.astype(jnp.bfloat16)))
    blocks = (tokens.reshape(rounds, group, LEN, D), cotangent.reshape(rounds, group, LEN, D), prefix_lengths.reshape(rounds, group), gene_counts.reshape(rounds, group), key_mask.reshape(rounds, group, LEN))
    zeros = tuple((jnp.zeros_like(item) for item in params))
    sums, (results, backs) = lax.scan(one_round, zeros, blocks)
    return (results.reshape(NCELLS, LEN, D), backs.reshape(NCELLS, LEN, D), sums[0], sums[1], sums[2], sums[3], sums[4], sums[5], sums[6], sums[7], sums[8], sums[9], sums[10], sums[11], sums[12])
```

```python
from functools import partial
import math

import jax
import jax.numpy as jnp
from jax import lax
from jax.experimental import pallas as pl
from jax.experimental.pallas import tpu as pltpu
from jax.sharding import PartitionSpec as P

HEADS = 20
VMEM_LIMIT = 56 * 1024 * 1024


def bits_of(count):
    return [1 << b for b in range(count.bit_length() - 1)]


def swap_with(array, axis, bit):
    count = lax.axis_size(axis)
    return lax.ppermute(array, axis, [(i, i ^ bit) for i in range(count)])


def spread_bits(array, seq_count, cell_count):
    seq_bits, cell_bits = len(bits_of(seq_count)), len(bits_of(cell_count))
    return array.reshape((2,) * (seq_bits + cell_bits) + array.shape[2:])


def halve(part, names, axis, bit):
    place = names.index((axis, bit))
    keep = lax.index_in_dim(part, 0, place, keepdims=False)
    send = lax.index_in_dim(part, 1, place, keepdims=False)
    got = swap_with(send, axis, bit)
    total = (keep.astype(jnp.float32) + got.astype(jnp.float32)).astype(jnp.bfloat16)
    return total, names[:place] + names[place + 1 :]


def bit_names(seq_count, cell_count):
    return [("seq", b) for b in reversed(bits_of(seq_count))] + [
        ("cells", b) for b in reversed(bits_of(cell_count))
    ]


def row_cover(rows, count):
    share = rows // count
    starts = [share * c // 8 * 8 for c in range(count)]
    height = max(share * (c + 1) - starts[c] for c in range(count))
    height = -(-height // 16) * 16
    return [min(s, rows - height) for s in starts], height


def outer_rows_kernel(starts, height, half, me_ref, left_ref, right_ref, send_ref, keep_ref, turned):
    step = pl.program_id(0)

    @pl.when(step == 0)
    def _():
        turned[...] = left_ref[...].T

    mine = me_ref[1]
    width = right_ref.shape[-1]
    for first in range(0, width, 256):
        last = min(first + 256, width)
        block = jnp.dot(
            turned[...], right_ref[0, :, first:last], preferred_element_type=jnp.float32
        )

        def store(target):
            for c, start in enumerate(starts):
                target[0, c ^ mine, :, first:last] = block[start : start + height].astype(
                    jnp.bfloat16
                )

        pl.when(step < half)(lambda: store(send_ref))
        pl.when(step >= half)(lambda: store(keep_ref))


def outer_rows(left, right, cell_count, me):
    seq_count, rows, width = right.shape
    starts, height = row_cover(left.shape[1], cell_count)
    half = seq_count // 2

    def rel(step):
        return jnp.where(step < half, 2 * step + 1, 2 * (step - half))

    block = (1, cell_count, height, width)
    shape = jax.ShapeDtypeStruct((half, cell_count, height, width), jnp.bfloat16)
    return pl.pallas_call(
        partial(outer_rows_kernel, starts, height, half),
        out_shape=(shape, shape),
        grid_spec=pltpu.PrefetchScalarGridSpec(
            num_scalar_prefetch=1,
            grid=(seq_count,),
            in_specs=[
                pl.BlockSpec(left.shape, lambda g, me: (0, 0)),
                pl.BlockSpec((1, rows, width), lambda g, me: (rel(g) ^ me[0], 0, 0)),
            ],
            out_specs=[
                pl.BlockSpec(block, lambda g, me: (jnp.minimum(g, half - 1), 0, 0, 0)),
                pl.BlockSpec(block, lambda g, me: (jnp.maximum(g - half, 0), 0, 0, 0)),
            ],
            scratch_shapes=[pltpu.VMEM((left.shape[1], rows), jnp.bfloat16)],
        ),
        compiler_params=pltpu.CompilerParams(vmem_limit_bytes=VMEM_LIMIT),
        cost_estimate=pl.CostEstimate(
            flops=2 * rows * left.shape[1] * width * seq_count,
            bytes_accessed=2 * (left.size + right.size + 2 * shape.size),
            transcendentals=0,
        ),
        name="outer_rows",
    )(me, left, right)


def outer_columns_kernel(share, seq_count, me_ref, left_ref, right_ref, send_ref, keep_ref, turned):
    @pl.when(pl.program_id(0) == 0)
    def _():
        turned[...] = left_ref[...].T

    mine = me_ref[0]
    block = jnp.dot(turned[...], right_ref[0], preferred_element_type=jnp.float32)
    for s in range(seq_count):
        rel = s ^ mine
        piece = block[s * share : (s + 1) * share].astype(jnp.bfloat16)

        def store(target):
            target[rel >> 1, 0] = piece

        pl.when((rel & 1) == 1)(lambda: store(send_ref))
        pl.when((rel & 1) == 0)(lambda: store(keep_ref))


def outer_columns(left, right, seq_count, me):
    cell_count, rows, width = right.shape
    share = left.shape[1] // seq_count
    half = seq_count // 2
    block = (half, 1, share, width)
    shape = jax.ShapeDtypeStruct((half, cell_count, share, width), jnp.bfloat16)
    return pl.pallas_call(
        partial(outer_columns_kernel, share, seq_count),
        out_shape=(shape, shape),
        grid_spec=pltpu.PrefetchScalarGridSpec(
            num_scalar_prefetch=1,
            grid=(cell_count,),
            in_specs=[
                pl.BlockSpec(left.shape, lambda g, me: (0, 0)),
                pl.BlockSpec((1, rows, width), lambda g, me: (g ^ me[1], 0, 0)),
            ],
            out_specs=[
                pl.BlockSpec(block, lambda g, me: (0, g, 0, 0)),
                pl.BlockSpec(block, lambda g, me: (0, g, 0, 0)),
            ],
            scratch_shapes=[pltpu.VMEM((left.shape[1], rows), jnp.bfloat16)],
        ),
        compiler_params=pltpu.CompilerParams(vmem_limit_bytes=VMEM_LIMIT),
        cost_estimate=pl.CostEstimate(
            flops=2 * rows * left.shape[1] * width * cell_count,
            bytes_accessed=2 * (left.size + right.size + 2 * shape.size),
            transcendentals=0,
        ),
        name="outer_columns",
    )(me, left, right)


def columns_cut(array, count):
    rows, width = array.shape
    return array.reshape(rows, count, width // count).transpose(1, 0, 2)


def scattered_sum(send, keep, seq_count, cell_count, order):
    got = swap_with(send, "seq", 1)
    part = (keep.astype(jnp.float32) + got.astype(jnp.float32)).astype(jnp.bfloat16)
    part = spread_bits(part, seq_count // 2, cell_count)
    names = bit_names(seq_count, cell_count)
    names.remove(("seq", 1))
    for axis, bit in order(names):
        part, names = halve(part, names, axis, bit)
    return part


def seq_first(names):
    return sorted([n for n in names if n[0] == "seq"]) + sorted(n for n in names if n[0] == "cells")


def seq_last(names):
    cells = sorted(n for n in names if n[0] == "cells")
    return cells + sorted(n for n in names if n[0] == "seq")


def seq_second(names):
    cells = sorted(n for n in names if n[0] == "cells")
    return cells[:1] + sorted(n for n in names if n[0] == "seq") + cells[1:]


def layer_norm(values, gain, shift):
    centre = jnp.mean(values, axis=-1, keepdims=True)
    centred = values - centre
    spread = jnp.mean(centred * centred, axis=-1, keepdims=True)
    return centred * lax.rsqrt(spread + 1e-05) * gain + shift


def on_device(
    tokens,
    first_gain,
    first_shift,
    mix_weight,
    query_bias,
    value_bias,
    out_weight,
    out_bias,
    second_gain,
    second_shift,
    up_weight,
    up_bias,
    down_weight,
    down_bias,
    cotangent,
    prefix_lengths,
    gene_counts,
    key_mask,
):
    cells_here, span, width = tokens.shape
    head_size = width // HEADS
    length = span * lax.axis_size("seq")
    start = lax.axis_index("seq") * span
    seq_count, cell_count = lax.axis_size("seq"), lax.axis_size("cells")
    me = jnp.stack([lax.axis_index("seq"), lax.axis_index("cells")]).astype(jnp.int32)
    group = math.gcd(cells_here, max(1, 512 // span))
    blocks = cells_here // group
    scale = 1.0 / math.sqrt(head_size)
    totals = prefix_lengths + gene_counts
    row_count = cells_here * span
    own_rows = start + jnp.arange(span)
    every_row = jnp.arange(length)

    def cut(array):
        return array.reshape((blocks, group) + array.shape[1:])

    def split_heads(array):
        return array.reshape(array.shape[:2] + (HEADS, head_size))

    def flat(array):
        return array.reshape(row_count, array.shape[-1])

    def score_block(queries, keys, prefix, total, keeps, row_places, key_places):
        raw = (
            jnp.einsum("gqhe,gkhe->ghqk", queries, keys, preferred_element_type=jnp.float32) * scale
        )
        places = key_places[None, None, :]
        rows = row_places[None, :, None]
        open_key = (
            (places < total[:, None, None])
            & keeps[:, None, :]
            & ((places <= rows) | (places < prefix[:, None, None]))
        )
        seen = open_key | (places == rows)
        return jnp.where(seen[:, None], raw, -1e30)

    def scores_back(scores, log_sum, back_heads, values):
        probs = jnp.exp(scores - log_sum[..., None])
        back_probs = jnp.einsum(
            "gqhe,gkhe->ghqk", back_heads, values, preferred_element_type=jnp.float32
        )
        return (probs, back_probs)

    inputs = tokens.astype(jnp.float32)
    normed = layer_norm(inputs, first_gain, first_shift).astype(jnp.bfloat16)
    mixed = jnp.dot(normed, mix_weight, preferred_element_type=jnp.float32)
    queries = (mixed[..., :width] + query_bias).astype(jnp.bfloat16)
    keys_low = mixed[..., width : 2 * width].astype(jnp.bfloat16)
    values_low = (mixed[..., 2 * width :] + value_bias).astype(jnp.bfloat16)
    all_keys, all_values, all_mask = (
        lax.all_gather(keys_low, "seq", axis=1, tiled=True),
        lax.all_gather(values_low, "seq", axis=1, tiled=True),
        lax.all_gather(key_mask.astype(jnp.bfloat16), "seq", axis=1, tiled=True),
    )
    keeps = all_mask > 0.5
    query_heads = cut(split_heads(queries))
    key_heads = cut(split_heads(all_keys))
    value_heads = cut(split_heads(all_values))
    prefix_blocks = cut(prefix_lengths)
    total_blocks = cut(totals)
    keep_blocks = cut(keeps)

    def attend_forward(block):
        query, keys, values, prefix, total, keep = block
        scores = score_block(query, keys, prefix, total, keep, own_rows, every_row)
        top = jnp.max(scores, axis=-1, keepdims=True)
        raised = jnp.exp(scores - top)
        summed = jnp.sum(raised, axis=-1, keepdims=True)
        probs = (raised / summed).astype(jnp.bfloat16)
        result = jnp.einsum("ghqk,gkhe->gqhe", probs, values, preferred_element_type=jnp.float32)
        return (result.astype(jnp.bfloat16), (top + jnp.log(summed))[..., 0])

    attended, log_sums = lax.map(
        attend_forward,
        (query_heads, key_heads, value_heads, prefix_blocks, total_blocks, keep_blocks),
    )
    attended = attended.reshape(cells_here, span, width)
    middle = inputs + (jnp.dot(attended, out_weight, preferred_element_type=jnp.float32) + out_bias)
    second = layer_norm(middle, second_gain, second_shift).astype(jnp.bfloat16)
    upper = jnp.dot(second, up_weight, preferred_element_type=jnp.float32) + up_bias
    gelu_tanh = partial(jax.nn.gelu, approximate=True)
    active = gelu_tanh(upper).astype(jnp.bfloat16)
    result = middle + jnp.dot(active, down_weight, preferred_element_type=jnp.float32) + down_bias
    block_out = result.astype(jnp.bfloat16)
    back_out = cotangent.astype(jnp.float32)
    down_bias_back = jnp.sum(flat(back_out), axis=0)
    back_active = jnp.einsum(
        "ctd,fd->ctf", cotangent, down_weight, preferred_element_type=jnp.float32
    )
    gelu_value, gelu_pull = jax.vjp(gelu_tanh, upper)
    back_upper = gelu_pull(back_active)[0].astype(jnp.bfloat16)
    down_shares = outer_columns(flat(cotangent), columns_cut(flat(active), cell_count), seq_count, me)
    up_shares = outer_rows(flat(second), columns_cut(flat(back_upper), seq_count), cell_count, me)
    down_part = scattered_sum(*down_shares, seq_count, cell_count, seq_first)
    up_part = scattered_sum(*up_shares, seq_count, cell_count, seq_last)
    up_bias_back = jnp.sum(flat(back_upper).astype(jnp.float32), axis=0)
    back_second = jnp.einsum(
        "ctf,df->ctd", back_upper, up_weight, preferred_element_type=jnp.float32
    )
    norm_value, norm_pull = jax.vjp(layer_norm, middle, second_gain, second_shift)
    middle_part, second_gain_back, second_shift_back = norm_pull(back_second)
    back_middle = back_out + middle_part
    back_branch = back_middle.astype(jnp.bfloat16)
    out_shares = outer_rows(
        flat(attended), columns_cut(flat(back_branch), seq_count), cell_count, me
    )
    out_part = scattered_sum(*out_shares, seq_count, cell_count, seq_second)
    out_bias_back = jnp.sum(flat(back_branch).astype(jnp.float32), axis=0)
    back_attended = jnp.einsum(
        "cte,de->ctd", back_branch, out_weight, preferred_element_type=jnp.float32
    ).astype(jnp.bfloat16)
    back_blocks = cut(split_heads(back_attended))

    def attend_backward(block):
        query, keys, values, prefix, total, keep, log_sum, back_heads = block
        scores = score_block(query, keys, prefix, total, keep, own_rows, every_row)
        probs, back_probs = scores_back(scores, log_sum, back_heads, values)
        probs_low = probs.astype(jnp.bfloat16)
        values_back = jnp.einsum(
            "ghqk,gqhe->gkhe", probs_low, back_heads, preferred_element_type=jnp.float32
        )
        centre = jnp.sum(back_probs * probs, axis=-1, keepdims=True)
        back_scores = (probs * (back_probs - centre)).astype(jnp.bfloat16)
        query_back = (
            jnp.einsum("ghqk,gkhe->gqhe", back_scores, keys, preferred_element_type=jnp.float32)
            * scale
        )
        keys_back = (
            jnp.einsum("ghqk,gqhe->gkhe", back_scores, query, preferred_element_type=jnp.float32)
            * scale
        )
        return (query_back, keys_back, values_back)

    query_back, keys_terms, values_terms = lax.map(
        attend_backward,
        (
            query_heads,
            key_heads,
            value_heads,
            prefix_blocks,
            total_blocks,
            keep_blocks,
            log_sums,
            back_blocks,
        ),
    )
    keys_back, values_back = (
        lax.psum_scatter(
            keys_terms.reshape(cells_here, length, width).astype(jnp.bfloat16),
            "seq",
            scatter_dimension=1,
            tiled=True,
        ).astype(jnp.float32),
        lax.psum_scatter(
            values_terms.reshape(cells_here, length, width).astype(jnp.bfloat16),
            "seq",
            scatter_dimension=1,
            tiled=True,
        ).astype(jnp.float32),
    )
    back_mixed = jnp.concatenate(
        [query_back.reshape(cells_here, span, width), keys_back, values_back], axis=-1
    ).astype(jnp.bfloat16)
    mix_shares = outer_rows(
        flat(normed), columns_cut(flat(back_mixed), seq_count), cell_count, me
    )
    mix_part = scattered_sum(*mix_shares, seq_count, cell_count, seq_second)
    query_bias_back = jnp.sum(flat(back_mixed[..., :width]).astype(jnp.float32), axis=0)
    value_bias_back = jnp.sum(flat(back_mixed[..., 2 * width :]).astype(jnp.float32), axis=0)
    back_normed = jnp.einsum(
        "cte,de->ctd", back_mixed, mix_weight, preferred_element_type=jnp.float32
    )
    first_value, first_pull = jax.vjp(layer_norm, inputs, first_gain, first_shift)
    inputs_part, first_gain_back, first_shift_back = first_pull(back_normed)
    tokens_back = (back_middle + inputs_part).astype(jnp.bfloat16)

    def own_rows_of(part, rows):
        starts, _ = row_cover(rows, cell_count)
        share = rows // cell_count
        shift = jnp.array([share * c - starts[c] for c in range(cell_count)])[me[1]]
        return lax.dynamic_slice_in_dim(part, shift, share, axis=0).astype(jnp.float32)

    vectors = (
        first_gain_back,
        first_shift_back,
        query_bias_back,
        value_bias_back,
        out_bias_back,
        second_gain_back,
        second_shift_back,
        up_bias_back,
        down_bias_back,
    )
    joined = jnp.concatenate([v.reshape(cell_count, -1) for v in vectors], axis=1)
    joined = joined[jnp.arange(cell_count) ^ me[1]]
    names = [("cells", b) for b in reversed(bits_of(cell_count))]
    joined = joined.reshape((2,) * len(names) + joined.shape[1:])
    for axis, bit in list(names):
        place = names.index((axis, bit))
        got = swap_with(lax.index_in_dim(joined, 1, place, keepdims=False), axis, bit)
        joined = lax.index_in_dim(joined, 0, place, keepdims=False) + got
        names.remove((axis, bit))
    for bit in bits_of(seq_count):
        joined = joined + swap_with(joined, "seq", bit)
    ends = [0]
    for v in vectors:
        ends.append(ends[-1] + v.shape[0] // cell_count)
    vectors = [joined[ends[i] : ends[i + 1]] for i in range(len(vectors))]
    matrices = (
        own_rows_of(mix_part, width),
        own_rows_of(out_part, width),
        own_rows_of(up_part, width),
        down_part.T.astype(jnp.float32),
    )
    return (
        block_out,
        tokens_back,
        vectors[0],
        vectors[1],
        matrices[0],
        vectors[2],
        vectors[3],
        matrices[1],
        vectors[4],
        vectors[5],
        vectors[6],
        matrices[2],
        vectors[7],
        matrices[3],
        vectors[8],
    )


def solution(mesh):
    return jax.shard_map(
        on_device,
        mesh=mesh,
        in_specs=(
            P("cells", "seq", None),
            P(),
            P(),
            P(),
            P(),
            P(),
            P(),
            P(),
            P(),
            P(),
            P(),
            P(),
            P(),
            P(),
            P("cells", "seq", None),
            P("cells"),
            P("cells"),
            P("cells", "seq"),
        ),
        out_specs=(
            P("cells", "seq", None),
            P("cells", "seq", None),
            P("cells"),
            P("cells"),
            P("cells", "seq"),
            P("cells"),
            P("cells"),
            P("cells", "seq"),
            P("cells"),
            P("cells"),
            P("cells"),
            P("cells", "seq"),
            P("cells"),
            P("cells", "seq"),
            P("cells"),
        ),
        check_vma=False,
    )
```

```python
from functools import partial
import math

import jax
import jax.numpy as jnp
from jax import lax
from jax.experimental import pallas as pl
from jax.experimental.pallas import tpu as pltpu
from jax.sharding import PartitionSpec as P

HEADS = 20
LANES = 128
TILE = 256
HEAD_PAD = 64
MASKED = -1e30
ONE_ROW = 56
SPLIT_ROW = 57
VMEM_LIMIT = 56 * 1024 * 1024
SHORT = pl.CostEstimate(flops=1, bytes_accessed=1, transcendentals=0)


def bits_of(count):
    return [1 << b for b in range(count.bit_length() - 1)]


def swap_with(array, axis, bit):
    count = lax.axis_size(axis)
    return lax.ppermute(array, axis, [(i, i ^ bit) for i in range(count)])


def without_bit(index, bit):
    return (index // (2 * bit)) * bit + index % bit


def add_halves_kernel(count, *refs):
    for n in range(count):
        mine_away, got_away, mine_here, got_here = refs[4 * n : 4 * n + 4]
        first = sum(refs[4 * p].shape[1] for p in range(n))
        rows = slice(first, first + mine_away.shape[1])
        for mine, got, result in (
            (mine_away, got_away, refs[4 * count]),
            (mine_here, got_here, refs[4 * count + 1]),
        ):
            total = mine[...].astype(jnp.float32) + got[...].astype(jnp.float32)
            result[:, rows, :] = total.astype(jnp.bfloat16)


def add_halves(pairs, bit):
    count, _, width = pairs[0][0].shape
    rows = sum(mine.shape[1] for mine, _ in pairs)
    shape = jax.ShapeDtypeStruct((count // 2, rows, width), jnp.bfloat16)
    in_specs, inputs = [], []
    for mine, got in pairs:
        for value in (bit, 0):
            spec = pl.BlockSpec(
                (1,) + mine.shape[1:],
                lambda g, value=value: ((g // bit) * (2 * bit) + value + g % bit, 0, 0),
            )
            in_specs += [spec, spec]
            inputs += [mine, got]
    out = pl.BlockSpec((1, rows, width), lambda g: (g, 0, 0))
    return pl.pallas_call(
        partial(add_halves_kernel, len(pairs)),
        out_shape=(shape, shape),
        grid=(count // 2,),
        in_specs=in_specs,
        out_specs=(out, out),
        compiler_params=pltpu.CompilerParams(vmem_limit_bytes=VMEM_LIMIT),
        cost_estimate=SHORT,
        name="add_halves",
    )(*inputs)


class Reduction:
    def __init__(self, label, names, order, send, keep, kind=None):
        self.labels = [label]
        self.kind = kind
        self.names, self.order = list(names), list(order)
        self.keep = keep
        self.heights = [keep.shape[1]]
        self.leave(send)

    def leave(self, send):
        axis, bit = self.order.pop(0)
        self.names.remove((axis, bit))
        self.got = swap_with(send, axis, bit)

    def step(self, last, *others):
        place = self.names.index(self.order[0])
        bit = 1 << (len(self.names) - 1 - place)
        pairs = [order_after((p.keep, p.got), last) for p in (self,) + others]
        for other in others:
            assert (other.names, other.order) == (self.names, self.order)
            self.heights += other.heights
            self.labels += other.labels
            other.labels, other.order = [], []
        send, self.keep = add_halves(pairs, bit)
        self.leave(send)
        return self.keep

    def finish(self, last):
        while self.order:
            last = self.step(last)
        total = order_after(self.keep, last).astype(jnp.float32) + self.got.astype(jnp.float32)
        ends = [sum(self.heights[:n]) for n in range(len(self.heights) + 1)]
        return {label: total[0, a:b] for label, a, b in zip(self.labels, ends, ends[1:])}


def row_cover(rows, count, unit=16):
    share = rows // count
    starts = [share * c // 8 * 8 for c in range(count)]
    height = max(share * (c + 1) - starts[c] for c in range(count))
    height = -(-height // unit) * unit
    return [min(s, rows - height) for s in starts], height


def head_groups(heads):
    first = -(-heads * 3 // 5)
    return [(0, first, 0), (first, heads - first, 3 * first)]


def no_grid_call(body, out_shape, name, flops, inputs, scratch, scalars=1):
    in_specs = [pl.BlockSpec(memory_space=pltpu.SMEM)] * scalars
    in_specs += [pl.BlockSpec(memory_space=pltpu.VMEM)] * (len(inputs) - scalars)
    moved = sum(x.size * x.dtype.itemsize for x in inputs)
    moved += sum(math.prod(x.shape) * x.dtype.itemsize for x in jax.tree.leaves(out_shape))
    return pl.pallas_call(
        body,
        out_shape=out_shape,
        in_specs=in_specs,
        out_specs=jax.tree.map(lambda _: pl.BlockSpec(memory_space=pltpu.VMEM), out_shape),
        scratch_shapes=scratch,
        compiler_params=pltpu.CompilerParams(vmem_limit_bytes=VMEM_LIMIT),
        cost_estimate=SHORT,
        name=name,
    )(*inputs)


def make_diagonal(diag_ref, keys, tile, prefix):
    first = tile * TILE
    shape = (TILE, TILE)
    key_at = lax.broadcasted_iota(jnp.int32, shape, 0)
    row_at = lax.broadcasted_iota(jnp.int32, shape, 1)
    opened = keys[first : first + TILE, ONE_ROW : ONE_ROW + 1].astype(jnp.float32) > -1.0
    near = (key_at <= row_at) | (key_at + first < prefix)
    seen = (near & opened) | (key_at == row_at)
    diag_ref[tile] = jnp.where(seen, 0.0, MASKED)


def without_mask(keys):
    lane = lax.broadcasted_iota(jnp.int32, keys.shape, 1)
    return jnp.where(lane == ONE_ROW, 0.0, keys.astype(jnp.float32)).astype(jnp.bfloat16)


def turned_rows(columns):
    return columns.astype(jnp.float32).T.astype(jnp.bfloat16)


def split_rows(columns, value):
    row = lax.broadcasted_iota(jnp.int32, columns.shape, 0)
    result = columns.astype(jnp.float32)
    for place in range(3):
        part = value.astype(jnp.bfloat16).astype(jnp.float32)
        value = value - part
        result = jnp.where(row == SPLIT_ROW + place, part, result)
    return result.astype(jnp.bfloat16)


def forward_kernel(seq_count, span, heads, head_size, rate, scalars, *refs):
    blocks, (weight, bias) = refs[:seq_count], refs[seq_count : seq_count + 2]
    groups = head_groups(heads)
    *qkv_groups, out = refs[seq_count + 2 : seq_count + 3 + len(groups)]
    *parts, rows, diag, scores = refs[seq_count + 3 + len(groups) :]
    me, prefix = scalars[0], scalars[2]
    length = span * seq_count
    tiles = length // TILE
    for r in range(seq_count):
        mixed = jnp.dot(weight[...], blocks[r][...], preferred_element_type=jnp.float32)
        mixed = (mixed + bias[...]).astype(jnp.bfloat16)
        place = pl.ds(pl.multiple_of((me ^ r) * span, LANES), span)
        mixed = mixed.reshape(3 * heads, HEAD_PAD, span)
        for (_, count, base), qkv in zip(groups, qkv_groups):
            qkv[:, :, place] = mixed[base : base + 3 * count]

    def turn(first, count, qkv, h, carry):
        rows[first + h] = turned_rows(qkv[count + h])
        return carry

    for (first, count, _), qkv in zip(groups, qkv_groups):
        lax.fori_loop(0, count, partial(turn, first, count, qkv), 0)
    for tile in range(tiles):
        make_diagonal(diag, rows.at[0], tile, prefix)

    def one_head(start, count, qkv, h, carry):
        for tile in range(tiles):
            across = slice(tile * TILE, (tile + 1) * TILE)
            query = qkv[h, :, across]
            tops = None
            for j in range(tile + 1):
                down = slice(j * TILE, (j + 1) * TILE)
                keys = rows[start + h, down, :]
                if j == tile:
                    keys = without_mask(keys)
                block = jnp.dot(keys, query, preferred_element_type=jnp.float32)
                if j == tile:
                    block = block + diag[tile]
                scores[down, :] = block
                top = jnp.max(block.reshape(TILE // 8, 8, TILE), axis=0)
                tops = top if tops is None else jnp.maximum(tops, top)
            top = jnp.max(tops, axis=0, keepdims=True)
            total = jnp.zeros((HEAD_PAD, TILE), jnp.float32)
            for j in range(tile + 1):
                down = slice(j * TILE, (j + 1) * TILE)
                probs = jnp.exp2((scores[down, :] - top) * rate).astype(jnp.bfloat16)
                total += jnp.dot(
                    qkv[2 * count + h, :, down], probs, preferred_element_type=jnp.float32
                )
            summed = total[ONE_ROW : ONE_ROW + 1]
            row = lax.broadcasted_iota(jnp.int32, total.shape, 0)
            log_sum = top * rate + jnp.log2(summed)
            out[start + h, :, across] = jnp.where(row == ONE_ROW, log_sum, total / summed)
        return carry

    for (first, count, _), qkv in zip(groups, qkv_groups):
        lax.fori_loop(0, count, partial(one_head, first, count, qkv), 0)
    for r in range(seq_count):
        place = pl.ds(pl.multiple_of((me ^ r) * span, LANES), span)
        piece = out[:, :head_size, place].reshape(heads * head_size, span)
        parts[r][...] = piece.astype(jnp.bfloat16)


def backward_kernel(
    seq_count, places, cell, span, first_head, heads, head_size, rate, earlier, scalars, *refs
):
    qkv, out, *rest = refs[:-9] if earlier is not None else refs[:-7]
    arrays = rest[: 1 + max(n for n, _ in places)]
    if earlier is not None:
        weights, backs = rest[len(arrays) : -earlier], rest[-earlier:]
        result, away, here_sums = refs[-9:-6]
    else:
        result = refs[-7]
    back, query_rows, key_rows, value_rows, gathered, diag = refs[-6:]
    me, prefix = scalars[0], scalars[2]
    length = span * seq_count
    tiles = length // TILE
    scale = 1.0 / math.sqrt(head_size)
    for r in range(seq_count):
        place = pl.ds(pl.multiple_of((me ^ r) * span, LANES), span)
        gathered[:, :, place] = arrays[places[r][0]][
            places[r][1], cell, first_head : first_head + heads
        ]
    key_rows[...] = turned_rows(qkv[heads])
    for tile in range(tiles):
        make_diagonal(diag, key_rows, tile, prefix)

    def one_head(h, carry):
        key_rows[...] = turned_rows(qkv[heads + h])
        value_rows[...] = turned_rows(qkv[2 * heads + h])
        held = gathered[h]
        centre = jnp.sum(
            held[:head_size].astype(jnp.float32) * out[first_head + h, :head_size],
            axis=0,
            keepdims=True,
        )
        gathered[h] = split_rows(held, -centre)
        log_sum = out[first_head + h, ONE_ROW : ONE_ROW + 1, :]
        qkv_q = split_rows(qkv[h], -log_sum / rate)
        query_rows[...] = jnp.zeros_like(query_rows)
        for j in range(tiles):
            down = slice(j * TILE, (j + 1) * TILE)
            keys, values = key_rows[down, :], value_rows[down, :]
            keys_column = qkv[heads + h, :, down]
            keys_back = jnp.zeros((TILE, HEAD_PAD), jnp.float32)
            values_back = jnp.zeros((TILE, HEAD_PAD), jnp.float32)
            for i in range(j, tiles):
                across = slice(i * TILE, (i + 1) * TILE)
                query = qkv_q[:, across]
                back_out = gathered[h, :, across]
                if i == j:
                    block = jnp.dot(without_mask(keys), query, preferred_element_type=jnp.float32)
                    block = block + diag[i]
                else:
                    block = jnp.dot(keys, query, preferred_element_type=jnp.float32)
                probs = jnp.exp2(block * rate)
                back_probs = jnp.dot(values, back_out, preferred_element_type=jnp.float32)
                back_scores = (probs * back_probs).astype(jnp.bfloat16)
                probs = probs.astype(jnp.bfloat16)
                turned = (((1,), (1,)), ((), ()))
                values_back += lax.dot_general(
                    probs, back_out, turned, preferred_element_type=jnp.float32
                )
                keys_back += lax.dot_general(
                    back_scores, query, turned, preferred_element_type=jnp.float32
                )
                query_rows[:, across] += jnp.dot(
                    keys_column, back_scores, preferred_element_type=jnp.float32
                )
            back[heads + h, down, :] = (keys_back * scale).astype(jnp.bfloat16)
            back[2 * heads + h, down, :] = values_back.astype(jnp.bfloat16)
        back[h] = (query_rows[...] * scale).T.astype(jnp.bfloat16)
        return carry

    lax.fori_loop(0, heads, one_head, 0)
    for block in range(seq_count):
        here = slice(block * span, (block + 1) * span)
        there = pl.ds(pl.multiple_of((me ^ block) * span, LANES), span)
        for first in range(0, 3 * heads, 2):
            pieces = [back[p, here, :] for p in range(first, min(first + 2, 3 * heads))]
            joined = pieces[0] if len(pieces) == 1 else jnp.concatenate(pieces, axis=1)
            left = first * HEAD_PAD
            result[there, left : left + joined.shape[1]] = joined
    if earlier is None:
        return
    for r in range(seq_count):
        target = away if r & 1 else here_sums
        turned = (((1,), (1,)), ((), ()))
        total = 0.0
        for weight, dense in zip(weights, [*backs, result]):
            total += lax.dot_general(
                weight[...],
                dense[r * span : (r + 1) * span, :],
                turned,
                preferred_element_type=jnp.float32,
            )
        target[r >> 1] = total.astype(jnp.bfloat16)


def attend_forward(scalars, blocks, weight, bias, heads, head_size):
    seq_count, span = len(blocks), blocks[0].shape[1]
    length = seq_count * span
    rate = math.log2(math.e) / math.sqrt(head_size)
    flops = 2 * weight.size * length + 4 * heads * HEAD_PAD * length * length
    return no_grid_call(
        partial(forward_kernel, seq_count, span, heads, head_size, rate),
        tuple(
            jax.ShapeDtypeStruct((3 * count, HEAD_PAD, length), jnp.bfloat16)
            for _, count, _ in head_groups(heads)
        )
        + (jax.ShapeDtypeStruct((heads, HEAD_PAD, length), jnp.float32),)
        + (jax.ShapeDtypeStruct((heads * head_size, span), jnp.bfloat16),) * seq_count,
        "attend_forward",
        flops,
        [scalars, *blocks, weight, bias],
        [
            pltpu.VMEM((heads, length, HEAD_PAD), jnp.bfloat16),
            pltpu.VMEM((length // TILE, TILE, TILE), jnp.float32),
            pltpu.VMEM((length, TILE), jnp.float32),
        ],
    )


def attend_backward(
    scalars, cell, qkv, out, arrays, places, first_head, head_size, weights=None, backs=()
):
    seq_count, span = len(places), arrays[0].shape[-1]
    heads = qkv.shape[0] // 3
    length = seq_count * span
    rate = math.log2(math.e) / math.sqrt(head_size)
    earlier = len(backs) if weights else None
    inputs = [scalars, qkv, out, *arrays]
    results = (jax.ShapeDtypeStruct((length, 3 * heads * HEAD_PAD), jnp.bfloat16),)
    if weights:
        inputs += [*weights, *backs]
        shape = (seq_count // 2, weights[0].shape[0], span)
        results += (jax.ShapeDtypeStruct(shape, jnp.bfloat16),) * 2
    return no_grid_call(
        partial(
            backward_kernel,
            seq_count,
            places,
            cell,
            span,
            first_head,
            heads,
            head_size,
            rate,
            earlier,
        ),
        results,
        "attend_backward",
        1,
        inputs,
        [
            pltpu.VMEM((3 * heads, length, HEAD_PAD), jnp.bfloat16),
            pltpu.VMEM((HEAD_PAD, length), jnp.float32),
            pltpu.VMEM((length, HEAD_PAD), jnp.bfloat16),
            pltpu.VMEM((length, HEAD_PAD), jnp.bfloat16),
            pltpu.VMEM((heads, HEAD_PAD, length), jnp.bfloat16),
            pltpu.VMEM((length // TILE, TILE, TILE), jnp.float32),
        ],
    )


def mix_outer_kernel(cell_count, share, cuts, count, scalars, *refs):
    blocks, backs = refs[: -count - 7], refs[-count - 7 : -7]
    *results, sums, turned, whole_sum = refs[-7:]
    span = blocks[0].shape[1]
    features = turned.shape[0]
    for n, block in enumerate(blocks):
        turned[:, n * span : (n + 1) * span] = block[:features, :]
    width = backs[0].shape[1]
    length = backs[0].shape[0]
    sums[...] = sum(
        jnp.sum(back[...].astype(jnp.float32), axis=0, keepdims=True) for back in backs
    )
    for first in range(0, width, TILE):
        last = min(first + TILE, width)
        total = None
        for n, back in enumerate(backs):
            part = jnp.dot(
                turned[:, n * length : (n + 1) * length],
                back[:, first:last],
                preferred_element_type=jnp.float32,
            )
            total = part if total is None else total + part
        whole_sum[:, first:last] = total
    for k in range(cell_count):
        c = k ^ scalars[1]
        start = jnp.minimum(lax.div(c * share, 8) * 8, features - cuts[-1])
        block = whole_sum[pl.ds(pl.multiple_of(start, 8), cuts[-1]), :].astype(jnp.bfloat16)
        for n, bit in enumerate((1, 2)):
            target = results[2 * n + (0 if k & bit else 1)]
            target[without_bit(k, bit)] = block[cuts[n] : cuts[n + 1]]


def mix_outer(scalars, blocks, backs, features, cell_count):
    _, height = row_cover(features, cell_count)
    cuts = (0, -(-height // 2 // 16) * 16, height)
    width = backs[0].shape[1]
    positions = sum(b.shape[0] for b in backs)
    halves = [(cell_count // 2, cuts[n + 1] - cuts[n], width) for n in (0, 0, 1, 1)]
    return no_grid_call(
        partial(mix_outer_kernel, cell_count, features // cell_count, cuts, len(backs)),
        tuple(jax.ShapeDtypeStruct(shape, jnp.bfloat16) for shape in halves)
        + (jax.ShapeDtypeStruct((1, width), jnp.float32),),
        "mix_outer",
        2 * positions * features * width,
        [scalars, *blocks, *backs],
        [
            pltpu.VMEM((features, positions), jnp.bfloat16),
            pltpu.VMEM((features, width), jnp.float32),
        ],
    )


def gathered_blocks(block, seq_count):
    held = {0: block}
    for bit in list(reversed(bits_of(seq_count))):
        held.update({r | bit: swap_with(x, "seq", bit) for r, x in list(held.items())})
    return [held[r] for r in range(seq_count)]


def route_upper(upper):
    return swap_with(upper, "seq", upper.shape[0])


def route_rest(lower, got):
    seq_count = 2 * len(lower)
    arrays = [x[None] for x in lower] + [got]
    held = {r: (r, 0) for r in range(len(lower))}
    held.update({len(lower) + r: (len(lower), r) for r in range(len(lower))})
    for bit in list(reversed(bits_of(seq_count)))[1:]:
        away = [r for r in held if r & bit]
        arrays.append(swap_with(jnp.stack([arrays[held[r][0]][held[r][1]] for r in away]), "seq", bit))
        held.update({r: (len(arrays) - 1, n) for n, r in enumerate(away)})
    return arrays, [held[r] for r in range(seq_count)]


def exchanged_blocks(blocks):
    return [blocks[0]] + [swap_with(blocks[r], "seq", r) for r in range(1, len(blocks))]


def chunks(width):
    return [(first, min(first + TILE, width)) for first in range(0, width, TILE)]


def dot(left, right):
    return jnp.dot(left, right, preferred_element_type=jnp.float32)


def dot_turned(left, right):
    return lax.dot_general(
        left, right, (((1,), (1,)), ((), ())), preferred_element_type=jnp.float32
    )


def centred_columns(values):
    centred = values - jnp.mean(values, axis=0, keepdims=True)
    spread = jnp.mean(centred * centred, axis=0, keepdims=True)
    rise = lax.rsqrt(spread + 1e-05)
    return centred * rise, rise


def norm_pull(normal, rise, back, gain):
    scaled = back * gain
    inner = scaled - jnp.mean(scaled, axis=0, keepdims=True)
    inner = inner - normal * jnp.mean(scaled * normal, axis=0, keepdims=True)
    return rise * inner


def columns_of(lines):
    turned = lines[...].T
    return [turned[:, n : n + 1] for n in range(8)]


def lines_of(columns):
    rows = columns[0].shape[0]
    room = [jnp.zeros((rows, 8 - len(columns)), jnp.float32)] if len(columns) < 8 else []
    return jnp.concatenate(list(columns) + room, axis=1).T


def first_norm_kernel(tokens, lines, hidden, *results):
    width = tokens.shape[1]
    gain, shift = columns_of(lines)[:2]
    for c, result in enumerate(results):
        normal, _ = centred_columns(tokens[c].astype(jnp.float32))
        result[:width, :] = (normal * gain + shift).astype(jnp.bfloat16)
        shape = (result.shape[0] - width, result.shape[1])
        mark = lax.broadcasted_iota(jnp.int32, shape, 0) == 0
        result[width:, :] = jnp.where(mark, hidden[c : c + 1, :], 0.0).astype(jnp.bfloat16)


def first_norm(tokens, lines, hidden, features):
    cells, _, span = tokens.shape
    return no_grid_call(
        first_norm_kernel,
        (jax.ShapeDtypeStruct((features, span), jnp.bfloat16),) * cells,
        "first_norm",
        10 * tokens.size,
        [tokens, lines, hidden],
        [],
        scalars=0,
    )


def second_norm_kernel(seq_count, scalars, weight, tokens, lines, *refs):
    parts = refs[:seq_count]
    middle, second, second_turned, attended, gather = refs[seq_count:]
    share = parts[0].shape[0]
    _, _, gain, shift, bias, *_ = columns_of(lines)
    for r in range(seq_count):
        place = pl.ds(pl.multiple_of((scalars[0] ^ r) * share, 8), share)
        gather[place, :] = parts[r][...].astype(jnp.float32)
    attended[...] = gather[: attended.shape[0], :].astype(jnp.bfloat16)
    total = dot(weight[...].T, attended[...])
    total = tokens[...].astype(jnp.float32) + (total + bias)
    middle[...] = total
    normal, _ = centred_columns(total)
    normed = (normal * gain + shift).astype(jnp.bfloat16)
    second_turned[...] = normed
    second[...] = normed.T


def second_norm(scalars, weight, tokens, lines, parts):
    width, span = tokens.shape
    seq_count = len(parts)
    return no_grid_call(
        partial(second_norm_kernel, seq_count),
        (
            jax.ShapeDtypeStruct((width, span), jnp.float32),
            jax.ShapeDtypeStruct((span, width), jnp.bfloat16),
            jax.ShapeDtypeStruct((width, span), jnp.bfloat16),
            jax.ShapeDtypeStruct((width, span), jnp.bfloat16),
        ),
        "second_norm",
        2 * span * width * width,
        [scalars, weight, tokens, lines, *parts],
        [pltpu.VMEM((seq_count * parts[0].shape[0], span), jnp.float32)],
    )


def weights_kernel(seq_count, heads, head_size, scalars, mix, weight, *turned):
    width = mix.shape[0]
    here = heads * head_size
    groups = head_groups(heads)
    weight[...] = jnp.zeros_like(weight)
    for s in range(seq_count):

        @pl.when(scalars[0] == s)
        def _():
            for p in range(3):
                first = s * here
                last = min(first + here, width)
                if last <= first:
                    continue
                start = (p * width + first) // LANES * LANES
                stop = min(-(-(p * width + last) // LANES) * LANES, mix.shape[1])
                block = mix[:, start:stop].astype(jnp.float32)
                block = block[:, p * width + first - start : p * width + last - start].T
                for group_first, count, base in groups:
                    for n in range(count):
                        h = group_first + n
                        if (h + 1) * head_size > last - first:
                            continue
                        place = (base + p * count + n) * HEAD_PAD
                        piece = block[h * head_size : (h + 1) * head_size]
                        room = jnp.zeros((HEAD_PAD - head_size, width), jnp.float32)
                        piece = jnp.concatenate([piece, room])
                        weight[place : place + HEAD_PAD, :width] = piece.astype(jnp.bfloat16)

    room = weight.shape[1] - width
    for (_, count, base), columns in zip(groups, turned):
        rows = slice(base * HEAD_PAD, (base + 3 * count) * HEAD_PAD)
        columns[...] = weight[rows, :width].T
        rows = slice((base + count) * HEAD_PAD, (base + 2 * count) * HEAD_PAD)
        row = lax.broadcasted_iota(jnp.int32, (count * HEAD_PAD, room), 0)
        lane = lax.broadcasted_iota(jnp.int32, (count * HEAD_PAD, room), 1)
        mark = (lane == 0) & (lax.rem(row, HEAD_PAD) == ONE_ROW)
        weight[rows, width:] = jnp.where(mark, 1.0, 0.0).astype(jnp.bfloat16)


def own_weights(scalars, mix, features, seq_count, heads, head_size):
    width = mix.shape[0]
    return no_grid_call(
        partial(weights_kernel, seq_count, heads, head_size),
        (jax.ShapeDtypeStruct((3 * heads * HEAD_PAD, features), jnp.bfloat16),)
        + tuple(
            jax.ShapeDtypeStruct((width, 3 * count * HEAD_PAD), jnp.bfloat16)
            for _, count, _ in head_groups(heads)
        ),
        "own_weights",
        1,
        [scalars, mix],
        [],
    )


def active_back_kernel(cotangent, down, result):
    for first, last in chunks(down.shape[1]):
        result[:, first:last] = dot(cotangent[...], down[:, first:last])


def active_back(scalars, cotangent, down):
    rows, width = cotangent.shape
    tile = hidden_tile(down.shape[1])
    shape = jax.ShapeDtypeStruct((rows, down.shape[1]), jnp.float32)
    return grid_call(
        lambda me, *refs: active_back_kernel(*refs),
        (down.shape[1] // tile,),
        [whole(cotangent), pl.BlockSpec((width, tile), lambda g, me: (0, g))],
        pl.BlockSpec((rows, tile), lambda g, me: (0, g)),
        shape,
        [],
        "active_back",
        1,
        (scalars, cotangent, down),
        1,
    )


def hidden_kernel(back_active, up, up_bias, *refs):
    *parts, active, back_upper, bias_back, second = refs

    @pl.when(pl.program_id(0) == 0)
    def _():
        for c, part in enumerate(parts):
            second[c * part.shape[0] : (c + 1) * part.shape[0], :] = part[...]

    inner = math.sqrt(2.0 / math.pi)
    for first, last in chunks(up.shape[1]):
        upper = dot(second[...], up[:, first:last]) + up_bias[:, first:last]
        back = back_active[:, first:last]
        square = upper * upper
        bend = jnp.tanh(inner * upper * (1.0 + 0.044715 * square))
        half = 0.5 + 0.5 * bend
        slope = half + (0.5 * inner) * upper * (1.0 - bend * bend) * (1.0 + 0.134145 * square)
        active[:, first:last] = (upper * half).astype(jnp.bfloat16)
        back = (back * slope).astype(jnp.bfloat16)
        back_upper[:, first:last] = back
        bias_back[:, first:last] = jnp.sum(back.astype(jnp.float32), axis=0, keepdims=True)


def grid_call(
    body, grid, in_specs, out_specs, out_shape, scratch, name, flops, inputs, moved, aliases=None
):
    return pl.pallas_call(
        body,
        out_shape=out_shape,
        grid_spec=pltpu.PrefetchScalarGridSpec(
            num_scalar_prefetch=1,
            grid=grid,
            in_specs=in_specs,
            out_specs=out_specs,
            scratch_shapes=scratch,
        ),
        compiler_params=pltpu.CompilerParams(vmem_limit_bytes=VMEM_LIMIT),
        cost_estimate=SHORT,
        input_output_aliases=aliases or {},
        name=name,
    )(*inputs)


def whole(array):
    zeros = (0,) * array.ndim
    return pl.BlockSpec(array.shape, lambda g, me: zeros)


def hidden_tile(hidden):
    return max(t for t in range(LANES, 1024, LANES) if hidden % t == 0)


def hidden_layer(scalars, second, back_active, up, up_bias):
    rows = sum(part.shape[0] for part in second)
    width = up.shape[0]
    hidden = up.shape[1]
    tile = hidden_tile(hidden)
    weight = pl.BlockSpec((width, tile), lambda g, me: (0, g))
    out = pl.BlockSpec((rows, tile), lambda g, me: (0, g))
    line = pl.BlockSpec((1, tile), lambda g, me: (0, g))
    return grid_call(
        lambda me, *refs: hidden_kernel(*refs),
        (hidden // tile,),
        [out, weight, line] + [whole(part) for part in second],
        [out, out, line],
        (
            jax.ShapeDtypeStruct((rows, hidden), jnp.bfloat16),
            jax.ShapeDtypeStruct((rows, hidden), jnp.bfloat16),
            jax.ShapeDtypeStruct((1, hidden), jnp.float32),
        ),
        [pltpu.VMEM((rows, width), jnp.bfloat16)],
        "hidden_layer",
        4 * rows * up.size,
        (scalars, back_active, up, up_bias, *second),
        4 * up.size + 4 * rows * hidden,
    )


def middle_back_kernel(
    seq_count,
    cells,
    scalars,
    back_upper,
    up,
    lines,
    cotangent,
    weight,
    *refs,
):
    middle, (back_middle, back_branch, sums) = refs[:cells], refs[cells : cells + 3]
    *parts, total, back_heads = refs[cells + 3 :]
    half = seq_count // 2
    step = pl.program_id(0)

    @pl.when(step == 0)
    def _():
        total[...] = jnp.zeros_like(total)

    for first, last in chunks(total.shape[1]):
        total[:, first:last] += dot_turned(up[...], back_upper[first:last, :])

    @pl.when(step == pl.num_programs(0) - 1)
    def _():
        span = cotangent.shape[2]
        heads = parts[0].shape[1]
        head_size = back_heads.shape[0] // (seq_count * heads)
        gain = columns_of(lines)[2]
        totals = [0.0] * 4
        for c in range(cells):
            here = slice(c * span, (c + 1) * span)
            normal, rise = centred_columns(middle[c][...])
            back = total[:, here]
            back_out = cotangent[c].astype(jnp.float32)
            back_mid = back_out + norm_pull(normal, rise, back, gain)
            back_middle[:, here] = back_mid
            branch = back_mid.astype(jnp.bfloat16)
            back_branch[:, here] = branch
            for n, term in enumerate((back * normal, back, branch.astype(jnp.float32), back_out)):
                totals[n] = totals[n] + jnp.sum(term, axis=1, keepdims=True)
            back_heads[: weight.shape[0], :] = dot(weight[...], branch)
            if back_heads.shape[0] > weight.shape[0]:
                rest = back_heads.shape[0] - weight.shape[0]
                back_heads[weight.shape[0] :, :] = jnp.zeros((rest, span), jnp.float32)
            for r in range(seq_count):
                first = (scalars[0] ^ r) * heads * head_size
                part = back_heads[pl.ds(pl.multiple_of(first, 8), heads * head_size), :]
                room = jnp.zeros((heads, HEAD_PAD - head_size, span), jnp.float32)
                part = jnp.concatenate([part.reshape(heads, head_size, span), room], axis=1)
                target = parts[r].at[c] if r < half else parts[half].at[r - half, c]
                target[...] = part.astype(jnp.bfloat16)
        sums[...] = lines_of(totals)


def middle_back(scalars, back_upper, up, middle, lines, cotangent, weight, seq_count, heads):
    rows, hidden = back_upper.shape
    cells, width, span = cotangent.shape
    head_size = width // HEADS
    tile = hidden_tile(hidden)
    outs = [
        jax.ShapeDtypeStruct((width, rows), jnp.float32),
        jax.ShapeDtypeStruct((width, rows), jnp.bfloat16),
        jax.ShapeDtypeStruct((8, width), jnp.float32),
    ]
    block = (cells, heads, HEAD_PAD, span)
    outs += [jax.ShapeDtypeStruct(block, jnp.bfloat16)] * (seq_count // 2)
    outs += [jax.ShapeDtypeStruct((seq_count // 2,) + block, jnp.bfloat16)]
    return grid_call(
        partial(middle_back_kernel, seq_count, cells),
        (hidden // tile,),
        [
            pl.BlockSpec((rows, tile), lambda g, me: (0, g)),
            pl.BlockSpec((width, tile), lambda g, me: (0, g)),
            whole(lines),
            whole(cotangent),
            whole(weight),
        ]
        + [whole(m) for m in middle],
        [whole(o) for o in outs],
        outs,
        [
            pltpu.VMEM((width, rows), jnp.float32),
            pltpu.VMEM((seq_count * heads * head_size, span), jnp.float32),
        ],
        "middle_back",
        2 * rows * up.size + 2 * rows * width * width,
        (scalars, back_upper, up, lines, cotangent, weight, *middle),
        1,
    )


def block_out_kernel(active, down, lines, *refs):
    *middle, result, total = refs
    step = pl.program_id(0)

    @pl.when(step == 0)
    def _():
        bias = columns_of(lines)[5]
        for c, part in enumerate(middle):
            span = part.shape[1]
            total[:, c * span : (c + 1) * span] = part[...] + bias

    for first, last in chunks(total.shape[1]):
        total[:, first:last] += dot_turned(down[...], active[first:last, :])

    @pl.when(step == pl.num_programs(0) - 1)
    def _():
        cells, _, span = result.shape
        for c in range(cells):
            result[c] = total[:, c * span : (c + 1) * span].astype(jnp.bfloat16)


def block_output(scalars, active, down, middle, lines):
    rows, hidden = active.shape
    cells, width = len(middle), middle[0].shape[0]
    tile = hidden_tile(hidden)
    out = jax.ShapeDtypeStruct((cells, width, rows // cells), jnp.bfloat16)
    return grid_call(
        lambda me, *refs: block_out_kernel(*refs),
        (hidden // tile,),
        [
            pl.BlockSpec((rows, tile), lambda g, me: (0, g)),
            pl.BlockSpec((width, tile), lambda g, me: (0, g)),
            whole(lines),
        ]
        + [whole(m) for m in middle],
        whole(out),
        out,
        [pltpu.VMEM((width, rows), jnp.float32)],
        "block_output",
        2 * rows * down.size,
        (scalars, active, down, lines, *middle),
        1,
    )


def take_columns(piece, right, count, which):
    width = piece.shape[1]
    for s in range(count):

        @pl.when(which == s)
        def _():
            first = s * width // LANES * LANES
            last = min(-(-(s + 1) * width // LANES) * LANES, right.shape[1])
            block = right[:, first:last]
            piece[...] = block[:, s * width - first : (s + 1) * width - first]


def up_outer_kernel(seq_count, cells, share, cut, zbit, split, scalars, right, *refs):
    left, rest = refs[:cells], refs[cells:]
    got = rest[0] if split else None
    *results, total, piece, joined = rest[3 if split else 0 :]
    rows = left[0].shape[0]
    core = 0 if split else 1

    @pl.when(pl.program_id(0) == 0)
    def _():
        for c, part in enumerate(left):
            joined[:, c * part.shape[1] : (c + 1) * part.shape[1]] = part[...]

    take_columns(piece, right, seq_count, (2 * pl.program_id(0) + core) ^ scalars[0])
    for first, last in chunks(piece.shape[1]):
        total[:, first:last] = dot(joined[...], piece[:, first:last])
    cell_count = results[0].shape[1] * (2 if split else 1)
    height = results[0].shape[2] if not split else got.shape[2]
    for k in range(cell_count):
        c = k ^ scalars[1]
        start = jnp.minimum(lax.div(c * share, 8) * 8, rows - height)
        block = total[pl.ds(pl.multiple_of(start, 8), height), :]
        if split:
            block = block + got[0, k].astype(jnp.float32)
            for n, (bit, part) in enumerate(((1, block[:cut]), (zbit, block[cut:]))):
                target = results[2 * n + (0 if k & bit else 1)]
                target[0, without_bit(k, bit)] = part.astype(jnp.bfloat16)
        else:
            results[0][0, k] = block.astype(jnp.bfloat16)


def up_outer(scalars, left, right, seq_count, cell_count, got=None, lower=None):
    tokens, width = right.shape[0], right.shape[1] // seq_count
    rows = left[0].shape[0]
    _, height = row_cover(rows, cell_count)
    half = seq_count // 2
    split = got is not None
    cut = two_thirds(height)
    in_specs = [whole(right)] + [whole(part) for part in left]
    inputs = [scalars, right, *left]
    aliases = {}
    if split:
        in_specs.append(pl.BlockSpec((1,) + got.shape[1:], lambda g, me: (g, 0, 0, 0)))
        in_specs += [pl.BlockSpec(memory_space=pl.ANY)] * 2
        inputs += [got, *lower]
        aliases = {len(inputs) - 2: 2, len(inputs) - 1: 3}
        outs = [(half, cell_count // 2, cut, width)] * 2 + [lower[0].shape] * 2
        low = height - cut
        blocks = [pl.BlockSpec((1,) + outs[0][1:], lambda g, me: (g, 0, 0, 0))] * 2
        blocks += [
            pl.BlockSpec((1, cell_count // 2, low, width), lambda g, me: (g, 0, 1, 0))
        ] * 2
    else:
        outs = [(half, cell_count, height, width)]
        blocks = [pl.BlockSpec((1,) + outs[0][1:], lambda g, me: (g, 0, 0, 0))]
    return grid_call(
        partial(
            up_outer_kernel,
            seq_count,
            len(left),
            rows // cell_count,
            cut,
            cell_count // seq_count,
            split,
        ),
        (half,),
        in_specs,
        blocks,
        [jax.ShapeDtypeStruct(out, jnp.bfloat16) for out in outs],
        [
            pltpu.VMEM((rows, width), jnp.float32),
            pltpu.VMEM((tokens, width), jnp.bfloat16),
            pltpu.VMEM((rows, tokens), jnp.bfloat16),
        ],
        "up_outer",
        1,
        inputs,
        1,
        aliases,
    )


def two_thirds(height):
    return -(-height * 2 // 3 // 16) * 16


def down_outer_kernel(seq_count, inner, cut, split, scalars, left, right, *refs):
    got = refs[0] if split else None
    *results, total, piece, wide, own = refs[1 if split else 0 :]
    half = seq_count // 2
    share = own.shape[0] // half
    span = left.shape[2]
    width = piece.shape[1] // inner
    low = scalars[1] & (inner - 1)
    step = pl.program_id(0)
    core = 0 if split else 1
    starts, height = row_cover(share, inner)

    @pl.when(step == 0)
    def _():
        for c in range(left.shape[0]):
            wide[:, c * span : (c + 1) * span] = left[c].astype(jnp.float32)
        for x in range(half):
            for s in range(seq_count):

                @pl.when(((2 * x + core) ^ scalars[0]) == s)
                def _():
                    own[x * share : (x + 1) * share, :] = wide[s * share : (s + 1) * share, :]

    take_columns(piece, right, seq_count, step ^ lax.div(scalars[1], inner))
    for first, last in chunks(piece.shape[1]):
        total[:, first:last] = dot(own[...].astype(jnp.bfloat16), piece[:, first:last])
    for q in range(inner):
        for x in range(half):
            block = total[x * share : (x + 1) * share, q * width : (q + 1) * width]
            block = jnp.concatenate([block[s : s + height] for s in starts], axis=1)
            if split:
                block = block + got[x, q ^ low].astype(jnp.float32)
                away = 2 * x >= half
                target = results[0 if away else 1]
                target[x % (half // 2), q ^ low] = block[:cut].astype(jnp.bfloat16)
                rest = block[cut:].astype(jnp.bfloat16)

                @pl.when(step & 1 == 1)
                def _():
                    results[2][x, q ^ low] = rest

                @pl.when(step & 1 == 0)
                def _():
                    results[3][x, q ^ low] = rest

            else:
                results[0][x, q ^ low] = block.astype(jnp.bfloat16)


def down_outer(scalars, left, right, seq_count, cell_count, got=None):
    tokens, width = right.shape[0], right.shape[1] // seq_count
    half = seq_count // 2
    inner = cell_count // seq_count
    share = left.shape[1] // seq_count
    split = got is not None
    _, height = row_cover(share, inner)
    cut = two_thirds(height)
    in_specs = [whole(left), whole(right)]
    inputs = [scalars, left, right]
    if split:
        in_specs.append(pl.BlockSpec((half, inner) + got.shape[2:], lambda g, me: (0, g, 0, 0)))
        inputs.append(got)
        low = height - cut
        outs = [(half // 2, cell_count, cut, width)] * 2
        outs += [(half, cell_count // 2, 2 * low, width)] * 2
        blocks = [pl.BlockSpec((half // 2, inner, cut, width), lambda g, me: (0, g, 0, 0))] * 2
        blocks += [pl.BlockSpec((half, inner, low, width), lambda g, me: (0, g // 2, 0, 0))] * 2
    else:
        outs = [(half, cell_count, height, width)]
        blocks = [pl.BlockSpec((half, inner, height, width), lambda g, me: (0, g, 0, 0))]
    return grid_call(
        partial(down_outer_kernel, seq_count, inner, cut, split),
        (seq_count,),
        in_specs,
        blocks,
        [jax.ShapeDtypeStruct(out, jnp.bfloat16) for out in outs],
        [
            pltpu.VMEM((half * share, width), jnp.float32),
            pltpu.VMEM((tokens, width), jnp.bfloat16),
            pltpu.VMEM((left.shape[1], tokens), jnp.float32),
            pltpu.VMEM((half * share, tokens), jnp.float32),
        ],
        "down_outer",
        1,
        inputs,
        1,
    )


def out_outer_kernel(seq_count, cells, share, scalars, right, *refs):
    left, (result, total, joined) = refs[:cells], refs[cells:]
    for c, part in enumerate(left):
        joined[:, c * part.shape[1] : (c + 1) * part.shape[1]] = part[...]
    rows = total.shape[0]
    for first, last in chunks(total.shape[1]):
        total[:, first:last] = dot_turned(joined[...], right[first:last, :])
    width = total.shape[1] // seq_count
    part = result.shape[2]
    for k in range(result.shape[1]):
        c = k ^ scalars[1]
        start = jnp.minimum(lax.div(c * share, 8) * 8, rows - seq_count * part)
        block = total[pl.ds(pl.multiple_of(start, 8), seq_count * part), :]
        for s in range(seq_count):
            piece = block[:, s * width : (s + 1) * width]
            groups = [piece[i * part : (i + 1) * part] for i in range(seq_count)]
            place = s ^ scalars[0]
            place = (place & 1) * (seq_count // 2) + (place >> 1)
            result[place, k] = jnp.concatenate(groups, axis=1).astype(jnp.bfloat16)


def out_outer(scalars, left, right, seq_count, cell_count):
    rows, tokens = right.shape
    _, height = row_cover(rows, cell_count, 16 * seq_count)
    shape = (seq_count, cell_count, height // seq_count, rows)
    return no_grid_call(
        partial(out_outer_kernel, seq_count, len(left), rows // cell_count),
        jax.ShapeDtypeStruct(shape, jnp.bfloat16),
        "out_outer",
        1,
        [scalars, right, *left],
        [pltpu.VMEM((rows, rows), jnp.float32), pltpu.VMEM((rows, tokens), jnp.bfloat16)],
    )


def mix_columns_kernel(heads, head_size, scalars, *refs):
    *blocks, result = refs
    places = {}
    for first, count, base in head_groups(heads):
        places.update({(p, first + n): base + p * count + n for p in range(3) for n in range(count)})
    seq_count = len(blocks)
    share = result.shape[1]
    width = HEADS * head_size
    for mine in range(seq_count):

        @pl.when(scalars[0] == mine)
        def _():
            for p in range(3):
                for head in range(HEADS):
                    first = p * width + head * head_size - mine * share
                    cut_left, cut_right = max(0, -first), min(head_size, share - first)
                    if cut_left >= cut_right:
                        continue
                    block = blocks[(head // heads) ^ mine]
                    source = places[p, head % heads] * HEAD_PAD
                    base = source // LANES * LANES
                    piece = block[:, base : min(base + LANES, block.shape[1])].astype(jnp.float32)
                    source -= base
                    result[:, first + cut_left : first + cut_right] = piece[
                        :, source + cut_left : source + cut_right
                    ]


def mix_columns(scalars, blocks, heads, head_size):
    rows = blocks[0].shape[0]
    return no_grid_call(
        partial(mix_columns_kernel, heads, head_size),
        jax.ShapeDtypeStruct((rows, 3 * HEADS * head_size // len(blocks)), jnp.float32),
        "mix_columns",
        1,
        [scalars, *blocks],
        [],
    )


def tokens_back_kernel(tokens, lines, back_middle, *refs):
    cells, _, span = tokens.shape
    terms, (result, sums) = refs[: 2 * cells], refs[2 * cells :]
    gain = columns_of(lines)[0]
    totals = [0.0] * 2
    for c in range(cells):
        normal, rise = centred_columns(tokens[c].astype(jnp.float32))
        back = terms[2 * c][...].astype(jnp.float32) + terms[2 * c + 1][...].astype(jnp.float32)
        back_in = back_middle[:, c * span : (c + 1) * span]
        back_in = back_in + norm_pull(normal, rise, back, gain)
        result[c] = back_in.astype(jnp.bfloat16)
        for n, term in enumerate((back * normal, back)):
            totals[n] = totals[n] + jnp.sum(term, axis=1, keepdims=True)
    sums[...] = lines_of(totals)


def tokens_back(tokens, lines, back_middle, terms):
    return no_grid_call(
        tokens_back_kernel,
        (
            jax.ShapeDtypeStruct(tokens.shape, jnp.bfloat16),
            jax.ShapeDtypeStruct((8, tokens.shape[1]), jnp.float32),
        ),
        "tokens_back",
        20 * tokens.size,
        [tokens, lines, back_middle, *terms],
        [],
        scalars=0,
    )


def order_after(values, *earlier):
    values, _ = lax.optimization_barrier((values, earlier))
    return values


def advance(parts, last):
    groups = {}
    running = [part for part in parts if part.order]
    arrived = [part.got for part in running]
    for part in running:
        part.got = order_after(part.got, arrived)
        key = (part.kind, tuple(part.names), tuple(part.order), part.keep.shape[2])
        groups.setdefault(key, []).append(part)
    for first, *others in groups.values():
        last = first.step(last, *others)
    return last


def on_device(
    tokens,
    first_gain,
    first_shift,
    mix_weight,
    query_bias,
    value_bias,
    out_weight,
    out_bias,
    second_gain,
    second_shift,
    up_weight,
    up_bias,
    down_weight,
    down_bias,
    cotangent,
    prefix_lengths,
    gene_counts,
    key_mask,
):
    cells_here, span, width = tokens.shape
    head_size = width // HEADS
    length = span * lax.axis_size("seq")
    start = lax.axis_index("seq") * span
    seq_count, cell_count = lax.axis_size("seq"), lax.axis_size("cells")
    me = jnp.stack([lax.axis_index("seq"), lax.axis_index("cells")]).astype(jnp.int32)
    totals = prefix_lengths + gene_counts
    row_count = cells_here * span
    own_rows = start + jnp.arange(span)
    heads_here = -(-HEADS // seq_count)
    head_total = heads_here * seq_count
    features = -(-(width + 1) // LANES) * LANES
    scalars = [jnp.concatenate([me, prefix_lengths[c : c + 1]]) for c in range(cells_here)]

    def flat(array):
        return array.reshape(row_count, array.shape[-1])

    def own_heads(array, at):
        lead = array.shape[:at]
        pad = [(0, 0)] * array.ndim
        pad[at] = (0, (head_total - HEADS) * head_size)
        array = jnp.pad(array, pad)
        here = heads_here * head_size
        array = lax.dynamic_slice_in_dim(array, me[0] * here, here, axis=at)
        return array.reshape(lead + (heads_here, head_size))

    def padded_heads(array, fills=()):
        room = HEAD_PAD - head_size
        tail = jnp.array(list(fills) + [0.0] * (room - len(fills)), array.dtype)
        tail = jnp.broadcast_to(tail, array.shape[:-1] + (room,))
        return jnp.concatenate([array, tail], axis=-1)

    bias_parts = (
        padded_heads(own_heads(query_bias, 0), (1.0,)),
        padded_heads(jnp.zeros((heads_here, head_size), jnp.float32), (0.0, 1.0, 1.0, 1.0)),
        padded_heads(own_heads(value_bias, 0), (1.0, 1.0, 1.0, 1.0)),
    )
    groups = head_groups(heads_here)
    bias = jnp.concatenate([p[h : h + n] for h, n, _ in groups for p in bias_parts]).reshape(-1, 1)

    open_here = (key_mask == 1) & (own_rows[None, :] < totals[:, None])
    hidden = jnp.where(open_here, 0.0, MASKED).astype(jnp.float32)
    nothing = jnp.zeros_like(first_gain)
    lines = jnp.stack(
        [first_gain, first_shift, second_gain, second_shift, out_bias, down_bias]
        + [nothing, nothing]
    )
    tokens_turned = tokens.transpose(0, 2, 1)
    cotangent_turned = cotangent.transpose(0, 2, 1)
    down_turned = down_weight.T
    normed = first_norm(tokens_turned, lines, hidden, features)
    weight, *weights_turned = own_weights(
        order_after(scalars[0], normed), mix_weight, features, seq_count, heads_here, head_size
    )
    own_cotangent = order_after(flat(cotangent), normed)
    x_bits = [b for b in reversed(bits_of(seq_count)) if b > 1]
    near = swap_with(jnp.stack(normed), "seq", 1)
    held = [{0: normed[c]} for c in range(cells_here)]
    earlier = ()
    for c in range(cells_here):
        for bit in x_bits:
            for r, block in list(held[c].items()):
                held[c][r | bit] = swap_with(order_after(block, *earlier), "seq", bit)
        earlier = (held[c][x_bits[0]], weight)
    back_active = active_back(
        scalars[0], order_after(own_cotangent, weight, held[0]), down_turned
    )
    normed_blocks = []
    for c in range(cells_here):
        after = (weight,) if c == 0 else (back_active,)
        for r, block in list(held[c].items()):
            held[c][r | 1] = near[c] if r == 0 else swap_with(order_after(block, *after), "seq", 1)
        normed_blocks.append([held[c][r] for r in range(seq_count)])

    attended, kept = [], []
    last = (back_active, bias)
    for c in range(cells_here):
        results = attend_forward(
            scalars[c], order_after(normed_blocks[c], *last), weight, bias, heads_here, head_size
        )
        qkv, out, parts = results[: len(groups)], results[len(groups)], results[len(groups) + 1 :]
        last = (out,)
        kept.append((qkv, out))
        attended.append(exchanged_blocks(parts))
    middle, second, second_turned, attended_turned = [], [], [], []
    for c in range(cells_here):
        results = second_norm(
            scalars[0],
            out_weight,
            tokens_turned[c],
            lines,
            order_after(attended[c], *last),
        )
        last = (results[0],)
        for held, result in zip((middle, second, second_turned, attended_turned), results):
            held.append(result)
    active, back_upper, up_bias_back = hidden_layer(
        scalars[0], second, back_active, up_weight, up_bias.reshape(1, -1)
    )
    (down_send,) = down_outer(scalars[0], cotangent_turned, active, seq_count, cell_count)
    down_got = swap_with(down_send, "seq", 1)
    (up_send,) = up_outer(
        scalars[0], second_turned, order_after(back_upper, down_send), seq_count, cell_count
    )
    up_got = swap_with(up_send, "seq", 1)
    *down_halves, lower_send, lower_keep = down_outer(
        scalars[0], cotangent_turned, order_after(active, up_send), seq_count, cell_count, down_got
    )
    *up_halves, lower_send, lower_keep = up_outer(
        scalars[0],
        second_turned,
        order_after(back_upper, down_halves),
        seq_count,
        cell_count,
        up_got,
        (lower_send, lower_keep),
    )

    def flat_blocks(array):
        return array.reshape((-1,) + array.shape[-2:])

    x_bits = [("seq", b) for b in reversed(bits_of(seq_count)) if b > 1]
    cell_bits = [("cells", b) for b in reversed(bits_of(cell_count))]
    names = x_bits + cell_bits
    y_bit, z_bit = ("cells", 1), ("cells", cell_count // seq_count)
    rest = [n for n in reversed(cell_bits) if n not in (y_bit, z_bit)]
    running = [
        Reduction("down", names, x_bits + [y_bit, z_bit] + rest, *map(flat_blocks, down_halves)),
        Reduction("up", names, [y_bit, z_bit] + x_bits + rest, *map(flat_blocks, up_halves)),
        Reduction(
            "both",
            names,
            [z_bit] + x_bits + [y_bit] + rest,
            flat_blocks(lower_send),
            flat_blocks(lower_keep),
        ),
    ]
    back_middle, back_branch, middle_sums, *back_heads = middle_back(
        scalars[0],
        order_after(back_upper, up_halves),
        up_weight,
        middle,
        lines,
        cotangent_turned,
        out_weight,
        seq_count,
        heads_here,
    )
    back_upper_half = route_upper(back_heads[-1])
    down_part, up_part, both_part = running
    last = down_part.step(back_heads)
    out_shares = out_outer(
        scalars[0],
        attended_turned,
        order_after(back_branch, last),
        seq_count,
        cell_count,
    )
    out_part = Reduction(
        "out",
        [("seq", 1)] + names,
        [("seq", 1), y_bit] + x_bits + [z_bit] + rest,
        flat_blocks(out_shares[seq_count // 2 :]),
        flat_blocks(out_shares[: seq_count // 2]),
    )
    last = advance([up_part, both_part], out_shares)
    back_arrays, back_places = route_rest(back_heads[:-1], order_after(back_upper_half, last))
    last = out_part.step(last)
    running.append(out_part)
    block_out = block_output(
        scalars[0], order_after(active, last), down_turned, middle, lines
    )
    last = block_out
    seq_bits = [("seq", 1)] + x_bits
    mixed_back, mix_parts = [[], []], []
    back_normed, bias_backs = [], []

    def mix_reductions(group, last):
        *halves, sums = mix_outer(
            scalars[0],
            [x for c in normed_blocks for x in c],
            order_after(mixed_back[group], last),
            width,
            cell_count,
        )
        bias_backs.append(sums)
        label = ["first", "second"][group]
        return [
            Reduction(label + " upper", cell_bits, [y_bit, z_bit] + rest, *halves[:2]),
            Reduction(label + " lower", cell_bits, [z_bit, y_bit] + rest, *halves[2:]),
        ], halves[0]

    for c in range(cells_here):
        qkv, out = kept[c]
        final = c == cells_here - 1
        for group, (first_head, _, _) in enumerate(groups):
            weights = weights_turned if group == len(groups) - 1 else None
            back, *sums = attend_backward(
                scalars[c],
                c,
                qkv[group],
                out,
                order_after(back_arrays, last),
                back_places,
                first_head,
                head_size,
                weights,
                [mixed_back[0][c]] if weights else (),
            )
            last = back
            mixed_back[group].append(back)
            if weights:
                back_normed.append(Reduction("normed", seq_bits, seq_bits, *sums, kind=c))
            else:
                running = [part for part in running if part.labels]
                last = advance(running, last)
                if c > 0:
                    last = back_normed[c - 1].step(last)
            if final:
                parts, last = mix_reductions(group, last)
                mix_parts.append(parts)
    ahead = [part for part in running if part.order]
    last = advance(mix_parts[0], (last, [part.got for part in back_normed[:-1]]))
    last = back_normed[-1].step(last)
    done = [part.got for part in running if not part.order]
    last = advance(mix_parts[1] + ahead, (last, done))
    last = advance(mix_parts[0], last)
    while any(part.order for part in back_normed):
        for part in back_normed:
            last = part.step(last) if part.order else last
    terms = [x for part in back_normed for x in (part.keep[0], part.got[0])]
    tokens_gradient, first_sums = tokens_back(
        tokens_turned, lines, back_middle, order_after(terms, last)
    )
    last = tokens_gradient
    running += mix_parts[0] + mix_parts[1]
    running = [part for part in running if part.labels]
    while any(part.order for part in running):
        last = advance(running, last)
    blocks = {}
    for part in running:
        blocks.update(part.finish(last))
    low = blocks["both"].shape[0] // 2

    def ungrouped(block, starts, share):
        pieces = jnp.split(block, len(starts), axis=1)
        cuts = [share * n - start for n, start in enumerate(starts)]
        return jnp.concatenate([p[c : c + share] for p, c in zip(pieces, cuts)])

    down_part = jnp.concatenate([blocks["down"], blocks["both"][:low]])
    down_share = width // seq_count
    down_starts, _ = row_cover(down_share, cell_count // seq_count)
    down_part = ungrouped(down_part, down_starts, down_share // len(down_starts))
    up_part = jnp.concatenate([blocks["up"], blocks["both"][low:]])
    mix_part = jnp.concatenate(
        [
            jnp.concatenate([blocks[g + " upper"], blocks[g + " lower"]])
            for g in ("first", "second")
        ],
        axis=1,
    )
    mix_part = mix_columns(
        scalars[0],
        gathered_blocks(mix_part.astype(jnp.bfloat16), seq_count),
        heads_here,
        head_size,
    )
    group = blocks["out"].shape[0]
    out_part = ungrouped(blocks["out"], [group * n for n in range(seq_count)], group)
    bias_backs = [
        sums.reshape(3, count, HEAD_PAD)[..., :head_size]
        for sums, (_, count, _) in zip(bias_backs, groups)
    ]
    bias_back = jnp.concatenate(bias_backs, axis=1)

    def all_heads(array):
        wide = jnp.zeros((head_total * head_size,), jnp.float32)
        wide = lax.dynamic_update_slice(
            wide, array.reshape(-1), (me[0] * heads_here * head_size,)
        )
        return wide[:width]

    query_bias_back, value_bias_back = all_heads(bias_back[0]), all_heads(bias_back[2])
    def own_rows_of(part, unit=16):
        starts, _ = row_cover(width, cell_count, unit)
        share = width // cell_count
        shift = jnp.array([share * c - starts[c] for c in range(cell_count)])[me[1]]
        return lax.dynamic_slice_in_dim(part, shift, share, axis=0)

    vectors = (
        first_sums[0],
        first_sums[1],
        query_bias_back,
        value_bias_back,
        middle_sums[2],
        middle_sums[0],
        middle_sums[1],
        up_bias_back.reshape(-1),
        middle_sums[3],
    )
    joined = jnp.concatenate([v.reshape(cell_count, -1) for v in vectors], axis=1)
    joined = joined[jnp.arange(cell_count) ^ me[1]]
    names = [("cells", b) for b in reversed(bits_of(cell_count))]
    joined = joined.reshape((2,) * len(names) + joined.shape[1:])
    for axis, bit in list(names):
        place = names.index((axis, bit))
        got = swap_with(lax.index_in_dim(joined, 1, place, keepdims=False), axis, bit)
        joined = lax.index_in_dim(joined, 0, place, keepdims=False) + got
        names.remove((axis, bit))
    for bit in bits_of(seq_count):
        joined = joined + swap_with(joined, "seq", bit)
    ends = [0]
    for v in vectors:
        ends.append(ends[-1] + v.shape[0] // cell_count)
    vectors = [joined[ends[i] : ends[i + 1]] for i in range(len(vectors))]
    matrices = (
        own_rows_of(mix_part),
        own_rows_of(out_part, 16 * seq_count),
        own_rows_of(up_part),
        down_part.T,
    )
    return (
        block_out.transpose(0, 2, 1),
        tokens_gradient.transpose(0, 2, 1),
        vectors[0],
        vectors[1],
        matrices[0],
        vectors[2],
        vectors[3],
        matrices[1],
        vectors[4],
        vectors[5],
        vectors[6],
        matrices[2],
        vectors[7],
        matrices[3],
        vectors[8],
    )


def solution(mesh):
    return jax.shard_map(
        on_device,
        mesh=mesh,
        in_specs=(
            P("cells", "seq", None),
            P(),
            P(),
            P(),
            P(),
            P(),
            P(),
            P(),
            P(),
            P(),
            P(),
            P(),
            P(),
            P(),
            P("cells", "seq", None),
            P("cells"),
            P("cells"),
            P("cells", "seq"),
        ),
        out_specs=(
            P("cells", "seq", None),
            P("cells", "seq", None),
            P("cells"),
            P("cells"),
            P("cells", "seq"),
            P("cells"),
            P("cells"),
            P("cells", "seq"),
            P("cells"),
            P("cells"),
            P("cells"),
            P("cells", "seq"),
            P("cells"),
            P("cells", "seq"),
            P("cells"),
        ),
        check_vma=False,
    )
```

```python
from functools import partial
import math

import jax
import jax.numpy as jnp
from jax import lax
from jax.experimental import pallas as pl
from jax.experimental.pallas import tpu as pltpu
from jax.sharding import PartitionSpec as P

HEADS = 20
LANES = 128
TILE = 256
HEAD_PAD = 64
MASKED = -1e30
ONE_ROW = 56
SPLIT_ROW = 57
VMEM_LIMIT = 20 * 1024 * 1024
SHORT = pl.CostEstimate(flops=1, bytes_accessed=1, transcendentals=0)


COSTS = {'widen': 3, 'attend_forward': 14, 'own_weights': 4}


def cost(name):
    return pl.CostEstimate(flops=COSTS.get(name, 0) * 10**9 + 1, bytes_accessed=1, transcendentals=0)


def bits_of(count):
    return [1 << b for b in range(count.bit_length() - 1)]


def swap_with(array, axis, bit):
    count = lax.axis_size(axis)
    return lax.ppermute(array, axis, [(i, i ^ bit) for i in range(count)])


def without_bit(index, bit):
    return (index // (2 * bit)) * bit + index % bit


def add_halves_kernel(count, *refs):
    for n in range(count):
        mine_away, got_away, mine_here, got_here = refs[4 * n : 4 * n + 4]
        first = sum(refs[4 * p].shape[1] for p in range(n))
        rows = slice(first, first + mine_away.shape[1])
        for mine, got, result in (
            (mine_away, got_away, refs[4 * count]),
            (mine_here, got_here, refs[4 * count + 1]),
        ):
            total = mine[...].astype(jnp.float32) + got[...].astype(jnp.float32)
            result[:, rows, :] = total.astype(jnp.bfloat16)


def add_halves(pairs, bit):
    count, _, width = pairs[0][0].shape
    rows = sum(mine.shape[1] for mine, _ in pairs)
    shape = jax.ShapeDtypeStruct((count // 2, rows, width), jnp.bfloat16)
    in_specs, inputs = [], []
    for mine, got in pairs:
        for value in (bit, 0):
            spec = pl.BlockSpec(
                (1,) + mine.shape[1:],
                lambda g, value=value: ((g // bit) * (2 * bit) + value + g % bit, 0, 0),
            )
            in_specs += [spec, spec]
            inputs += [mine, got]
    out = pl.BlockSpec((1, rows, width), lambda g: (g, 0, 0))
    return pl.pallas_call(
        partial(add_halves_kernel, len(pairs)),
        out_shape=(shape, shape),
        grid=(count // 2,),
        in_specs=in_specs,
        out_specs=(out, out),
        compiler_params=pltpu.CompilerParams(vmem_limit_bytes=VMEM_LIMIT),
        cost_estimate=SHORT,
        name="add_halves",
    )(*inputs)


class Reduction:
    def __init__(self, label, names, order, send, keep, kind=None):
        self.labels = [label]
        self.kind = kind
        self.names, self.order = list(names), list(order)
        self.keep = keep
        self.heights = [keep.shape[1]]
        self.leave(send)

    def leave(self, send):
        axis, bit = self.order.pop(0)
        self.names.remove((axis, bit))
        self.got = swap_with(send, axis, bit)

    def step(self, last, *others):
        place = self.names.index(self.order[0])
        bit = 1 << (len(self.names) - 1 - place)
        pairs = [order_after((p.keep, p.got), last) for p in (self,) + others]
        for other in others:
            assert (other.names, other.order) == (self.names, self.order)
            self.heights += other.heights
            self.labels += other.labels
            other.labels, other.order = [], []
        send, self.keep = add_halves(pairs, bit)
        self.leave(send)
        return self.keep

    def finish(self, last):
        while self.order:
            last = self.step(last)
        total = order_after(self.keep, last).astype(jnp.float32) + self.got.astype(jnp.float32)
        ends = [sum(self.heights[:n]) for n in range(len(self.heights) + 1)]
        return {label: total[0, a:b] for label, a, b in zip(self.labels, ends, ends[1:])}


def row_cover(rows, count, unit=16):
    share = rows // count
    starts = [share * c // 8 * 8 for c in range(count)]
    height = max(share * (c + 1) - starts[c] for c in range(count))
    height = -(-height // unit) * unit
    return [min(s, rows - height) for s in starts], height


def head_groups(heads):
    first = -(-heads * 3 // 5)
    return [(0, first, 0), (first, heads - first, 3 * first)]


def no_grid_call(body, out_shape, name, flops, inputs, scratch, scalars=1):
    in_specs = [pl.BlockSpec(memory_space=pltpu.SMEM)] * scalars
    in_specs += [pl.BlockSpec(memory_space=pltpu.VMEM)] * (len(inputs) - scalars)
    moved = sum(x.size * x.dtype.itemsize for x in inputs)
    moved += sum(math.prod(x.shape) * x.dtype.itemsize for x in jax.tree.leaves(out_shape))
    return pl.pallas_call(
        body,
        out_shape=out_shape,
        in_specs=in_specs,
        out_specs=jax.tree.map(lambda _: pl.BlockSpec(memory_space=pltpu.VMEM), out_shape),
        scratch_shapes=scratch,
        compiler_params=pltpu.CompilerParams(vmem_limit_bytes=VMEM_LIMIT),
        cost_estimate=cost(name),
        name=name,
    )(*inputs)


def make_diagonal(diag_ref, keys, tile, prefix):
    first = tile * TILE
    shape = (TILE, TILE)
    key_at = lax.broadcasted_iota(jnp.int32, shape, 0)
    row_at = lax.broadcasted_iota(jnp.int32, shape, 1)
    opened = keys[first : first + TILE, ONE_ROW : ONE_ROW + 1].astype(jnp.float32) > -1.0
    near = (key_at <= row_at) | (key_at + first < prefix)
    seen = (near & opened) | (key_at == row_at)
    diag_ref[tile] = jnp.where(seen, 0.0, MASKED)


def without_mask(keys):
    lane = lax.broadcasted_iota(jnp.int32, keys.shape, 1)
    return jnp.where(lane == ONE_ROW, 0.0, keys.astype(jnp.float32)).astype(jnp.bfloat16)


def turned_rows(columns):
    return columns.astype(jnp.float32).T.astype(jnp.bfloat16)


def split_rows(columns, value):
    row = lax.broadcasted_iota(jnp.int32, columns.shape, 0)
    result = columns.astype(jnp.float32)
    for place in range(3):
        part = value.astype(jnp.bfloat16).astype(jnp.float32)
        value = value - part
        result = jnp.where(row == SPLIT_ROW + place, part, result)
    return result.astype(jnp.bfloat16)


def forward_kernel(seq_count, cell, span, heads, head_size, rate, scalars, *refs):
    blocks, (weight, bias, gain, shift) = refs[:seq_count], refs[seq_count : seq_count + 4]
    groups = head_groups(heads)
    *qkv_groups, out, normed = refs[seq_count + 4 : seq_count + 6 + len(groups)]
    *parts, rows, diag, scores = refs[seq_count + 6 + len(groups) :]
    width = gain.shape[0]
    gain, shift = columns_of(gain, shift)
    me, prefix = scalars[0], scalars[2 + cell]
    length = span * seq_count
    tiles = length // TILE
    for r in range(seq_count):
        here = slice(r * span, (r + 1) * span)
        normal, _ = centred_columns(blocks[r][:width, :].astype(jnp.float32))
        normed[:width, here] = (normal * gain + shift).astype(jnp.bfloat16)
        normed[width:, here] = blocks[r][width:, :]
        mixed = jnp.dot(weight[...], normed[:, here], preferred_element_type=jnp.float32)
        mixed = (mixed + bias[...]).astype(jnp.bfloat16)
        place = pl.ds(pl.multiple_of((me ^ r) * span, LANES), span)
        mixed = mixed.reshape(3 * heads, HEAD_PAD, span)
        for (_, count, base), qkv in zip(groups, qkv_groups):
            qkv[:, :, place] = mixed[base : base + 3 * count]

    def turn(first, count, qkv, h, carry):
        rows[first + h] = turned_rows(qkv[count + h])
        return carry

    for (first, count, _), qkv in zip(groups, qkv_groups):
        lax.fori_loop(0, count, partial(turn, first, count, qkv), 0)
    for tile in range(tiles):
        make_diagonal(diag, rows.at[0], tile, prefix)

    def one_head(start, count, qkv, h, carry):
        for tile in range(tiles):
            across = slice(tile * TILE, (tile + 1) * TILE)
            query = qkv[h, :, across]
            tops = None
            for j in range(tile + 1):
                down = slice(j * TILE, (j + 1) * TILE)
                keys = rows[start + h, down, :]
                if j == tile:
                    keys = without_mask(keys)
                block = jnp.dot(keys, query, preferred_element_type=jnp.float32)
                if j == tile:
                    block = block + diag[tile]
                scores[down, :] = block
                top = jnp.max(block.reshape(TILE // 8, 8, TILE), axis=0)
                tops = top if tops is None else jnp.maximum(tops, top)
            top = jnp.max(tops, axis=0, keepdims=True)
            total = jnp.zeros((HEAD_PAD, TILE), jnp.float32)
            for j in range(tile + 1):
                down = slice(j * TILE, (j + 1) * TILE)
                probs = jnp.exp2((scores[down, :] - top) * rate).astype(jnp.bfloat16)
                total += jnp.dot(
                    qkv[2 * count + h, :, down], probs, preferred_element_type=jnp.float32
                )
            summed = total[ONE_ROW : ONE_ROW + 1]
            row = lax.broadcasted_iota(jnp.int32, total.shape, 0)
            log_sum = top * rate + jnp.log2(summed)
            out[start + h, :, across] = jnp.where(row == ONE_ROW, log_sum, total / summed)
        return carry

    for (first, count, _), qkv in zip(groups, qkv_groups):
        lax.fori_loop(0, count, partial(one_head, first, count, qkv), 0)
    for r in range(seq_count):
        place = pl.ds(pl.multiple_of((me ^ r) * span, LANES), span)
        piece = out[:, :head_size, place].reshape(heads * head_size, span)
        parts[r][...] = piece.astype(jnp.bfloat16)


def backward_kernel(seq_count, places, cell, span, first_head, heads, head_size, rate, scalars, *refs):
    qkv, out, *arrays, result = refs[:-6]
    back, query_rows, key_rows, value_rows, gathered, diag = refs[-6:]
    me, prefix = scalars[0], scalars[2 + cell]
    length = span * seq_count
    tiles = length // TILE
    scale = 1.0 / math.sqrt(head_size)
    for r in range(seq_count):
        place = pl.ds(pl.multiple_of((me ^ r) * span, LANES), span)
        gathered[:, :, place] = arrays[places[r][0]][
            places[r][1], cell, first_head : first_head + heads
        ]
    key_rows[...] = turned_rows(qkv[heads])
    for tile in range(tiles):
        make_diagonal(diag, key_rows, tile, prefix)

    def one_head(h, carry):
        key_rows[...] = turned_rows(qkv[heads + h])
        value_rows[...] = turned_rows(qkv[2 * heads + h])
        held = gathered[h]
        centre = jnp.sum(
            held[:head_size].astype(jnp.float32) * out[first_head + h, :head_size],
            axis=0,
            keepdims=True,
        )
        gathered[h] = split_rows(held, -centre)
        log_sum = out[first_head + h, ONE_ROW : ONE_ROW + 1, :]
        qkv_q = split_rows(qkv[h], -log_sum / rate)
        query_rows[...] = jnp.zeros_like(query_rows)
        for j in range(tiles):
            down = slice(j * TILE, (j + 1) * TILE)
            keys, values = key_rows[down, :], value_rows[down, :]
            keys_column = qkv[heads + h, :, down]
            keys_back = jnp.zeros((TILE, HEAD_PAD), jnp.float32)
            values_back = jnp.zeros((TILE, HEAD_PAD), jnp.float32)
            for i in range(j, tiles):
                across = slice(i * TILE, (i + 1) * TILE)
                query = qkv_q[:, across]
                back_out = gathered[h, :, across]
                if i == j:
                    block = jnp.dot(without_mask(keys), query, preferred_element_type=jnp.float32)
                    block = block + diag[i]
                else:
                    block = jnp.dot(keys, query, preferred_element_type=jnp.float32)
                probs = jnp.exp2(block * rate)
                back_probs = jnp.dot(values, back_out, preferred_element_type=jnp.float32)
                back_scores = (probs * back_probs).astype(jnp.bfloat16)
                probs = probs.astype(jnp.bfloat16)
                turned = (((1,), (1,)), ((), ()))
                values_back += lax.dot_general(
                    probs, back_out, turned, preferred_element_type=jnp.float32
                )
                keys_back += lax.dot_general(
                    back_scores, query, turned, preferred_element_type=jnp.float32
                )
                query_rows[:, across] += jnp.dot(
                    keys_column, back_scores, preferred_element_type=jnp.float32
                )
            back[heads + h, down, :] = (keys_back * scale).astype(jnp.bfloat16)
            back[2 * heads + h, down, :] = values_back.astype(jnp.bfloat16)
        back[h] = (query_rows[...] * scale).T.astype(jnp.bfloat16)
        return carry

    lax.fori_loop(0, heads, one_head, 0)
    for block in range(seq_count):
        here = slice(block * span, (block + 1) * span)
        there = pl.ds(pl.multiple_of((me ^ block) * span, LANES), span)
        for first in range(0, 3 * heads, 2):
            pieces = [back[p, here, :] for p in range(first, min(first + 2, 3 * heads))]
            joined = pieces[0] if len(pieces) == 1 else jnp.concatenate(pieces, axis=1)
            left = first * HEAD_PAD
            result[there, left : left + joined.shape[1]] = joined

def attend_forward(scalars, cell, blocks, weight, bias, gain, shift, heads, head_size):
    seq_count, span = len(blocks), blocks[0].shape[1]
    length = seq_count * span
    rate = math.log2(math.e) / math.sqrt(head_size)
    flops = 2 * weight.size * length + 4 * heads * HEAD_PAD * length * length
    return no_grid_call(
        partial(forward_kernel, seq_count, cell, span, heads, head_size, rate),
        tuple(
            jax.ShapeDtypeStruct((3 * count, HEAD_PAD, length), jnp.bfloat16)
            for _, count, _ in head_groups(heads)
        )
        + (
            jax.ShapeDtypeStruct((heads, HEAD_PAD, length), jnp.float32),
            jax.ShapeDtypeStruct((blocks[0].shape[0], length), jnp.bfloat16),
        )
        + (jax.ShapeDtypeStruct((heads * head_size, span), jnp.bfloat16),) * seq_count,
        "attend_forward",
        flops,
        [scalars, *blocks, weight, bias, gain, shift],
        [
            pltpu.VMEM((heads, length, HEAD_PAD), jnp.bfloat16),
            pltpu.VMEM((length // TILE, TILE, TILE), jnp.float32),
            pltpu.VMEM((length, TILE), jnp.float32),
        ],
    )


def attend_backward(scalars, cell, qkv, out, arrays, places, first_head, head_size):
    seq_count, span = len(places), arrays[0].shape[-1]
    heads = qkv.shape[0] // 3
    length = seq_count * span
    rate = math.log2(math.e) / math.sqrt(head_size)
    return no_grid_call(
        partial(
            backward_kernel, seq_count, places, cell, span, first_head, heads, head_size, rate
        ),
        jax.ShapeDtypeStruct((length, 3 * heads * HEAD_PAD), jnp.bfloat16),
        "attend_backward",
        1,
        [scalars, qkv, out, *arrays],
        [
            pltpu.VMEM((3 * heads, length, HEAD_PAD), jnp.bfloat16),
            pltpu.VMEM((HEAD_PAD, length), jnp.float32),
            pltpu.VMEM((length, HEAD_PAD), jnp.bfloat16),
            pltpu.VMEM((length, HEAD_PAD), jnp.bfloat16),
            pltpu.VMEM((heads, HEAD_PAD, length), jnp.bfloat16),
            pltpu.VMEM((length // TILE, TILE, TILE), jnp.float32),
        ],
    )


def normed_back_kernel(seq_count, count, *refs):
    weights, backs = refs[:count], refs[count : 2 * count]
    tokens, results = refs[2 * count : 2 * count + seq_count], refs[2 * count + seq_count : -1]
    sums = refs[-1]
    width, span = results[0].shape
    totals = [0.0] * 2
    for r in range(seq_count):
        rows = slice(r * span, (r + 1) * span)
        back = sum(dot_turned(w[...], part[rows, :]) for w, part in zip(weights, backs))
        results[r][...] = back.astype(jnp.bfloat16)
        normal, _ = centred_columns(tokens[r][:width, :].astype(jnp.float32))
        for n, term in enumerate((back * normal, back)):
            totals[n] = totals[n] + jnp.sum(term, axis=1, keepdims=True)
    sums[...] = lines_of(totals)


def normed_back(weights, backs, tokens):
    seq_count = len(tokens)
    span = backs[0].shape[0] // seq_count
    width = weights[0].shape[0]
    shape = jax.ShapeDtypeStruct((width, span), jnp.bfloat16)
    return no_grid_call(
        partial(normed_back_kernel, seq_count, len(backs)),
        (shape,) * seq_count + (jax.ShapeDtypeStruct((8, width), jnp.float32),),
        "normed_back",
        1,
        [*weights, *backs, *tokens],
        [],
        scalars=0,
    )


def mix_outer_kernel(cell_count, share, cuts, count, scalars, *refs):
    normed, backs, (*results, sums, whole_sum) = refs[:count], refs[count : 2 * count], refs[2 * count :]
    features, width = whole_sum.shape
    sums[...] = sum(
        jnp.sum(back[...].astype(jnp.float32), axis=0, keepdims=True) for back in backs
    )
    for first, last in chunks(width):
        whole_sum[:, first:last] = sum(
            dot(left[:features, :], back[:, first:last]) for left, back in zip(normed, backs)
        )
    for k in range(cell_count):
        c = k ^ scalars[1]
        start = jnp.minimum(lax.div(c * share, 8) * 8, features - cuts[-1])
        block = whole_sum[pl.ds(pl.multiple_of(start, 8), cuts[-1]), :].astype(jnp.bfloat16)
        for n, bit in enumerate((1, 2)):
            target = results[2 * n + (0 if k & bit else 1)]
            target[without_bit(k, bit)] = block[cuts[n] : cuts[n + 1]]


def mix_outer(scalars, normed, backs, features, cell_count):
    _, height = row_cover(features, cell_count)
    cuts = (0, -(-height // 2 // 16) * 16, height)
    width = backs[0].shape[1]
    halves = [(cell_count // 2, cuts[n + 1] - cuts[n], width) for n in (0, 0, 1, 1)]
    return no_grid_call(
        partial(mix_outer_kernel, cell_count, features // cell_count, cuts, len(backs)),
        tuple(jax.ShapeDtypeStruct(shape, jnp.bfloat16) for shape in halves)
        + (jax.ShapeDtypeStruct((1, width), jnp.float32),),
        "mix_outer",
        1,
        [scalars, *normed, *backs],
        [pltpu.VMEM((features, width), jnp.float32)],
    )


def gathered_blocks(block, seq_count):
    held = {0: block}
    for bit in list(reversed(bits_of(seq_count))):
        held.update({r | bit: swap_with(x, "seq", bit) for r, x in list(held.items())})
    return [held[r] for r in range(seq_count)]


class PositionSum:
    def __init__(self, blocks):
        self.held = dict(enumerate(blocks))
        self.bits = bits_of(len(blocks))
        self.leave()

    def leave(self):
        bit = self.bits.pop(0)
        self.got = {r: swap_with(self.held[r | bit], "seq", bit) for r in self.held if not r & bit}

    def step(self, last):
        held, got = order_after((self.held, self.got), last)
        self.held = {r: add_low(held[r], x) for r, x in got.items()}
        self.leave()
        return self.held[0]

    def terms(self):
        return [self.held[0], self.got[0]]


class VectorSum:
    def __init__(self, blocks, seq_count):
        cells = [("cells", bit) for bit in reversed(bits_of(blocks.shape[0]))]
        self.order = cells + [("seq", bit) for bit in bits_of(seq_count)]
        self.leave(blocks)

    def leave(self, blocks):
        axis, bit = self.order.pop(0)
        half = blocks.shape[0] // 2 if axis == "cells" else 0
        self.keep = blocks[:half] if half else blocks
        self.got = swap_with(blocks[half:], axis, bit)

    def step(self, last):
        keep, got = order_after((self.keep, self.got), last)
        self.keep = keep + got
        if self.order:
            self.leave(self.keep)
        return self.keep


def add_low(left, right):
    return (left.astype(jnp.float32) + right.astype(jnp.float32)).astype(jnp.bfloat16)


def route_upper(upper):
    return swap_with(upper, "seq", upper.shape[0])


def route_rest(lower, got):
    seq_count = 2 * len(lower)
    arrays = [x[None] for x in lower] + [got]
    held = {r: (r, 0) for r in range(len(lower))}
    held.update({len(lower) + r: (len(lower), r) for r in range(len(lower))})
    for bit in list(reversed(bits_of(seq_count)))[1:]:
        away = [r for r in held if r & bit]
        arrays.append(swap_with(jnp.stack([arrays[held[r][0]][held[r][1]] for r in away]), "seq", bit))
        held.update({r: (len(arrays) - 1, n) for n, r in enumerate(away)})
    return arrays, [held[r] for r in range(seq_count)]


def exchanged_blocks(blocks):
    return [blocks[0]] + [swap_with(blocks[r], "seq", r) for r in range(1, len(blocks))]


def chunks(width):
    return [(first, min(first + TILE, width)) for first in range(0, width, TILE)]


def dot(left, right):
    return jnp.dot(left, right, preferred_element_type=jnp.float32)


def dot_turned(left, right):
    return lax.dot_general(
        left, right, (((1,), (1,)), ((), ())), preferred_element_type=jnp.float32
    )


def centred_columns(values):
    centred = values - jnp.mean(values, axis=0, keepdims=True)
    spread = jnp.mean(centred * centred, axis=0, keepdims=True)
    rise = lax.rsqrt(spread + 1e-05)
    return centred * rise, rise


def norm_pull(normal, rise, back, gain):
    scaled = back * gain
    inner = scaled - jnp.mean(scaled, axis=0, keepdims=True)
    inner = inner - normal * jnp.mean(scaled * normal, axis=0, keepdims=True)
    return rise * inner


def columns_of(*vectors):
    rows = [vector[...].reshape(1, -1) for vector in vectors]
    rows += [jnp.zeros_like(rows[0])] * (8 - len(rows))
    turned = jnp.concatenate(rows, axis=0).T
    return [turned[:, n : n + 1] for n in range(len(vectors))]


def lines_of(columns):
    rows = columns[0].shape[0]
    room = [jnp.zeros((rows, 8 - len(columns)), jnp.float32)] if len(columns) < 8 else []
    return jnp.concatenate(list(columns) + room, axis=1).T


def widen_kernel(cell, cells, scalars, tokens, key_mask, result):
    width, span = tokens.shape[1:]
    place = lax.broadcasted_iota(jnp.int32, (1, span), 1) + scalars[0] * span
    result[:width, :] = tokens[0]
    seen = (key_mask[cell : cell + 1, :] == 1) & (place < scalars[2 + cells + cell])
    shape = (result.shape[0] - width, span)
    mark = lax.broadcasted_iota(jnp.int32, shape, 0) == 0
    hidden = jnp.where(seen, 0.0, MASKED)
    result[width:, :] = jnp.where(mark, hidden, 0.0).astype(jnp.bfloat16)


def widen(scalars, cell, tokens, key_mask, features):
    cells, width, span = tokens.shape
    return grid_call(
        partial(widen_kernel, cell, cells),
        (1,),
        [pl.BlockSpec((1, width, span), lambda g, me: (cell, 0, 0)), whole(key_mask)],
        pl.BlockSpec((features, span), lambda g, me: (0, 0)),
        jax.ShapeDtypeStruct((features, span), jnp.bfloat16),
        [],
        "widen",
        1,
        (scalars, tokens, key_mask),
        1,
    )


def second_norm_kernel(seq_count, scalars, weight, tokens, gain, shift, bias, *refs):
    parts = refs[:seq_count]
    middle, second, second_turned, attended, gather = refs[seq_count:]
    share = parts[0].shape[0]
    gain, shift, bias = columns_of(gain, shift, bias)
    for r in range(seq_count):
        place = pl.ds(pl.multiple_of((scalars[0] ^ r) * share, 8), share)
        gather[place, :] = parts[r][...].astype(jnp.float32)
    attended[...] = gather[: attended.shape[0], :].astype(jnp.bfloat16)
    total = dot(weight[...].T, attended[...])
    total = tokens[...].astype(jnp.float32) + (total + bias)
    middle[...] = total
    normal, _ = centred_columns(total)
    normed = (normal * gain + shift).astype(jnp.bfloat16)
    second_turned[...] = normed
    second[...] = normed.T


def second_norm(scalars, weight, tokens, vectors, parts):
    width, span = tokens.shape
    seq_count = len(parts)
    return no_grid_call(
        partial(second_norm_kernel, seq_count),
        (
            jax.ShapeDtypeStruct((width, span), jnp.float32),
            jax.ShapeDtypeStruct((span, width), jnp.bfloat16),
            jax.ShapeDtypeStruct((width, span), jnp.bfloat16),
            jax.ShapeDtypeStruct((width, span), jnp.bfloat16),
        ),
        "second_norm",
        2 * span * width * width,
        [scalars, weight, tokens, *vectors, *parts],
        [pltpu.VMEM((seq_count * parts[0].shape[0], span), jnp.float32)],
    )


def weights_kernel(seq_count, heads, head_size, scalars, mix, query, value, weight, bias, *turned):
    width = mix.shape[0]
    here = heads * head_size
    groups = head_groups(heads)
    weight[...] = jnp.zeros_like(weight)
    vectors = columns_of(query, value)
    row = lax.broadcasted_iota(jnp.int32, (HEAD_PAD, 1), 0)
    for _, count, base in groups:
        for p, least in ((0, (ONE_ROW, ONE_ROW + 1)), (1, (SPLIT_ROW, HEAD_PAD)), (2, (ONE_ROW, HEAD_PAD))):
            fill = jnp.where((row >= least[0]) & (row < least[1]), 1.0, 0.0)
            for n in range(count):
                place = (base + p * count + n) * HEAD_PAD
                bias[place : place + HEAD_PAD, :] = fill
    for s in range(seq_count):

        @pl.when(scalars[0] == s)
        def _():
            for p in range(3):
                first = s * here
                last = min(first + here, width)
                if last <= first:
                    continue
                start = (p * width + first) // LANES * LANES
                stop = min(-(-(p * width + last) // LANES) * LANES, mix.shape[1])
                block = mix[:, start:stop].astype(jnp.float32)
                block = block[:, p * width + first - start : p * width + last - start].T
                for group_first, count, base in groups:
                    for n in range(count):
                        h = group_first + n
                        if (h + 1) * head_size > last - first:
                            continue
                        place = (base + p * count + n) * HEAD_PAD
                        piece = block[h * head_size : (h + 1) * head_size]
                        room = jnp.zeros((HEAD_PAD - head_size, width), jnp.float32)
                        piece = jnp.concatenate([piece, room])
                        weight[place : place + HEAD_PAD, :width] = piece.astype(jnp.bfloat16)
                        if p != 1:
                            own = vectors[p // 2][first + h * head_size : first + (h + 1) * head_size]
                            bias[place : place + head_size, :] = own

    room = weight.shape[1] - width
    for (_, count, base), columns in zip(groups, turned):
        rows = slice(base * HEAD_PAD, (base + 3 * count) * HEAD_PAD)
        columns[...] = weight[rows, :width].T
        rows = slice((base + count) * HEAD_PAD, (base + 2 * count) * HEAD_PAD)
        row = lax.broadcasted_iota(jnp.int32, (count * HEAD_PAD, room), 0)
        lane = lax.broadcasted_iota(jnp.int32, (count * HEAD_PAD, room), 1)
        mark = (lane == 0) & (lax.rem(row, HEAD_PAD) == ONE_ROW)
        weight[rows, width:] = jnp.where(mark, 1.0, 0.0).astype(jnp.bfloat16)


def own_weights(scalars, mix, query, value, features, seq_count, heads, head_size):
    width = mix.shape[0]
    return no_grid_call(
        partial(weights_kernel, seq_count, heads, head_size),
        (
            jax.ShapeDtypeStruct((3 * heads * HEAD_PAD, features), jnp.bfloat16),
            jax.ShapeDtypeStruct((3 * heads * HEAD_PAD, 1), jnp.float32),
        )
        + tuple(
            jax.ShapeDtypeStruct((width, 3 * count * HEAD_PAD), jnp.bfloat16)
            for _, count, _ in head_groups(heads)
        ),
        "own_weights",
        1,
        [scalars, mix, query, value],
        [],
    )


def active_back_kernel(cotangent, down, result):
    for first, last in chunks(down.shape[1]):
        result[:, first:last] = dot(cotangent[...], down[:, first:last])


def active_back(scalars, cotangent, down):
    rows, width = cotangent.shape
    tile = hidden_tile(down.shape[1])
    shape = jax.ShapeDtypeStruct((rows, down.shape[1]), jnp.float32)
    return grid_call(
        lambda me, *refs: active_back_kernel(*refs),
        (down.shape[1] // tile,),
        [whole(cotangent), pl.BlockSpec((width, tile), lambda g, me: (0, g))],
        pl.BlockSpec((rows, tile), lambda g, me: (0, g)),
        shape,
        [],
        "active_back",
        1,
        (scalars, cotangent, down),
        1,
    )


def hidden_kernel(back_active, up, up_bias, *refs):
    *parts, active, back_upper, bias_back, second = refs

    @pl.when(pl.program_id(0) == 0)
    def _():
        for c, part in enumerate(parts):
            second[c * part.shape[0] : (c + 1) * part.shape[0], :] = part[...]

    inner = math.sqrt(2.0 / math.pi)
    for first, last in chunks(up.shape[1]):
        upper = dot(second[...], up[:, first:last]) + up_bias[:, first:last]
        back = back_active[:, first:last]
        square = upper * upper
        bend = jnp.tanh(inner * upper * (1.0 + 0.044715 * square))
        half = 0.5 + 0.5 * bend
        slope = half + (0.5 * inner) * upper * (1.0 - bend * bend) * (1.0 + 0.134145 * square)
        active[:, first:last] = (upper * half).astype(jnp.bfloat16)
        back = (back * slope).astype(jnp.bfloat16)
        back_upper[:, first:last] = back
        bias_back[:, first:last] = jnp.sum(back.astype(jnp.float32), axis=0, keepdims=True)


def grid_call(
    body, grid, in_specs, out_specs, out_shape, scratch, name, flops, inputs, moved, aliases=None
):
    return pl.pallas_call(
        body,
        out_shape=out_shape,
        grid_spec=pltpu.PrefetchScalarGridSpec(
            num_scalar_prefetch=1,
            grid=grid,
            in_specs=in_specs,
            out_specs=out_specs,
            scratch_shapes=scratch,
        ),
        compiler_params=pltpu.CompilerParams(vmem_limit_bytes=VMEM_LIMIT),
        cost_estimate=cost(name),
        input_output_aliases=aliases or {},
        name=name,
    )(*inputs)


def whole(array):
    zeros = (0,) * array.ndim
    return pl.BlockSpec(array.shape, lambda g, me: zeros)


def hidden_tile(hidden):
    return max(t for t in range(LANES, 1024, LANES) if hidden % t == 0)


def hidden_layer(scalars, second, back_active, up, up_bias):
    rows = sum(part.shape[0] for part in second)
    width = up.shape[0]
    hidden = up.shape[1]
    tile = hidden_tile(hidden)
    weight = pl.BlockSpec((width, tile), lambda g, me: (0, g))
    out = pl.BlockSpec((rows, tile), lambda g, me: (0, g))
    line = pl.BlockSpec((1, tile), lambda g, me: (0, g))
    return grid_call(
        lambda me, *refs: hidden_kernel(*refs),
        (hidden // tile,),
        [out, weight, line] + [whole(part) for part in second],
        [out, out, line],
        (
            jax.ShapeDtypeStruct((rows, hidden), jnp.bfloat16),
            jax.ShapeDtypeStruct((rows, hidden), jnp.bfloat16),
            jax.ShapeDtypeStruct((1, hidden), jnp.float32),
        ),
        [pltpu.VMEM((rows, width), jnp.bfloat16)],
        "hidden_layer",
        4 * rows * up.size,
        (scalars, back_active, up, up_bias, *second),
        4 * up.size + 4 * rows * hidden,
    )


def middle_back_kernel(
    seq_count,
    cells,
    scalars,
    back_upper,
    up,
    gain,
    cotangent,
    weight,
    *refs,
):
    middle, (back_middle, back_branch, sums) = refs[:cells], refs[cells : cells + 3]
    *parts, total, back_heads = refs[cells + 3 :]
    half = seq_count // 2
    step = pl.program_id(0)

    @pl.when(step == 0)
    def _():
        total[...] = jnp.zeros_like(total)

    for first, last in chunks(total.shape[1]):
        total[:, first:last] += dot_turned(up[...], back_upper[first:last, :])

    @pl.when(step == pl.num_programs(0) - 1)
    def _():
        span = cotangent.shape[2]
        heads = parts[0].shape[1]
        head_size = back_heads.shape[0] // (seq_count * heads)
        (gain_column,) = columns_of(gain)
        totals = [0.0] * 4
        for c in range(cells):
            here = slice(c * span, (c + 1) * span)
            normal, rise = centred_columns(middle[c][...])
            back = total[:, here]
            back_out = cotangent[c].astype(jnp.float32)
            back_mid = back_out + norm_pull(normal, rise, back, gain_column)
            back_middle[:, here] = back_mid
            branch = back_mid.astype(jnp.bfloat16)
            back_branch[:, here] = branch
            for n, term in enumerate((back * normal, back, branch.astype(jnp.float32), back_out)):
                totals[n] = totals[n] + jnp.sum(term, axis=1, keepdims=True)
            back_heads[: weight.shape[0], :] = dot(weight[...], branch)
            if back_heads.shape[0] > weight.shape[0]:
                rest = back_heads.shape[0] - weight.shape[0]
                back_heads[weight.shape[0] :, :] = jnp.zeros((rest, span), jnp.float32)
            for r in range(seq_count):
                first = (scalars[0] ^ r) * heads * head_size
                part = back_heads[pl.ds(pl.multiple_of(first, 8), heads * head_size), :]
                room = jnp.zeros((heads, HEAD_PAD - head_size, span), jnp.float32)
                part = jnp.concatenate([part.reshape(heads, head_size, span), room], axis=1)
                target = parts[r].at[c] if r < half else parts[half].at[r - half, c]
                target[...] = part.astype(jnp.bfloat16)
        sums[...] = lines_of(totals)


def middle_back(scalars, back_upper, up, middle, gain, cotangent, weight, seq_count, heads):
    rows, hidden = back_upper.shape
    cells, width, span = cotangent.shape
    head_size = width // HEADS
    tile = hidden_tile(hidden)
    outs = [
        jax.ShapeDtypeStruct((width, rows), jnp.float32),
        jax.ShapeDtypeStruct((width, rows), jnp.bfloat16),
        jax.ShapeDtypeStruct((8, width), jnp.float32),
    ]
    block = (cells, heads, HEAD_PAD, span)
    outs += [jax.ShapeDtypeStruct(block, jnp.bfloat16)] * (seq_count // 2)
    outs += [jax.ShapeDtypeStruct((seq_count // 2,) + block, jnp.bfloat16)]
    return grid_call(
        partial(middle_back_kernel, seq_count, cells),
        (hidden // tile,),
        [
            pl.BlockSpec((rows, tile), lambda g, me: (0, g)),
            pl.BlockSpec((width, tile), lambda g, me: (0, g)),
            whole(gain),
            whole(cotangent),
            whole(weight),
        ]
        + [whole(m) for m in middle],
        [whole(o) for o in outs],
        outs,
        [
            pltpu.VMEM((width, rows), jnp.float32),
            pltpu.VMEM((seq_count * heads * head_size, span), jnp.float32),
        ],
        "middle_back",
        2 * rows * up.size + 2 * rows * width * width,
        (scalars, back_upper, up, gain, cotangent, weight, *middle),
        1,
    )


def block_out_kernel(active, down, bias, *refs):
    *middle, result, total = refs
    step = pl.program_id(0)

    @pl.when(step == 0)
    def _():
        (bias_column,) = columns_of(bias)
        for c, part in enumerate(middle):
            span = part.shape[1]
            total[:, c * span : (c + 1) * span] = part[...] + bias_column

    for first, last in chunks(total.shape[1]):
        total[:, first:last] += dot_turned(down[...], active[first:last, :])

    @pl.when(step == pl.num_programs(0) - 1)
    def _():
        cells, _, span = result.shape
        for c in range(cells):
            result[c] = total[:, c * span : (c + 1) * span].astype(jnp.bfloat16)


def block_output(scalars, active, down, middle, bias):
    rows, hidden = active.shape
    cells, width = len(middle), middle[0].shape[0]
    tile = hidden_tile(hidden)
    out = jax.ShapeDtypeStruct((cells, width, rows // cells), jnp.bfloat16)
    return grid_call(
        lambda me, *refs: block_out_kernel(*refs),
        (hidden // tile,),
        [
            pl.BlockSpec((rows, tile), lambda g, me: (0, g)),
            pl.BlockSpec((width, tile), lambda g, me: (0, g)),
            whole(bias),
        ]
        + [whole(m) for m in middle],
        whole(out),
        out,
        [pltpu.VMEM((width, rows), jnp.float32)],
        "block_output",
        2 * rows * down.size,
        (scalars, active, down, bias, *middle),
        1,
    )


def take_columns(piece, right, count, which):
    width = piece.shape[1]
    for s in range(count):

        @pl.when(which == s)
        def _():
            first = s * width // LANES * LANES
            last = min(-(-(s + 1) * width // LANES) * LANES, right.shape[1])
            block = right[:, first:last]
            piece[...] = block[:, s * width - first : (s + 1) * width - first]


def up_outer_kernel(seq_count, cells, share, cut, zbit, split, scalars, right, *refs):
    left, rest = refs[:cells], refs[cells:]
    got = rest[0] if split else None
    *results, total, piece, joined = rest[3 if split else 0 :]
    rows = left[0].shape[0]
    core = 0 if split else 1

    @pl.when(pl.program_id(0) == 0)
    def _():
        for c, part in enumerate(left):
            joined[:, c * part.shape[1] : (c + 1) * part.shape[1]] = part[...]

    take_columns(piece, right, seq_count, (2 * pl.program_id(0) + core) ^ scalars[0])
    for first, last in chunks(piece.shape[1]):
        total[:, first:last] = dot(joined[...], piece[:, first:last])
    cell_count = results[0].shape[1] * (2 if split else 1)
    height = results[0].shape[2] if not split else got.shape[2]
    for k in range(cell_count):
        c = k ^ scalars[1]
        start = jnp.minimum(lax.div(c * share, 8) * 8, rows - height)
        block = total[pl.ds(pl.multiple_of(start, 8), height), :]
        if split:
            block = block + got[0, k].astype(jnp.float32)
            for n, (bit, part) in enumerate(((1, block[:cut]), (zbit, block[cut:]))):
                target = results[2 * n + (0 if k & bit else 1)]
                target[0, without_bit(k, bit)] = part.astype(jnp.bfloat16)
        else:
            results[0][0, k] = block.astype(jnp.bfloat16)


def up_outer(scalars, left, right, seq_count, cell_count, got=None, lower=None):
    tokens, width = right.shape[0], right.shape[1] // seq_count
    rows = left[0].shape[0]
    _, height = row_cover(rows, cell_count)
    half = seq_count // 2
    split = got is not None
    cut = two_thirds(height)
    in_specs = [whole(right)] + [whole(part) for part in left]
    inputs = [scalars, right, *left]
    aliases = {}
    if split:
        in_specs.append(pl.BlockSpec((1,) + got.shape[1:], lambda g, me: (g, 0, 0, 0)))
        in_specs += [pl.BlockSpec(memory_space=pl.ANY)] * 2
        inputs += [got, *lower]
        aliases = {len(inputs) - 2: 2, len(inputs) - 1: 3}
        outs = [(half, cell_count // 2, cut, width)] * 2 + [lower[0].shape] * 2
        low = height - cut
        blocks = [pl.BlockSpec((1,) + outs[0][1:], lambda g, me: (g, 0, 0, 0))] * 2
        blocks += [
            pl.BlockSpec((1, cell_count // 2, low, width), lambda g, me: (g, 0, 1, 0))
        ] * 2
    else:
        outs = [(half, cell_count, height, width)]
        blocks = [pl.BlockSpec((1,) + outs[0][1:], lambda g, me: (g, 0, 0, 0))]
    return grid_call(
        partial(
            up_outer_kernel,
            seq_count,
            len(left),
            rows // cell_count,
            cut,
            cell_count // seq_count,
            split,
        ),
        (half,),
        in_specs,
        blocks,
        [jax.ShapeDtypeStruct(out, jnp.bfloat16) for out in outs],
        [
            pltpu.VMEM((rows, width), jnp.float32),
            pltpu.VMEM((tokens, width), jnp.bfloat16),
            pltpu.VMEM((rows, tokens), jnp.bfloat16),
        ],
        "up_outer",
        1,
        inputs,
        1,
        aliases,
    )


def two_thirds(height):
    return -(-height * 2 // 3 // 16) * 16


def down_outer_kernel(seq_count, inner, cut, split, scalars, left, right, *refs):
    got = refs[0] if split else None
    *results, total, piece, wide, own = refs[1 if split else 0 :]
    half = seq_count // 2
    share = own.shape[0] // half
    span = left.shape[2]
    width = piece.shape[1] // inner
    low = scalars[1] & (inner - 1)
    step = pl.program_id(0)
    core = 0 if split else 1
    starts, height = row_cover(share, inner)

    @pl.when(step == 0)
    def _():
        for c in range(left.shape[0]):
            wide[:, c * span : (c + 1) * span] = left[c].astype(jnp.float32)
        for x in range(half):
            for s in range(seq_count):

                @pl.when(((2 * x + core) ^ scalars[0]) == s)
                def _():
                    own[x * share : (x + 1) * share, :] = wide[s * share : (s + 1) * share, :]

    take_columns(piece, right, seq_count, step ^ lax.div(scalars[1], inner))
    for first, last in chunks(piece.shape[1]):
        total[:, first:last] = dot(own[...].astype(jnp.bfloat16), piece[:, first:last])
    for q in range(inner):
        for x in range(half):
            block = total[x * share : (x + 1) * share, q * width : (q + 1) * width]
            block = jnp.concatenate([block[s : s + height] for s in starts], axis=1)
            if split:
                block = block + got[x, q ^ low].astype(jnp.float32)
                away = 2 * x >= half
                target = results[0 if away else 1]
                target[x % (half // 2), q ^ low] = block[:cut].astype(jnp.bfloat16)
                rest = block[cut:].astype(jnp.bfloat16)

                @pl.when(step & 1 == 1)
                def _():
                    results[2][x, q ^ low] = rest

                @pl.when(step & 1 == 0)
                def _():
                    results[3][x, q ^ low] = rest

            else:
                results[0][x, q ^ low] = block.astype(jnp.bfloat16)


def down_outer(scalars, left, right, seq_count, cell_count, got=None):
    tokens, width = right.shape[0], right.shape[1] // seq_count
    half = seq_count // 2
    inner = cell_count // seq_count
    share = left.shape[1] // seq_count
    split = got is not None
    _, height = row_cover(share, inner)
    cut = two_thirds(height)
    in_specs = [whole(left), whole(right)]
    inputs = [scalars, left, right]
    if split:
        in_specs.append(pl.BlockSpec((half, inner) + got.shape[2:], lambda g, me: (0, g, 0, 0)))
        inputs.append(got)
        low = height - cut
        outs = [(half // 2, cell_count, cut, width)] * 2
        outs += [(half, cell_count // 2, 2 * low, width)] * 2
        blocks = [pl.BlockSpec((half // 2, inner, cut, width), lambda g, me: (0, g, 0, 0))] * 2
        blocks += [pl.BlockSpec((half, inner, low, width), lambda g, me: (0, g // 2, 0, 0))] * 2
    else:
        outs = [(half, cell_count, height, width)]
        blocks = [pl.BlockSpec((half, inner, height, width), lambda g, me: (0, g, 0, 0))]
    return grid_call(
        partial(down_outer_kernel, seq_count, inner, cut, split),
        (seq_count,),
        in_specs,
        blocks,
        [jax.ShapeDtypeStruct(out, jnp.bfloat16) for out in outs],
        [
            pltpu.VMEM((half * share, width), jnp.float32),
            pltpu.VMEM((tokens, width), jnp.bfloat16),
            pltpu.VMEM((left.shape[1], tokens), jnp.float32),
            pltpu.VMEM((half * share, tokens), jnp.float32),
        ],
        "down_outer",
        1,
        inputs,
        1,
    )


def out_outer_kernel(seq_count, cells, share, scalars, right, *refs):
    left, (result, total, joined) = refs[:cells], refs[cells:]
    for c, part in enumerate(left):
        joined[:, c * part.shape[1] : (c + 1) * part.shape[1]] = part[...]
    rows = total.shape[0]
    for first, last in chunks(total.shape[1]):
        total[:, first:last] = dot_turned(joined[...], right[first:last, :])
    width = total.shape[1] // seq_count
    _, cell_count, part, room = result.shape
    groups = room // width
    for k in range(cell_count):
        c = k ^ scalars[1]
        start = jnp.minimum(lax.div(c * share, 8) * 8, rows - groups * part)
        block = total[pl.ds(pl.multiple_of(start, 8), groups * part), :]
        for s in range(seq_count):
            piece = block[:, s * width : (s + 1) * width]
            pieces = [piece[i * part : (i + 1) * part] for i in range(groups)]
            pieces.append(jnp.zeros((part, room - groups * width), jnp.float32))
            place = s ^ scalars[0]
            place = (place & 1) * (seq_count // 2) + (place >> 1)
            result[place, k] = jnp.concatenate(pieces, axis=1).astype(jnp.bfloat16)


def out_outer(scalars, left, right, room, seq_count, cell_count):
    rows, tokens = right.shape
    groups = room * seq_count // rows
    _, height = row_cover(rows, cell_count, 16 * groups)
    shape = (seq_count, cell_count, height // groups, room)
    return no_grid_call(
        partial(out_outer_kernel, seq_count, len(left), rows // cell_count),
        jax.ShapeDtypeStruct(shape, jnp.bfloat16),
        "out_outer",
        1,
        [scalars, right, *left],
        [pltpu.VMEM((rows, rows), jnp.float32), pltpu.VMEM((rows, tokens), jnp.bfloat16)],
    )


def vector_kernel(cells, heads, head_size, seq_count, scalars, middle, hidden, *refs):
    first, sums, (result, own) = refs[:cells], refs[cells:-2], refs[-2:]
    own[...] = jnp.zeros_like(own)
    width = middle.shape[1]
    for s in range(seq_count):

        @pl.when(scalars[0] == s)
        def _():
            for (start, count, _), part in zip(head_groups(heads), sums):
                for n in range(count):
                    at = ((s * heads) + start + n) * head_size
                    if at >= width:
                        continue
                    for row, p in enumerate((0, 2)):
                        source = (p * count + n) * HEAD_PAD
                        own[row : row + 1, at : at + head_size] = part[
                            :, source : source + head_size
                        ]

    total = sum(part[0:2, :] for part in first)
    lines = [total[0:1], total[1:2], own[0:1, :], own[1:2, :]]
    lines += [middle[n : n + 1, :] for n in (2, 0, 1, 3)]
    count, rows, share = result.shape
    for c in range(count):
        place = c ^ scalars[1]
        for n, line in enumerate(lines):
            result[place, n : n + 1, :] = line[:, c * share : (c + 1) * share]
        for n in range(rows - 8):
            at = (c * (rows - 8) + n) * share
            result[place, 8 + n : 9 + n, :] = hidden[:, at : at + share]


def vector_blocks(
    scalars, first, sums, middle, hidden, heads, head_size, seq_count, cell_count
):
    share = middle.shape[1] // cell_count
    rows = 8 + hidden.shape[1] // middle.shape[1]
    return no_grid_call(
        partial(vector_kernel, len(first), heads, head_size, seq_count),
        jax.ShapeDtypeStruct((cell_count, rows, share), jnp.float32),
        "vector_blocks",
        1,
        [scalars, middle, hidden, *first, *sums],
        [pltpu.VMEM((8, middle.shape[1]), jnp.float32)],
    )


def mix_columns_kernel(heads, head_size, scalars, *refs):
    *blocks, result = refs
    places = {}
    for first, count, base in head_groups(heads):
        places.update({(p, first + n): base + p * count + n for p in range(3) for n in range(count)})
    seq_count = len(blocks)
    share = result.shape[1]
    width = HEADS * head_size
    for mine in range(seq_count):

        @pl.when(scalars[0] == mine)
        def _():
            for p in range(3):
                for head in range(HEADS):
                    first = p * width + head * head_size - mine * share
                    cut_left, cut_right = max(0, -first), min(head_size, share - first)
                    if cut_left >= cut_right:
                        continue
                    block = blocks[(head // heads) ^ mine]
                    source = places[p, head % heads] * HEAD_PAD
                    base = source // LANES * LANES
                    piece = block[:, base : min(base + LANES, block.shape[1])].astype(jnp.float32)
                    source -= base
                    result[:, first + cut_left : first + cut_right] = piece[
                        :, source + cut_left : source + cut_right
                    ]


def mix_columns(scalars, blocks, heads, head_size):
    rows = blocks[0].shape[0]
    return no_grid_call(
        partial(mix_columns_kernel, heads, head_size),
        jax.ShapeDtypeStruct((rows, 3 * HEADS * head_size // len(blocks)), jnp.float32),
        "mix_columns",
        1,
        [scalars, *blocks],
        [],
    )


def tokens_back_kernel(tokens, gain, back_middle, *refs):
    *terms, result = refs
    cells, _, span = tokens.shape
    (gain,) = columns_of(gain)
    for c in range(cells):
        normal, rise = centred_columns(tokens[c].astype(jnp.float32))
        back = terms[2 * c][...].astype(jnp.float32) + terms[2 * c + 1][...].astype(jnp.float32)
        back_in = back_middle[:, c * span : (c + 1) * span]
        back_in = back_in + norm_pull(normal, rise, back, gain)
        result[c] = back_in.astype(jnp.bfloat16)


def tokens_back(tokens, gain, back_middle, terms):
    return no_grid_call(
        tokens_back_kernel,
        jax.ShapeDtypeStruct(tokens.shape, jnp.bfloat16),
        "tokens_back",
        1,
        [tokens, gain, back_middle, *terms],
        [],
        scalars=0,
    )


def order_after(values, *earlier):
    values, _ = lax.optimization_barrier((values, earlier))
    return values


def advance(parts, last):
    groups = {}
    running = [part for part in parts if part.order]
    arrived = [part.got for part in running]
    for part in running:
        part.got = order_after(part.got, arrived)
        key = (part.kind, tuple(part.names), tuple(part.order), part.keep.shape[2])
        groups.setdefault(key, []).append(part)
    for first, *others in groups.values():
        last = first.step(last, *others)
    return last


def on_device(
    tokens,
    first_gain,
    first_shift,
    mix_weight,
    query_bias,
    value_bias,
    out_weight,
    out_bias,
    second_gain,
    second_shift,
    up_weight,
    up_bias,
    down_weight,
    down_bias,
    cotangent,
    prefix_lengths,
    gene_counts,
    key_mask,
):
    cells_here, span, width = tokens.shape
    head_size = width // HEADS
    length = span * lax.axis_size("seq")
    start = lax.axis_index("seq") * span
    seq_count, cell_count = lax.axis_size("seq"), lax.axis_size("cells")
    me = jnp.stack([lax.axis_index("seq"), lax.axis_index("cells")]).astype(jnp.int32)
    totals = prefix_lengths + gene_counts
    row_count = cells_here * span
    own_rows = start + jnp.arange(span)
    heads_here = -(-HEADS // seq_count)
    head_total = heads_here * seq_count
    features = -(-(width + 1) // LANES) * LANES
    scalars = jnp.concatenate([me, prefix_lengths, totals])

    def flat(array):
        return array.reshape(row_count, array.shape[-1])

    groups = head_groups(heads_here)
    tokens_turned = tokens.transpose(0, 2, 1)
    cotangent_turned = cotangent.transpose(0, 2, 1)
    down_turned = down_weight.T
    wide = []
    for c in range(cells_here):
        wide.append(widen(order_after(scalars, wide), c, tokens_turned, key_mask, features))
    weight, bias, *weights_turned = own_weights(
        order_after(scalars, wide),
        mix_weight,
        query_bias,
        value_bias,
        features,
        seq_count,
        heads_here,
        head_size,
    )
    x_bits = [b for b in reversed(bits_of(seq_count)) if b > 1]
    near = [swap_with(block, "seq", 1) for block in wide]
    back_active = active_back(scalars, order_after(flat(cotangent), weight), down_turned)
    held = [{0: wide[c]} for c in range(cells_here)]
    for c in range(cells_here):
        for bit in x_bits:
            for r, block in list(held[c].items()):
                after = (held[c - 1][x_bits[0]], back_active) if c > 0 else ()
                held[c][r | bit] = swap_with(order_after(block, *after), "seq", bit)

    attended, kept = [], []
    last = (back_active,)
    blocks, normed = [], []
    for c in range(cells_here):
        after = last
        for r, block in list(held[c].items()):
            held[c][r | 1] = near[c] if r == 0 else swap_with(order_after(block, *after), "seq", 1)
        blocks.append([held[c][r] for r in range(seq_count)])
        results = attend_forward(
            scalars,
            c,
            order_after(blocks[c], *last),
            weight,
            bias,
            first_gain,
            first_shift,
            heads_here,
            head_size,
        )
        qkv, (out, normed_cell, *parts) = results[: len(groups)], results[len(groups) :]
        last = (out,)
        kept.append((qkv, out))
        normed.append(normed_cell)
        attended.append(exchanged_blocks(parts))
    middle, second, second_turned, attended_turned = [], [], [], []
    for c in range(cells_here):
        results = second_norm(
            scalars,
            out_weight,
            tokens_turned[c],
            (second_gain, second_shift, out_bias),
            order_after(attended[c], *last),
        )
        last = (results[0],)
        for held, result in zip((middle, second, second_turned, attended_turned), results):
            held.append(result)
    active, back_upper, up_bias_back = hidden_layer(
        scalars, second, back_active, up_weight, up_bias.reshape(1, -1)
    )
    (down_send,) = down_outer(scalars, cotangent_turned, active, seq_count, cell_count)
    down_got = swap_with(down_send, "seq", 1)
    (up_send,) = up_outer(
        scalars, second_turned, order_after(back_upper, down_send), seq_count, cell_count
    )
    up_got = swap_with(up_send, "seq", 1)
    *down_halves, lower_send, lower_keep = down_outer(
        scalars, cotangent_turned, order_after(active, up_send), seq_count, cell_count, down_got
    )
    *up_halves, lower_send, lower_keep = up_outer(
        scalars,
        second_turned,
        order_after(back_upper, down_halves),
        seq_count,
        cell_count,
        up_got,
        (lower_send, lower_keep),
    )

    def flat_blocks(array):
        return array.reshape((-1,) + array.shape[-2:])

    x_bits = [("seq", b) for b in reversed(bits_of(seq_count)) if b > 1]
    cell_bits = [("cells", b) for b in reversed(bits_of(cell_count))]
    names = x_bits + cell_bits
    y_bit, z_bit = ("cells", 1), ("cells", cell_count // seq_count)
    rest = [n for n in reversed(cell_bits) if n not in (y_bit, z_bit)]
    running = [
        Reduction("down", names, x_bits + [y_bit, z_bit] + rest, *map(flat_blocks, down_halves)),
        Reduction("up", names, [y_bit, z_bit] + x_bits + rest, *map(flat_blocks, up_halves)),
        Reduction(
            "both",
            names,
            [z_bit] + x_bits + [y_bit] + rest,
            flat_blocks(lower_send),
            flat_blocks(lower_keep),
        ),
    ]
    back_middle, back_branch, middle_sums, *back_heads = middle_back(
        scalars,
        order_after(back_upper, up_halves),
        up_weight,
        middle,
        second_gain,
        cotangent_turned,
        out_weight,
        seq_count,
        heads_here,
    )
    back_upper_half = route_upper(back_heads[-1])
    down_part, up_part, both_part = running
    out_shares = out_outer(
        scalars,
        attended_turned,
        order_after(back_branch, back_heads),
        3 * groups[0][1] * HEAD_PAD,
        seq_count,
        cell_count,
    )
    out_part = Reduction(
        "out",
        [("seq", 1)] + names,
        [("seq", 1)] + x_bits + [y_bit, z_bit] + rest,
        flat_blocks(out_shares[seq_count // 2 :]),
        flat_blocks(out_shares[: seq_count // 2]),
    )
    block_out = block_output(
        scalars, order_after(active, out_shares), down_turned, middle, down_bias
    )
    last = down_part.step(block_out)
    back_arrays, back_places = route_rest(
        back_heads[:-1], order_after(back_upper_half, last)
    )
    last = advance([up_part, both_part], last)
    mixed_back, mix_parts = [[], []], []
    back_normed, bias_backs, first_sums = [], [], []

    def mix_reductions(group, last):
        *halves, sums = mix_outer(
            scalars,
            normed,
            order_after(mixed_back[group], last),
            width,
            cell_count,
        )
        bias_backs.append(sums)
        label = ["first", "second"][group]
        return [
            Reduction(label + " upper", cell_bits, [y_bit, z_bit] + rest, *halves[:2]),
            Reduction(label + " lower", cell_bits, [z_bit, y_bit] + rest, *halves[2:]),
        ], halves[0]

    def attend_group(c, group, last):
        qkv, out = kept[c]
        back = attend_backward(
            scalars,
            c,
            qkv[group],
            out,
            order_after(back_arrays, last),
            back_places,
            groups[group][0],
            head_size,
        )
        mixed_back[group].append(back)
        return back

    def normed_reduction(c, last):
        *parts, sums = normed_back(
            weights_turned, [order_after(mixed_back[g][c], last) for g in range(2)], blocks[c]
        )
        first_sums.append(sums)
        back_normed.append(PositionSum(parts))
        return sums

    for c in range(cells_here):
        final = c == cells_here - 1
        last = attend_group(c, 0, last)
        if final:
            for earlier in range(c):
                last = normed_reduction(earlier, last)
            last = advance(running, last)
            last = out_part.step(last)
            parts, last = mix_reductions(0, last)
            mix_parts.append(parts)
            for part in back_normed:
                last = part.step(last)
        last = attend_group(c, 1, last)
        if c == 0:
            last = advance(running, last)
    while len(out_part.order) >= len(cell_bits):
        last = out_part.step(last)
    parts, last = mix_reductions(1, last)
    mix_parts.append(parts + [out_part])
    last = advance(mix_parts[0], last)
    last = normed_reduction(cells_here - 1, last)
    done = [part.got for part in running if part.labels and not part.order]
    vectors = VectorSum(
        vector_blocks(
            scalars,
            order_after(first_sums, last),
            bias_backs,
            middle_sums,
            up_bias_back,
            heads_here,
            head_size,
            seq_count,
            cell_count,
        ),
        seq_count,
    )
    last = advance(mix_parts[1], (last, [part.got for part in back_normed[:-1]]))
    last = vectors.step(last)
    last = advance(mix_parts[0], last)
    last = back_normed[-1].step((last, done))
    last = vectors.step(last)
    last = advance(mix_parts[1], last)
    last = vectors.step(last)
    while any(part.bits for part in back_normed):
        for part in back_normed:
            last = part.step(last) if part.bits else last
    running += mix_parts[0] + mix_parts[1]
    running = [part for part in running if part.labels]
    while any(part.order for part in running):
        last = advance(running, last)
    while vectors.order:
        last = vectors.step(last)
    terms = [x for part in back_normed for x in part.terms()]
    tokens_gradient = tokens_back(
        tokens_turned, first_gain, back_middle, order_after(terms, last)
    )
    last = tokens_gradient
    joined = vectors.step(last)[0]
    vectors = [*(joined[n] for n in range(7)), joined[8:].reshape(-1), joined[7]]
    blocks = {}
    for part in running:
        blocks.update(part.finish(last))
    low = blocks["both"].shape[0] // 2

    def ungrouped(block, starts, share):
        pieces = jnp.split(block, len(starts), axis=1)
        cuts = [share * n - start for n, start in enumerate(starts)]
        return jnp.concatenate([p[c : c + share] for p, c in zip(pieces, cuts)])

    down_part = jnp.concatenate([blocks["down"], blocks["both"][:low]])
    down_share = width // seq_count
    down_starts, _ = row_cover(down_share, cell_count // seq_count)
    down_part = ungrouped(down_part, down_starts, down_share // len(down_starts))
    up_part = jnp.concatenate([blocks["up"], blocks["both"][low:]])
    mix_part = jnp.concatenate(
        [
            jnp.concatenate([blocks[g + " upper"], blocks[g + " lower"]])
            for g in ("first", "second")
        ],
        axis=1,
    )
    mix_part = mix_columns(
        scalars,
        gathered_blocks(mix_part.astype(jnp.bfloat16), seq_count),
        heads_here,
        head_size,
    )
    group = blocks["out"].shape[0]
    out_groups = blocks["out"].shape[1] * seq_count // width
    out_part = blocks["out"][:, : out_groups * (width // seq_count)]
    out_part = ungrouped(out_part, [group * n for n in range(out_groups)], group)

    def own_rows_of(part, unit=16):
        starts, _ = row_cover(width, cell_count, unit)
        share = width // cell_count
        shift = jnp.array([share * c - starts[c] for c in range(cell_count)])[me[1]]
        return lax.dynamic_slice_in_dim(part, shift, share, axis=0)

    matrices = (
        own_rows_of(mix_part),
        own_rows_of(out_part, 16 * out_groups),
        own_rows_of(up_part),
        down_part.T,
    )
    return (
        block_out.transpose(0, 2, 1),
        tokens_gradient.transpose(0, 2, 1),
        vectors[0],
        vectors[1],
        matrices[0],
        vectors[2],
        vectors[3],
        matrices[1],
        vectors[4],
        vectors[5],
        vectors[6],
        matrices[2],
        vectors[7],
        matrices[3],
        vectors[8],
    )


def solution(mesh):
    return jax.shard_map(
        on_device,
        mesh=mesh,
        in_specs=(
            P("cells", "seq", None),
            P(),
            P(),
            P(),
            P(),
            P(),
            P(),
            P(),
            P(),
            P(),
            P(),
            P(),
            P(),
            P(),
            P("cells", "seq", None),
            P("cells"),
            P("cells"),
            P("cells", "seq"),
        ),
        out_specs=(
            P("cells", "seq", None),
            P("cells", "seq", None),
            P("cells"),
            P("cells"),
            P("cells", "seq"),
            P("cells"),
            P("cells"),
            P("cells", "seq"),
            P("cells"),
            P("cells"),
            P("cells"),
            P("cells", "seq"),
            P("cells"),
            P("cells", "seq"),
            P("cells"),
        ),
        check_vma=False,
    )
```

```python
from functools import partial
import math

import jax
import jax.numpy as jnp
from jax import lax
from jax.experimental import pallas as pl
from jax.experimental.pallas import tpu as pltpu
from jax.sharding import PartitionSpec as P

HEADS = 20
LANES = 128
TILE = 256
HEAD_PAD = 64
MASKED = -1e30
ONE_ROW = 56
SPLIT_ROW = 57
VMEM_LIMIT = 20 * 1024 * 1024
SHORT = pl.CostEstimate(flops=1, bytes_accessed=1, transcendentals=0)


COSTS = {'widen': 3, 'attend_forward': 14, 'own_weights': 4}


def cost(name):
    return pl.CostEstimate(flops=COSTS.get(name, 0) * 10**9 + 1, bytes_accessed=1, transcendentals=0)


def bits_of(count):
    return [1 << b for b in range(count.bit_length() - 1)]


def swap_with(array, axis, bit):
    count = lax.axis_size(axis)
    return lax.ppermute(array, axis, [(i, i ^ bit) for i in range(count)])


def without_bit(index, bit):
    return (index // (2 * bit)) * bit + index % bit


def add_halves_kernel(count, *refs):
    for n in range(count):
        mine_away, got_away, mine_here, got_here = refs[4 * n : 4 * n + 4]
        first = sum(refs[4 * p].shape[1] for p in range(n))
        rows = slice(first, first + mine_away.shape[1])
        for mine, got, result in (
            (mine_away, got_away, refs[4 * count]),
            (mine_here, got_here, refs[4 * count + 1]),
        ):
            total = mine[...].astype(jnp.float32) + got[...].astype(jnp.float32)
            result[:, rows, :] = total.astype(jnp.bfloat16)


def add_halves(pairs, bit):
    count, _, width = pairs[0][0].shape
    rows = sum(mine.shape[1] for mine, _ in pairs)
    shape = jax.ShapeDtypeStruct((count // 2, rows, width), jnp.bfloat16)
    in_specs, inputs = [], []
    for mine, got in pairs:
        for value in (bit, 0):
            spec = pl.BlockSpec(
                (1,) + mine.shape[1:],
                lambda g, value=value: ((g // bit) * (2 * bit) + value + g % bit, 0, 0),
            )
            in_specs += [spec, spec]
            inputs += [mine, got]
    out = pl.BlockSpec((1, rows, width), lambda g: (g, 0, 0))
    return pl.pallas_call(
        partial(add_halves_kernel, len(pairs)),
        out_shape=(shape, shape),
        grid=(count // 2,),
        in_specs=in_specs,
        out_specs=(out, out),
        compiler_params=pltpu.CompilerParams(vmem_limit_bytes=VMEM_LIMIT),
        cost_estimate=SHORT,
        name="add_halves",
    )(*inputs)


class Reduction:
    def __init__(self, label, names, order, send, keep, kind=None):
        self.labels = [label]
        self.kind = kind
        self.names, self.order = list(names), list(order)
        self.keep = keep
        self.heights = [keep.shape[1]]
        self.leave(send)

    def leave(self, send):
        axis, bit = self.order.pop(0)
        self.names.remove((axis, bit))
        self.got = swap_with(send, axis, bit)

    def step(self, last, *others):
        place = self.names.index(self.order[0])
        bit = 1 << (len(self.names) - 1 - place)
        pairs = [order_after((p.keep, p.got), last) for p in (self,) + others]
        for other in others:
            assert (other.names, other.order) == (self.names, self.order)
            self.heights += other.heights
            self.labels += other.labels
            other.labels, other.order = [], []
        send, self.keep = add_halves(pairs, bit)
        self.leave(send)
        return self.keep

    def finish(self, last):
        while self.order:
            last = self.step(last)
        total = order_after(self.keep, last).astype(jnp.float32) + self.got.astype(jnp.float32)
        ends = [sum(self.heights[:n]) for n in range(len(self.heights) + 1)]
        return {label: total[0, a:b] for label, a, b in zip(self.labels, ends, ends[1:])}


def row_cover(rows, count, unit=16):
    share = rows // count
    starts = [share * c // 8 * 8 for c in range(count)]
    height = max(share * (c + 1) - starts[c] for c in range(count))
    height = -(-height // unit) * unit
    return [min(s, rows - height) for s in starts], height


def head_groups(heads):
    first = -(-heads * 3 // 5)
    return [(0, first, 0), (first, heads - first, 3 * first)]


def no_grid_call(body, out_shape, name, flops, inputs, scratch, scalars=1):
    in_specs = [pl.BlockSpec(memory_space=pltpu.SMEM)] * scalars
    in_specs += [pl.BlockSpec(memory_space=pltpu.VMEM)] * (len(inputs) - scalars)
    moved = sum(x.size * x.dtype.itemsize for x in inputs)
    moved += sum(math.prod(x.shape) * x.dtype.itemsize for x in jax.tree.leaves(out_shape))
    return pl.pallas_call(
        body,
        out_shape=out_shape,
        in_specs=in_specs,
        out_specs=jax.tree.map(lambda _: pl.BlockSpec(memory_space=pltpu.VMEM), out_shape),
        scratch_shapes=scratch,
        compiler_params=pltpu.CompilerParams(vmem_limit_bytes=VMEM_LIMIT),
        cost_estimate=cost(name),
        name=name,
    )(*inputs)


def make_diagonal(diag_ref, keys, tile, prefix):
    first = tile * TILE
    shape = (TILE, TILE)
    key_at = lax.broadcasted_iota(jnp.int32, shape, 0)
    row_at = lax.broadcasted_iota(jnp.int32, shape, 1)
    opened = keys[first : first + TILE, ONE_ROW : ONE_ROW + 1].astype(jnp.float32) > -1.0
    near = (key_at <= row_at) | (key_at + first < prefix)
    seen = (near & opened) | (key_at == row_at)
    diag_ref[tile] = jnp.where(seen, 0.0, MASKED)


def without_mask(keys):
    lane = lax.broadcasted_iota(jnp.int32, keys.shape, 1)
    return jnp.where(lane == ONE_ROW, 0.0, keys.astype(jnp.float32)).astype(jnp.bfloat16)


def turned_rows(columns):
    return columns.astype(jnp.float32).T.astype(jnp.bfloat16)


def split_rows(columns, value):
    row = lax.broadcasted_iota(jnp.int32, columns.shape, 0)
    result = columns.astype(jnp.float32)
    for place in range(3):
        part = value.astype(jnp.bfloat16).astype(jnp.float32)
        value = value - part
        result = jnp.where(row == SPLIT_ROW + place, part, result)
    return result.astype(jnp.bfloat16)


def forward_kernel(seq_count, cell, span, heads, head_size, rate, scalars, *refs):
    blocks, (weight, bias, gain, shift) = refs[:seq_count], refs[seq_count : seq_count + 4]
    groups = head_groups(heads)
    *qkv_groups, out, normed = refs[seq_count + 4 : seq_count + 6 + len(groups)]
    *parts, rows, diag, scores = refs[seq_count + 6 + len(groups) :]
    width = gain.shape[0]
    gain, shift = columns_of(gain, shift)
    me, prefix = scalars[0], scalars[2 + cell]
    length = span * seq_count
    tiles = length // TILE
    for r in range(seq_count):
        here = slice(r * span, (r + 1) * span)
        normal, _ = centred_columns(blocks[r][:width, :].astype(jnp.float32))
        normed[:width, here] = (normal * gain + shift).astype(jnp.bfloat16)
        normed[width:, here] = blocks[r][width:, :]
        mixed = jnp.dot(weight[...], normed[:, here], preferred_element_type=jnp.float32)
        mixed = (mixed + bias[...]).astype(jnp.bfloat16)
        place = pl.ds(pl.multiple_of((me ^ r) * span, LANES), span)
        mixed = mixed.reshape(3 * heads, HEAD_PAD, span)
        for (_, count, base), qkv in zip(groups, qkv_groups):
            qkv[:, :, place] = mixed[base : base + 3 * count]

    def turn(first, count, qkv, h, carry):
        rows[first + h] = turned_rows(qkv[count + h])
        return carry

    for (first, count, _), qkv in zip(groups, qkv_groups):
        lax.fori_loop(0, count, partial(turn, first, count, qkv), 0)
    for tile in range(tiles):
        make_diagonal(diag, rows.at[0], tile, prefix)

    def one_head(start, count, qkv, h, carry):
        for tile in range(tiles):
            across = slice(tile * TILE, (tile + 1) * TILE)
            query = qkv[h, :, across]
            tops = None
            for j in range(tile + 1):
                down = slice(j * TILE, (j + 1) * TILE)
                keys = rows[start + h, down, :]
                if j == tile:
                    keys = without_mask(keys)
                block = jnp.dot(keys, query, preferred_element_type=jnp.float32)
                if j == tile:
                    block = block + diag[tile]
                scores[down, :] = block
                top = jnp.max(block.reshape(TILE // 8, 8, TILE), axis=0)
                tops = top if tops is None else jnp.maximum(tops, top)
            top = jnp.max(tops, axis=0, keepdims=True)
            total = jnp.zeros((HEAD_PAD, TILE), jnp.float32)
            for j in range(tile + 1):
                down = slice(j * TILE, (j + 1) * TILE)
                probs = jnp.exp2((scores[down, :] - top) * rate).astype(jnp.bfloat16)
                total += jnp.dot(
                    qkv[2 * count + h, :, down], probs, preferred_element_type=jnp.float32
                )
            summed = total[ONE_ROW : ONE_ROW + 1]
            row = lax.broadcasted_iota(jnp.int32, total.shape, 0)
            log_sum = top * rate + jnp.log2(summed)
            out[start + h, :, across] = jnp.where(row == ONE_ROW, log_sum, total / summed)
        return carry

    for (first, count, _), qkv in zip(groups, qkv_groups):
        lax.fori_loop(0, count, partial(one_head, first, count, qkv), 0)
    for r in range(seq_count):
        place = pl.ds(pl.multiple_of((me ^ r) * span, LANES), span)
        piece = out[:, :head_size, place].reshape(heads * head_size, span)
        parts[r][...] = piece.astype(jnp.bfloat16)


def backward_kernel(seq_count, places, cell, span, first_head, heads, head_size, rate, scalars, *refs):
    qkv, out, *arrays, result = refs[:-6]
    back, query_rows, key_rows, value_rows, gathered, diag = refs[-6:]
    me, prefix = scalars[0], scalars[2 + cell]
    length = span * seq_count
    tiles = length // TILE
    scale = 1.0 / math.sqrt(head_size)
    for r in range(seq_count):
        place = pl.ds(pl.multiple_of((me ^ r) * span, LANES), span)
        gathered[:, :, place] = arrays[places[r][0]][
            places[r][1], cell, first_head : first_head + heads
        ]
    key_rows[...] = turned_rows(qkv[heads])
    for tile in range(tiles):
        make_diagonal(diag, key_rows, tile, prefix)

    def one_head(h, carry):
        key_rows[...] = turned_rows(qkv[heads + h])
        value_rows[...] = turned_rows(qkv[2 * heads + h])
        held = gathered[h]
        centre = jnp.sum(
            held[:head_size].astype(jnp.float32) * out[first_head + h, :head_size],
            axis=0,
            keepdims=True,
        )
        gathered[h] = split_rows(held, -centre)
        log_sum = out[first_head + h, ONE_ROW : ONE_ROW + 1, :]
        qkv_q = split_rows(qkv[h], -log_sum / rate)
        query_rows[...] = jnp.zeros_like(query_rows)
        for j in range(tiles):
            down = slice(j * TILE, (j + 1) * TILE)
            keys, values = key_rows[down, :], value_rows[down, :]
            keys_column = qkv[heads + h, :, down]
            keys_back = jnp.zeros((TILE, HEAD_PAD), jnp.float32)
            values_back = jnp.zeros((TILE, HEAD_PAD), jnp.float32)
            for i in range(j, tiles):
                across = slice(i * TILE, (i + 1) * TILE)
                query = qkv_q[:, across]
                back_out = gathered[h, :, across]
                if i == j:
                    block = jnp.dot(without_mask(keys), query, preferred_element_type=jnp.float32)
                    block = block + diag[i]
                else:
                    block = jnp.dot(keys, query, preferred_element_type=jnp.float32)
                probs = jnp.exp2(block * rate)
                back_probs = jnp.dot(values, back_out, preferred_element_type=jnp.float32)
                back_scores = (probs * back_probs).astype(jnp.bfloat16)
                probs = probs.astype(jnp.bfloat16)
                turned = (((1,), (1,)), ((), ()))
                values_back += lax.dot_general(
                    probs, back_out, turned, preferred_element_type=jnp.float32
                )
                keys_back += lax.dot_general(
                    back_scores, query, turned, preferred_element_type=jnp.float32
                )
                query_rows[:, across] += jnp.dot(
                    keys_column, back_scores, preferred_element_type=jnp.float32
                )
            back[heads + h, down, :] = (keys_back * scale).astype(jnp.bfloat16)
            back[2 * heads + h, down, :] = values_back.astype(jnp.bfloat16)
        back[h] = (query_rows[...] * scale).T.astype(jnp.bfloat16)
        return carry

    lax.fori_loop(0, heads, one_head, 0)
    for block in range(seq_count):
        here = slice(block * span, (block + 1) * span)
        there = pl.ds(pl.multiple_of((me ^ block) * span, LANES), span)
        for first in range(0, 3 * heads, 2):
            pieces = [back[p, here, :] for p in range(first, min(first + 2, 3 * heads))]
            joined = pieces[0] if len(pieces) == 1 else jnp.concatenate(pieces, axis=1)
            left = first * HEAD_PAD
            result[there, left : left + joined.shape[1]] = joined

def attend_forward(scalars, cell, blocks, weight, bias, gain, shift, heads, head_size):
    seq_count, span = len(blocks), blocks[0].shape[1]
    length = seq_count * span
    rate = math.log2(math.e) / math.sqrt(head_size)
    flops = 2 * weight.size * length + 4 * heads * HEAD_PAD * length * length
    return no_grid_call(
        partial(forward_kernel, seq_count, cell, span, heads, head_size, rate),
        tuple(
            jax.ShapeDtypeStruct((3 * count, HEAD_PAD, length), jnp.bfloat16)
            for _, count, _ in head_groups(heads)
        )
        + (
            jax.ShapeDtypeStruct((heads, HEAD_PAD, length), jnp.float32),
            jax.ShapeDtypeStruct((blocks[0].shape[0], length), jnp.bfloat16),
        )
        + (jax.ShapeDtypeStruct((heads * head_size, span), jnp.bfloat16),) * seq_count,
        "attend_forward",
        flops,
        [scalars, *blocks, weight, bias, gain, shift],
        [
            pltpu.VMEM((heads, length, HEAD_PAD), jnp.bfloat16),
            pltpu.VMEM((length // TILE, TILE, TILE), jnp.float32),
            pltpu.VMEM((length, TILE), jnp.float32),
        ],
    )


def attend_backward(scalars, cell, qkv, out, arrays, places, first_head, head_size):
    seq_count, span = len(places), arrays[0].shape[-1]
    heads = qkv.shape[0] // 3
    length = seq_count * span
    rate = math.log2(math.e) / math.sqrt(head_size)
    return no_grid_call(
        partial(
            backward_kernel, seq_count, places, cell, span, first_head, heads, head_size, rate
        ),
        jax.ShapeDtypeStruct((length, 3 * heads * HEAD_PAD), jnp.bfloat16),
        "attend_backward",
        1,
        [scalars, qkv, out, *arrays],
        [
            pltpu.VMEM((3 * heads, length, HEAD_PAD), jnp.bfloat16),
            pltpu.VMEM((HEAD_PAD, length), jnp.float32),
            pltpu.VMEM((length, HEAD_PAD), jnp.bfloat16),
            pltpu.VMEM((length, HEAD_PAD), jnp.bfloat16),
            pltpu.VMEM((heads, HEAD_PAD, length), jnp.bfloat16),
            pltpu.VMEM((length // TILE, TILE, TILE), jnp.float32),
        ],
    )


def normed_back_kernel(seq_count, count, *refs):
    weights, backs = refs[:count], refs[count : 2 * count]
    tokens, results = refs[2 * count : 2 * count + seq_count], refs[2 * count + seq_count : -1]
    sums = refs[-1]
    width, span = results[0].shape
    totals = [0.0] * 2
    for r in range(seq_count):
        rows = slice(r * span, (r + 1) * span)
        back = sum(dot_turned(w[...], part[rows, :]) for w, part in zip(weights, backs))
        results[r][...] = back.astype(jnp.bfloat16)
        normal, _ = centred_columns(tokens[r][:width, :].astype(jnp.float32))
        for n, term in enumerate((back * normal, back)):
            totals[n] = totals[n] + jnp.sum(term, axis=1, keepdims=True)
    sums[...] = lines_of(totals)


def normed_back(weights, backs, tokens):
    seq_count = len(tokens)
    span = backs[0].shape[0] // seq_count
    width = weights[0].shape[0]
    shape = jax.ShapeDtypeStruct((width, span), jnp.bfloat16)
    return no_grid_call(
        partial(normed_back_kernel, seq_count, len(backs)),
        (shape,) * seq_count + (jax.ShapeDtypeStruct((8, width), jnp.float32),),
        "normed_back",
        1,
        [*weights, *backs, *tokens],
        [],
        scalars=0,
    )


def mix_outer_kernel(cell_count, share, cuts, count, scalars, *refs):
    normed, backs, (*results, sums, whole_sum) = refs[:count], refs[count : 2 * count], refs[2 * count :]
    features, width = whole_sum.shape
    sums[...] = sum(
        jnp.sum(back[...].astype(jnp.float32), axis=0, keepdims=True) for back in backs
    )
    for first, last in chunks(width):
        whole_sum[:, first:last] = sum(
            dot(left[:features, :], back[:, first:last]) for left, back in zip(normed, backs)
        )
    for k in range(cell_count):
        c = k ^ scalars[1]
        start = jnp.minimum(lax.div(c * share, 8) * 8, features - cuts[-1])
        block = whole_sum[pl.ds(pl.multiple_of(start, 8), cuts[-1]), :].astype(jnp.bfloat16)
        for n, bit in enumerate((1, 2)):
            target = results[2 * n + (0 if k & bit else 1)]
            target[without_bit(k, bit)] = block[cuts[n] : cuts[n + 1]]


def mix_outer(scalars, normed, backs, features, cell_count):
    _, height = row_cover(features, cell_count)
    cuts = (0, -(-height // 2 // 16) * 16, height)
    width = backs[0].shape[1]
    halves = [(cell_count // 2, cuts[n + 1] - cuts[n], width) for n in (0, 0, 1, 1)]
    return no_grid_call(
        partial(mix_outer_kernel, cell_count, features // cell_count, cuts, len(backs)),
        tuple(jax.ShapeDtypeStruct(shape, jnp.bfloat16) for shape in halves)
        + (jax.ShapeDtypeStruct((1, width), jnp.float32),),
        "mix_outer",
        1,
        [scalars, *normed, *backs],
        [pltpu.VMEM((features, width), jnp.float32)],
    )


def gathered_blocks(block, seq_count):
    held = {0: block}
    for bit in list(reversed(bits_of(seq_count))):
        held.update({r | bit: swap_with(x, "seq", bit) for r, x in list(held.items())})
    return [held[r] for r in range(seq_count)]


class PositionSum:
    def __init__(self, blocks):
        self.held = dict(enumerate(blocks))
        self.bits = bits_of(len(blocks))
        self.leave()

    def leave(self):
        bit = self.bits.pop(0)
        self.got = {r: swap_with(self.held[r | bit], "seq", bit) for r in self.held if not r & bit}

    def step(self, last):
        held, got = order_after((self.held, self.got), last)
        self.held = {r: add_low(held[r], x) for r, x in got.items()}
        self.leave()
        return self.held[0]

    def terms(self):
        return [self.held[0], self.got[0]]


class VectorSum:
    def __init__(self, blocks, seq_count):
        cells = [("cells", bit) for bit in reversed(bits_of(blocks.shape[0]))]
        self.order = cells + [("seq", bit) for bit in bits_of(seq_count)]
        self.leave(blocks)

    def leave(self, blocks):
        axis, bit = self.order.pop(0)
        half = blocks.shape[0] // 2 if axis == "cells" else 0
        self.keep = blocks[:half] if half else blocks
        self.got = swap_with(blocks[half:], axis, bit)

    def step(self, last):
        keep, got = order_after((self.keep, self.got), last)
        self.keep = keep + got
        if self.order:
            self.leave(self.keep)
        return self.keep


def add_low(left, right):
    return (left.astype(jnp.float32) + right.astype(jnp.float32)).astype(jnp.bfloat16)


def route_upper(upper):
    return swap_with(upper, "seq", upper.shape[0])


def route_rest(lower, got):
    seq_count = 2 * len(lower)
    arrays = [x[None] for x in lower] + [got]
    held = {r: (r, 0) for r in range(len(lower))}
    held.update({len(lower) + r: (len(lower), r) for r in range(len(lower))})
    for bit in list(reversed(bits_of(seq_count)))[1:]:
        away = [r for r in held if r & bit]
        arrays.append(swap_with(jnp.stack([arrays[held[r][0]][held[r][1]] for r in away]), "seq", bit))
        held.update({r: (len(arrays) - 1, n) for n, r in enumerate(away)})
    return arrays, [held[r] for r in range(seq_count)]


def exchanged_blocks(blocks):
    return [blocks[0]] + [swap_with(blocks[r], "seq", r) for r in range(1, len(blocks))]


def chunks(width):
    return [(first, min(first + TILE, width)) for first in range(0, width, TILE)]


def dot(left, right):
    return jnp.dot(left, right, preferred_element_type=jnp.float32)


def dot_turned(left, right):
    return lax.dot_general(
        left, right, (((1,), (1,)), ((), ())), preferred_element_type=jnp.float32
    )


def centred_columns(values):
    centred = values - jnp.mean(values, axis=0, keepdims=True)
    spread = jnp.mean(centred * centred, axis=0, keepdims=True)
    rise = lax.rsqrt(spread + 1e-05)
    return centred * rise, rise


def norm_pull(normal, rise, back, gain):
    scaled = back * gain
    inner = scaled - jnp.mean(scaled, axis=0, keepdims=True)
    inner = inner - normal * jnp.mean(scaled * normal, axis=0, keepdims=True)
    return rise * inner


def columns_of(*vectors):
    rows = [vector[...].reshape(1, -1) for vector in vectors]
    rows += [jnp.zeros_like(rows[0])] * (8 - len(rows))
    turned = jnp.concatenate(rows, axis=0).T
    return [turned[:, n : n + 1] for n in range(len(vectors))]


def lines_of(columns):
    rows = columns[0].shape[0]
    room = [jnp.zeros((rows, 8 - len(columns)), jnp.float32)] if len(columns) < 8 else []
    return jnp.concatenate(list(columns) + room, axis=1).T


def widen_kernel(cell, cells, scalars, tokens, key_mask, result):
    width, span = tokens.shape[1:]
    place = lax.broadcasted_iota(jnp.int32, (1, span), 1) + scalars[0] * span
    result[:width, :] = tokens[0]
    seen = (key_mask[cell : cell + 1, :] == 1) & (place < scalars[2 + cells + cell])
    shape = (result.shape[0] - width, span)
    mark = lax.broadcasted_iota(jnp.int32, shape, 0) == 0
    hidden = jnp.where(seen, 0.0, MASKED)
    result[width:, :] = jnp.where(mark, hidden, 0.0).astype(jnp.bfloat16)


def widen(scalars, cell, tokens, key_mask, features):
    cells, width, span = tokens.shape
    return grid_call(
        partial(widen_kernel, cell, cells),
        (1,),
        [pl.BlockSpec((1, width, span), lambda g, me: (cell, 0, 0)), whole(key_mask)],
        pl.BlockSpec((features, span), lambda g, me: (0, 0)),
        jax.ShapeDtypeStruct((features, span), jnp.bfloat16),
        [],
        "widen",
        1,
        (scalars, tokens, key_mask),
        1,
    )


def second_norm_kernel(seq_count, scalars, weight, tokens, gain, shift, bias, *refs):
    parts = refs[:seq_count]
    middle, second, second_turned, attended, gather = refs[seq_count:]
    share = parts[0].shape[0]
    gain, shift, bias = columns_of(gain, shift, bias)
    for r in range(seq_count):
        place = pl.ds(pl.multiple_of((scalars[0] ^ r) * share, 8), share)
        gather[place, :] = parts[r][...].astype(jnp.float32)
    attended[...] = gather[: attended.shape[0], :].astype(jnp.bfloat16)
    total = dot(weight[...].T, attended[...])
    total = tokens[...].astype(jnp.float32) + (total + bias)
    middle[...] = total
    normal, _ = centred_columns(total)
    normed = (normal * gain + shift).astype(jnp.bfloat16)
    second_turned[...] = normed
    second[...] = normed.T


def second_norm(scalars, weight, tokens, vectors, parts):
    width, span = tokens.shape
    seq_count = len(parts)
    return no_grid_call(
        partial(second_norm_kernel, seq_count),
        (
            jax.ShapeDtypeStruct((width, span), jnp.float32),
            jax.ShapeDtypeStruct((span, width), jnp.bfloat16),
            jax.ShapeDtypeStruct((width, span), jnp.bfloat16),
            jax.ShapeDtypeStruct((width, span), jnp.bfloat16),
        ),
        "second_norm",
        2 * span * width * width,
        [scalars, weight, tokens, *vectors, *parts],
        [pltpu.VMEM((seq_count * parts[0].shape[0], span), jnp.float32)],
    )


def weights_kernel(seq_count, heads, head_size, scalars, mix, query, value, weight, bias, *turned):
    width = mix.shape[0]
    here = heads * head_size
    groups = head_groups(heads)
    weight[...] = jnp.zeros_like(weight)
    vectors = columns_of(query, value)
    row = lax.broadcasted_iota(jnp.int32, (HEAD_PAD, 1), 0)
    for _, count, base in groups:
        for p, least in ((0, (ONE_ROW, ONE_ROW + 1)), (1, (SPLIT_ROW, HEAD_PAD)), (2, (ONE_ROW, HEAD_PAD))):
            fill = jnp.where((row >= least[0]) & (row < least[1]), 1.0, 0.0)
            for n in range(count):
                place = (base + p * count + n) * HEAD_PAD
                bias[place : place + HEAD_PAD, :] = fill
    for s in range(seq_count):

        @pl.when(scalars[0] == s)
        def _():
            for p in range(3):
                first = s * here
                last = min(first + here, width)
                if last <= first:
                    continue
                start = (p * width + first) // LANES * LANES
                stop = min(-(-(p * width + last) // LANES) * LANES, mix.shape[1])
                block = mix[:, start:stop].astype(jnp.float32)
                block = block[:, p * width + first - start : p * width + last - start].T
                for group_first, count, base in groups:
                    for n in range(count):
                        h = group_first + n
                        if (h + 1) * head_size > last - first:
                            continue
                        place = (base + p * count + n) * HEAD_PAD
                        piece = block[h * head_size : (h + 1) * head_size]
                        room = jnp.zeros((HEAD_PAD - head_size, width), jnp.float32)
                        piece = jnp.concatenate([piece, room])
                        weight[place : place + HEAD_PAD, :width] = piece.astype(jnp.bfloat16)
                        if p != 1:
                            own = vectors[p // 2][first + h * head_size : first + (h + 1) * head_size]
                            bias[place : place + head_size, :] = own

    room = weight.shape[1] - width
    for (_, count, base), columns in zip(groups, turned):
        rows = slice(base * HEAD_PAD, (base + 3 * count) * HEAD_PAD)
        columns[...] = weight[rows, :width].T
        rows = slice((base + count) * HEAD_PAD, (base + 2 * count) * HEAD_PAD)
        row = lax.broadcasted_iota(jnp.int32, (count * HEAD_PAD, room), 0)
        lane = lax.broadcasted_iota(jnp.int32, (count * HEAD_PAD, room), 1)
        mark = (lane == 0) & (lax.rem(row, HEAD_PAD) == ONE_ROW)
        weight[rows, width:] = jnp.where(mark, 1.0, 0.0).astype(jnp.bfloat16)


def own_weights(scalars, mix, query, value, features, seq_count, heads, head_size):
    width = mix.shape[0]
    return no_grid_call(
        partial(weights_kernel, seq_count, heads, head_size),
        (
            jax.ShapeDtypeStruct((3 * heads * HEAD_PAD, features), jnp.bfloat16),
            jax.ShapeDtypeStruct((3 * heads * HEAD_PAD, 1), jnp.float32),
        )
        + tuple(
            jax.ShapeDtypeStruct((width, 3 * count * HEAD_PAD), jnp.bfloat16)
            for _, count, _ in head_groups(heads)
        ),
        "own_weights",
        1,
        [scalars, mix, query, value],
        [],
    )


def active_back_kernel(cotangent, down, result):
    for first, last in chunks(down.shape[1]):
        result[:, first:last] = dot(cotangent[...], down[:, first:last])


def active_back(scalars, cotangent, down):
    rows, width = cotangent.shape
    tile = hidden_tile(down.shape[1])
    shape = jax.ShapeDtypeStruct((rows, down.shape[1]), jnp.float32)
    return grid_call(
        lambda me, *refs: active_back_kernel(*refs),
        (down.shape[1] // tile,),
        [whole(cotangent), pl.BlockSpec((width, tile), lambda g, me: (0, g))],
        pl.BlockSpec((rows, tile), lambda g, me: (0, g)),
        shape,
        [],
        "active_back",
        1,
        (scalars, cotangent, down),
        1,
    )


def hidden_kernel(back_active, up, up_bias, *refs):
    *parts, active, back_upper, bias_back, second = refs

    @pl.when(pl.program_id(0) == 0)
    def _():
        for c, part in enumerate(parts):
            second[c * part.shape[0] : (c + 1) * part.shape[0], :] = part[...]

    inner = math.sqrt(2.0 / math.pi)
    for first, last in chunks(up.shape[1]):
        upper = dot(second[...], up[:, first:last]) + up_bias[:, first:last]
        back = back_active[:, first:last]
        square = upper * upper
        bend = jnp.tanh(inner * upper * (1.0 + 0.044715 * square))
        half = 0.5 + 0.5 * bend
        slope = half + (0.5 * inner) * upper * (1.0 - bend * bend) * (1.0 + 0.134145 * square)
        active[:, first:last] = (upper * half).astype(jnp.bfloat16)
        back = (back * slope).astype(jnp.bfloat16)
        back_upper[:, first:last] = back
        bias_back[:, first:last] = jnp.sum(back.astype(jnp.float32), axis=0, keepdims=True)


def grid_call(
    body, grid, in_specs, out_specs, out_shape, scratch, name, flops, inputs, moved, aliases=None
):
    return pl.pallas_call(
        body,
        out_shape=out_shape,
        grid_spec=pltpu.PrefetchScalarGridSpec(
            num_scalar_prefetch=1,
            grid=grid,
            in_specs=in_specs,
            out_specs=out_specs,
            scratch_shapes=scratch,
        ),
        compiler_params=pltpu.CompilerParams(vmem_limit_bytes=VMEM_LIMIT),
        cost_estimate=cost(name),
        input_output_aliases=aliases or {},
        name=name,
    )(*inputs)


def whole(array):
    zeros = (0,) * array.ndim
    return pl.BlockSpec(array.shape, lambda g, me: zeros)


def hidden_tile(hidden):
    return max(t for t in range(LANES, 1024, LANES) if hidden % t == 0)


def hidden_layer(scalars, second, back_active, up, up_bias):
    rows = sum(part.shape[0] for part in second)
    width = up.shape[0]
    hidden = up.shape[1]
    tile = hidden_tile(hidden)
    weight = pl.BlockSpec((width, tile), lambda g, me: (0, g))
    out = pl.BlockSpec((rows, tile), lambda g, me: (0, g))
    line = pl.BlockSpec((1, tile), lambda g, me: (0, g))
    return grid_call(
        lambda me, *refs: hidden_kernel(*refs),
        (hidden // tile,),
        [out, weight, line] + [whole(part) for part in second],
        [out, out, line],
        (
            jax.ShapeDtypeStruct((rows, hidden), jnp.bfloat16),
            jax.ShapeDtypeStruct((rows, hidden), jnp.bfloat16),
            jax.ShapeDtypeStruct((1, hidden), jnp.float32),
        ),
        [pltpu.VMEM((rows, width), jnp.bfloat16)],
        "hidden_layer",
        4 * rows * up.size,
        (scalars, back_active, up, up_bias, *second),
        4 * up.size + 4 * rows * hidden,
    )


def middle_back_kernel(
    seq_count,
    cells,
    scalars,
    back_upper,
    up,
    gain,
    cotangent,
    weight,
    *refs,
):
    middle, (back_middle, back_branch, sums) = refs[:cells], refs[cells : cells + 3]
    *parts, total, back_heads = refs[cells + 3 :]
    half = seq_count // 2
    step = pl.program_id(0)

    @pl.when(step == 0)
    def _():
        total[...] = jnp.zeros_like(total)

    for first, last in chunks(total.shape[1]):
        total[:, first:last] += dot_turned(up[...], back_upper[first:last, :])

    @pl.when(step == pl.num_programs(0) - 1)
    def _():
        span = cotangent.shape[2]
        heads = parts[0].shape[1]
        head_size = back_heads.shape[0] // (seq_count * heads)
        (gain_column,) = columns_of(gain)
        totals = [0.0] * 4
        for c in range(cells):
            here = slice(c * span, (c + 1) * span)
            normal, rise = centred_columns(middle[c][...])
            back = total[:, here]
            back_out = cotangent[c].astype(jnp.float32)
            back_mid = back_out + norm_pull(normal, rise, back, gain_column)
            back_middle[:, here] = back_mid
            branch = back_mid.astype(jnp.bfloat16)
            back_branch[:, here] = branch
            for n, term in enumerate((back * normal, back, branch.astype(jnp.float32), back_out)):
                totals[n] = totals[n] + jnp.sum(term, axis=1, keepdims=True)
            back_heads[: weight.shape[0], :] = dot(weight[...], branch)
            if back_heads.shape[0] > weight.shape[0]:
                rest = back_heads.shape[0] - weight.shape[0]
                back_heads[weight.shape[0] :, :] = jnp.zeros((rest, span), jnp.float32)
            for r in range(seq_count):
                first = (scalars[0] ^ r) * heads * head_size
                part = back_heads[pl.ds(pl.multiple_of(first, 8), heads * head_size), :]
                room = jnp.zeros((heads, HEAD_PAD - head_size, span), jnp.float32)
                part = jnp.concatenate([part.reshape(heads, head_size, span), room], axis=1)
                target = parts[r].at[c] if r < half else parts[half].at[r - half, c]
                target[...] = part.astype(jnp.bfloat16)
        sums[...] = lines_of(totals)


def middle_back(scalars, back_upper, up, middle, gain, cotangent, weight, seq_count, heads):
    rows, hidden = back_upper.shape
    cells, width, span = cotangent.shape
    head_size = width // HEADS
    tile = hidden_tile(hidden)
    outs = [
        jax.ShapeDtypeStruct((width, rows), jnp.float32),
        jax.ShapeDtypeStruct((width, rows), jnp.bfloat16),
        jax.ShapeDtypeStruct((8, width), jnp.float32),
    ]
    block = (cells, heads, HEAD_PAD, span)
    outs += [jax.ShapeDtypeStruct(block, jnp.bfloat16)] * (seq_count // 2)
    outs += [jax.ShapeDtypeStruct((seq_count // 2,) + block, jnp.bfloat16)]
    return grid_call(
        partial(middle_back_kernel, seq_count, cells),
        (hidden // tile,),
        [
            pl.BlockSpec((rows, tile), lambda g, me: (0, g)),
            pl.BlockSpec((width, tile), lambda g, me: (0, g)),
            whole(gain),
            whole(cotangent),
            whole(weight),
        ]
        + [whole(m) for m in middle],
        [whole(o) for o in outs],
        outs,
        [
            pltpu.VMEM((width, rows), jnp.float32),
            pltpu.VMEM((seq_count * heads * head_size, span), jnp.float32),
        ],
        "middle_back",
        2 * rows * up.size + 2 * rows * width * width,
        (scalars, back_upper, up, gain, cotangent, weight, *middle),
        1,
    )


def block_out_kernel(active, down, bias, *refs):
    *middle, result, total = refs
    step = pl.program_id(0)

    @pl.when(step == 0)
    def _():
        (bias_column,) = columns_of(bias)
        for c, part in enumerate(middle):
            span = part.shape[1]
            total[:, c * span : (c + 1) * span] = part[...] + bias_column

    for first, last in chunks(total.shape[1]):
        total[:, first:last] += dot_turned(down[...], active[first:last, :])

    @pl.when(step == pl.num_programs(0) - 1)
    def _():
        cells, _, span = result.shape
        for c in range(cells):
            result[c] = total[:, c * span : (c + 1) * span].astype(jnp.bfloat16)


def block_output(scalars, active, down, middle, bias):
    rows, hidden = active.shape
    cells, width = len(middle), middle[0].shape[0]
    tile = hidden_tile(hidden)
    out = jax.ShapeDtypeStruct((cells, width, rows // cells), jnp.bfloat16)
    return grid_call(
        lambda me, *refs: block_out_kernel(*refs),
        (hidden // tile,),
        [
            pl.BlockSpec((rows, tile), lambda g, me: (0, g)),
            pl.BlockSpec((width, tile), lambda g, me: (0, g)),
            whole(bias),
        ]
        + [whole(m) for m in middle],
        whole(out),
        out,
        [pltpu.VMEM((width, rows), jnp.float32)],
        "block_output",
        2 * rows * down.size,
        (scalars, active, down, bias, *middle),
        1,
    )


def take_columns(piece, right, count, which):
    width = piece.shape[1]
    for s in range(count):

        @pl.when(which == s)
        def _():
            first = s * width // LANES * LANES
            last = min(-(-(s + 1) * width // LANES) * LANES, right.shape[1])
            block = right[:, first:last]
            piece[...] = block[:, s * width - first : (s + 1) * width - first]


def up_outer_kernel(seq_count, cells, share, cut, zbit, split, scalars, right, *refs):
    left, rest = refs[:cells], refs[cells:]
    got = rest[0] if split else None
    *results, total, piece, joined = rest[3 if split else 0 :]
    rows = left[0].shape[0]
    core = 0 if split else 1

    @pl.when(pl.program_id(0) == 0)
    def _():
        for c, part in enumerate(left):
            joined[:, c * part.shape[1] : (c + 1) * part.shape[1]] = part[...]

    take_columns(piece, right, seq_count, (2 * pl.program_id(0) + core) ^ scalars[0])
    for first, last in chunks(piece.shape[1]):
        total[:, first:last] = dot(joined[...], piece[:, first:last])
    cell_count = results[0].shape[1] * (2 if split else 1)
    height = results[0].shape[2] if not split else got.shape[2]
    for k in range(cell_count):
        c = k ^ scalars[1]
        start = jnp.minimum(lax.div(c * share, 8) * 8, rows - height)
        block = total[pl.ds(pl.multiple_of(start, 8), height), :]
        if split:
            block = block + got[0, k].astype(jnp.float32)
            for n, (bit, part) in enumerate(((1, block[:cut]), (zbit, block[cut:]))):
                target = results[2 * n + (0 if k & bit else 1)]
                target[0, without_bit(k, bit)] = part.astype(jnp.bfloat16)
        else:
            results[0][0, k] = block.astype(jnp.bfloat16)


def up_outer(scalars, left, right, seq_count, cell_count, got=None, lower=None):
    tokens, width = right.shape[0], right.shape[1] // seq_count
    rows = left[0].shape[0]
    _, height = row_cover(rows, cell_count)
    half = seq_count // 2
    split = got is not None
    cut = two_thirds(height)
    in_specs = [whole(right)] + [whole(part) for part in left]
    inputs = [scalars, right, *left]
    aliases = {}
    if split:
        in_specs.append(pl.BlockSpec((1,) + got.shape[1:], lambda g, me: (g, 0, 0, 0)))
        in_specs += [pl.BlockSpec(memory_space=pl.ANY)] * 2
        inputs += [got, *lower]
        aliases = {len(inputs) - 2: 2, len(inputs) - 1: 3}
        outs = [(half, cell_count // 2, cut, width)] * 2 + [lower[0].shape] * 2
        low = height - cut
        blocks = [pl.BlockSpec((1,) + outs[0][1:], lambda g, me: (g, 0, 0, 0))] * 2
        blocks += [
            pl.BlockSpec((1, cell_count // 2, low, width), lambda g, me: (g, 0, 1, 0))
        ] * 2
    else:
        outs = [(half, cell_count, height, width)]
        blocks = [pl.BlockSpec((1,) + outs[0][1:], lambda g, me: (g, 0, 0, 0))]
    return grid_call(
        partial(
            up_outer_kernel,
            seq_count,
            len(left),
            rows // cell_count,
            cut,
            cell_count // seq_count,
            split,
        ),
        (half,),
        in_specs,
        blocks,
        [jax.ShapeDtypeStruct(out, jnp.bfloat16) for out in outs],
        [
            pltpu.VMEM((rows, width), jnp.float32),
            pltpu.VMEM((tokens, width), jnp.bfloat16),
            pltpu.VMEM((rows, tokens), jnp.bfloat16),
        ],
        "up_outer",
        1,
        inputs,
        1,
        aliases,
    )


def two_thirds(height):
    return -(-height * 2 // 3 // 16) * 16


def down_outer_kernel(seq_count, inner, cut, split, scalars, left, right, *refs):
    got = refs[0] if split else None
    *results, total, piece, wide, own = refs[1 if split else 0 :]
    half = seq_count // 2
    share = own.shape[0] // half
    span = left.shape[2]
    width = piece.shape[1] // inner
    low = scalars[1] & (inner - 1)
    step = pl.program_id(0)
    core = 0 if split else 1
    starts, height = row_cover(share, inner)

    @pl.when(step == 0)
    def _():
        for c in range(left.shape[0]):
            wide[:, c * span : (c + 1) * span] = left[c].astype(jnp.float32)
        for x in range(half):
            for s in range(seq_count):

                @pl.when(((2 * x + core) ^ scalars[0]) == s)
                def _():
                    own[x * share : (x + 1) * share, :] = wide[s * share : (s + 1) * share, :]

    take_columns(piece, right, seq_count, step ^ lax.div(scalars[1], inner))
    for first, last in chunks(piece.shape[1]):
        total[:, first:last] = dot(own[...].astype(jnp.bfloat16), piece[:, first:last])
    for q in range(inner):
        for x in range(half):
            block = total[x * share : (x + 1) * share, q * width : (q + 1) * width]
            block = jnp.concatenate([block[s : s + height] for s in starts], axis=1)
            if split:
                block = block + got[x, q ^ low].astype(jnp.float32)
                away = 2 * x >= half
                target = results[0 if away else 1]
                target[x % (half // 2), q ^ low] = block[:cut].astype(jnp.bfloat16)
                rest = block[cut:].astype(jnp.bfloat16)

                @pl.when(step & 1 == 1)
                def _():
                    results[2][x, q ^ low] = rest

                @pl.when(step & 1 == 0)
                def _():
                    results[3][x, q ^ low] = rest

            else:
                results[0][x, q ^ low] = block.astype(jnp.bfloat16)


def down_outer(scalars, left, right, seq_count, cell_count, got=None):
    tokens, width = right.shape[0], right.shape[1] // seq_count
    half = seq_count // 2
    inner = cell_count // seq_count
    share = left.shape[1] // seq_count
    split = got is not None
    _, height = row_cover(share, inner)
    cut = two_thirds(height)
    in_specs = [whole(left), whole(right)]
    inputs = [scalars, left, right]
    if split:
        in_specs.append(pl.BlockSpec((half, inner) + got.shape[2:], lambda g, me: (0, g, 0, 0)))
        inputs.append(got)
        low = height - cut
        outs = [(half // 2, cell_count, cut, width)] * 2
        outs += [(half, cell_count // 2, 2 * low, width)] * 2
        blocks = [pl.BlockSpec((half // 2, inner, cut, width), lambda g, me: (0, g, 0, 0))] * 2
        blocks += [pl.BlockSpec((half, inner, low, width), lambda g, me: (0, g // 2, 0, 0))] * 2
    else:
        outs = [(half, cell_count, height, width)]
        blocks = [pl.BlockSpec((half, inner, height, width), lambda g, me: (0, g, 0, 0))]
    return grid_call(
        partial(down_outer_kernel, seq_count, inner, cut, split),
        (seq_count,),
        in_specs,
        blocks,
        [jax.ShapeDtypeStruct(out, jnp.bfloat16) for out in outs],
        [
            pltpu.VMEM((half * share, width), jnp.float32),
            pltpu.VMEM((tokens, width), jnp.bfloat16),
            pltpu.VMEM((left.shape[1], tokens), jnp.float32),
            pltpu.VMEM((half * share, tokens), jnp.float32),
        ],
        "down_outer",
        1,
        inputs,
        1,
    )


def out_outer_kernel(seq_count, cells, share, scalars, right, *refs):
    left, (result, total, joined) = refs[:cells], refs[cells:]
    for c, part in enumerate(left):
        joined[:, c * part.shape[1] : (c + 1) * part.shape[1]] = part[...]
    rows = total.shape[0]
    for first, last in chunks(total.shape[1]):
        total[:, first:last] = dot_turned(joined[...], right[first:last, :])
    width = total.shape[1] // seq_count
    _, cell_count, part, room = result.shape
    groups = room // width
    for k in range(cell_count):
        c = k ^ scalars[1]
        start = jnp.minimum(lax.div(c * share, 8) * 8, rows - groups * part)
        block = total[pl.ds(pl.multiple_of(start, 8), groups * part), :]
        for s in range(seq_count):
            piece = block[:, s * width : (s + 1) * width]
            pieces = [piece[i * part : (i + 1) * part] for i in range(groups)]
            pieces.append(jnp.zeros((part, room - groups * width), jnp.float32))
            place = s ^ scalars[0]
            place = (place & 1) * (seq_count // 2) + (place >> 1)
            result[place, k] = jnp.concatenate(pieces, axis=1).astype(jnp.bfloat16)


def out_outer(scalars, left, right, room, seq_count, cell_count):
    rows, tokens = right.shape
    groups = room * seq_count // rows
    _, height = row_cover(rows, cell_count, 16 * groups)
    shape = (seq_count, cell_count, height // groups, room)
    return no_grid_call(
        partial(out_outer_kernel, seq_count, len(left), rows // cell_count),
        jax.ShapeDtypeStruct(shape, jnp.bfloat16),
        "out_outer",
        1,
        [scalars, right, *left],
        [pltpu.VMEM((rows, rows), jnp.float32), pltpu.VMEM((rows, tokens), jnp.bfloat16)],
    )


def vector_kernel(cells, heads, head_size, seq_count, scalars, middle, hidden, *refs):
    first, sums, (result, own) = refs[:cells], refs[cells:-2], refs[-2:]
    own[...] = jnp.zeros_like(own)
    width = middle.shape[1]
    for s in range(seq_count):

        @pl.when(scalars[0] == s)
        def _():
            for (start, count, _), part in zip(head_groups(heads), sums):
                for n in range(count):
                    at = ((s * heads) + start + n) * head_size
                    if at >= width:
                        continue
                    for row, p in enumerate((0, 2)):
                        source = (p * count + n) * HEAD_PAD
                        own[row : row + 1, at : at + head_size] = part[
                            :, source : source + head_size
                        ]

    total = sum(part[0:2, :] for part in first)
    lines = [total[0:1], total[1:2], own[0:1, :], own[1:2, :]]
    lines += [middle[n : n + 1, :] for n in (2, 0, 1, 3)]
    count, rows, share = result.shape
    for c in range(count):
        place = c ^ scalars[1]
        for n, line in enumerate(lines):
            result[place, n : n + 1, :] = line[:, c * share : (c + 1) * share]
        for n in range(rows - 8):
            at = (c * (rows - 8) + n) * share
            result[place, 8 + n : 9 + n, :] = hidden[:, at : at + share]


def vector_blocks(
    scalars, first, sums, middle, hidden, heads, head_size, seq_count, cell_count
):
    share = middle.shape[1] // cell_count
    rows = 8 + hidden.shape[1] // middle.shape[1]
    return no_grid_call(
        partial(vector_kernel, len(first), heads, head_size, seq_count),
        jax.ShapeDtypeStruct((cell_count, rows, share), jnp.float32),
        "vector_blocks",
        1,
        [scalars, middle, hidden, *first, *sums],
        [pltpu.VMEM((8, middle.shape[1]), jnp.float32)],
    )


def mix_columns_kernel(heads, head_size, scalars, *refs):
    *blocks, result = refs
    places = {}
    for first, count, base in head_groups(heads):
        places.update({(p, first + n): base + p * count + n for p in range(3) for n in range(count)})
    seq_count = len(blocks)
    share = result.shape[1]
    width = HEADS * head_size
    for mine in range(seq_count):

        @pl.when(scalars[0] == mine)
        def _():
            for p in range(3):
                for head in range(HEADS):
                    first = p * width + head * head_size - mine * share
                    cut_left, cut_right = max(0, -first), min(head_size, share - first)
                    if cut_left >= cut_right:
                        continue
                    block = blocks[(head // heads) ^ mine]
                    source = places[p, head % heads] * HEAD_PAD
                    base = source // LANES * LANES
                    piece = block[:, base : min(base + LANES, block.shape[1])].astype(jnp.float32)
                    source -= base
                    result[:, first + cut_left : first + cut_right] = piece[
                        :, source + cut_left : source + cut_right
                    ]


def mix_columns(scalars, blocks, heads, head_size):
    rows = blocks[0].shape[0]
    return no_grid_call(
        partial(mix_columns_kernel, heads, head_size),
        jax.ShapeDtypeStruct((rows, 3 * HEADS * head_size // len(blocks)), jnp.float32),
        "mix_columns",
        1,
        [scalars, *blocks],
        [],
    )


def tokens_back_kernel(tokens, gain, back_middle, *refs):
    *terms, result = refs
    cells, _, span = tokens.shape
    (gain,) = columns_of(gain)
    for c in range(cells):
        normal, rise = centred_columns(tokens[c].astype(jnp.float32))
        back = terms[2 * c][...].astype(jnp.float32) + terms[2 * c + 1][...].astype(jnp.float32)
        back_in = back_middle[:, c * span : (c + 1) * span]
        back_in = back_in + norm_pull(normal, rise, back, gain)
        result[c] = back_in.astype(jnp.bfloat16)


def tokens_back(tokens, gain, back_middle, terms):
    return no_grid_call(
        tokens_back_kernel,
        jax.ShapeDtypeStruct(tokens.shape, jnp.bfloat16),
        "tokens_back",
        1,
        [tokens, gain, back_middle, *terms],
        [],
        scalars=0,
    )


def order_after(values, *earlier):
    values, _ = lax.optimization_barrier((values, earlier))
    return values


def advance(parts, last):
    groups = {}
    running = [part for part in parts if part.order]
    arrived = [part.got for part in running]
    for part in running:
        part.got = order_after(part.got, arrived)
        key = (part.kind, tuple(part.names), tuple(part.order), part.keep.shape[2])
        groups.setdefault(key, []).append(part)
    for first, *others in groups.values():
        last = first.step(last, *others)
    return last


def on_device(
    tokens,
    first_gain,
    first_shift,
    mix_weight,
    query_bias,
    value_bias,
    out_weight,
    out_bias,
    second_gain,
    second_shift,
    up_weight,
    up_bias,
    down_weight,
    down_bias,
    cotangent,
    prefix_lengths,
    gene_counts,
    key_mask,
):
    cells_here, span, width = tokens.shape
    head_size = width // HEADS
    length = span * lax.axis_size("seq")
    start = lax.axis_index("seq") * span
    seq_count, cell_count = lax.axis_size("seq"), lax.axis_size("cells")
    me = jnp.stack([lax.axis_index("seq"), lax.axis_index("cells")]).astype(jnp.int32)
    totals = prefix_lengths + gene_counts
    row_count = cells_here * span
    own_rows = start + jnp.arange(span)
    heads_here = -(-HEADS // seq_count)
    head_total = heads_here * seq_count
    features = -(-(width + 1) // LANES) * LANES
    scalars = jnp.concatenate([me, prefix_lengths, totals])

    def flat(array):
        return array.reshape(row_count, array.shape[-1])

    groups = head_groups(heads_here)
    tokens_turned = tokens.transpose(0, 2, 1)
    cotangent_turned = cotangent.transpose(0, 2, 1)
    down_turned = down_weight.T
    wide = []
    for c in range(cells_here):
        wide.append(widen(order_after(scalars, wide), c, tokens_turned, key_mask, features))
    weight, bias, *weights_turned = own_weights(
        order_after(scalars, wide),
        mix_weight,
        query_bias,
        value_bias,
        features,
        seq_count,
        heads_here,
        head_size,
    )
    x_bits = [b for b in reversed(bits_of(seq_count)) if b > 1]
    near = [swap_with(block, "seq", 1) for block in wide]
    back_active = active_back(scalars, order_after(flat(cotangent), weight), down_turned)
    held = [{0: wide[c]} for c in range(cells_here)]
    for c in range(cells_here):
        for bit in x_bits:
            for r, block in list(held[c].items()):
                after = (held[c - 1][x_bits[0]], back_active) if c > 0 else ()
                held[c][r | bit] = swap_with(order_after(block, *after), "seq", bit)

    attended, kept = [], []
    last = (back_active,)
    blocks, normed = [], []
    for c in range(cells_here):
        after = last
        for r, block in list(held[c].items()):
            held[c][r | 1] = near[c] if r == 0 else swap_with(order_after(block, *after), "seq", 1)
        blocks.append([held[c][r] for r in range(seq_count)])
        results = attend_forward(
            scalars,
            c,
            order_after(blocks[c], *last),
            weight,
            bias,
            first_gain,
            first_shift,
            heads_here,
            head_size,
        )
        qkv, (out, normed_cell, *parts) = results[: len(groups)], results[len(groups) :]
        last = (out,)
        kept.append((qkv, out))
        normed.append(normed_cell)
        attended.append(exchanged_blocks(parts))
    middle, second, second_turned, attended_turned = [], [], [], []
    for c in range(cells_here):
        results = second_norm(
            scalars,
            out_weight,
            tokens_turned[c],
            (second_gain, second_shift, out_bias),
            order_after(attended[c], *last),
        )
        last = (results[0],)
        for held, result in zip((middle, second, second_turned, attended_turned), results):
            held.append(result)
    active, back_upper, up_bias_back = hidden_layer(
        scalars, second, back_active, up_weight, up_bias.reshape(1, -1)
    )
    (down_send,) = down_outer(scalars, cotangent_turned, active, seq_count, cell_count)
    down_got = swap_with(down_send, "seq", 1)
    (up_send,) = up_outer(
        scalars, second_turned, order_after(back_upper, down_send), seq_count, cell_count
    )
    up_got = swap_with(up_send, "seq", 1)
    *down_halves, lower_send, lower_keep = down_outer(
        scalars, cotangent_turned, order_after(active, up_send), seq_count, cell_count, down_got
    )
    *up_halves, lower_send, lower_keep = up_outer(
        scalars,
        second_turned,
        order_after(back_upper, down_halves),
        seq_count,
        cell_count,
        up_got,
        (lower_send, lower_keep),
    )

    def flat_blocks(array):
        return array.reshape((-1,) + array.shape[-2:])

    x_bits = [("seq", b) for b in reversed(bits_of(seq_count)) if b > 1]
    cell_bits = [("cells", b) for b in reversed(bits_of(cell_count))]
    names = x_bits + cell_bits
    y_bit, z_bit = ("cells", 1), ("cells", cell_count // seq_count)
    rest = [n for n in reversed(cell_bits) if n not in (y_bit, z_bit)]
    running = [
        Reduction("down", names, x_bits + [y_bit, z_bit] + rest, *map(flat_blocks, down_halves)),
        Reduction("up", names, [y_bit, z_bit] + x_bits + rest, *map(flat_blocks, up_halves)),
        Reduction(
            "both",
            names,
            [z_bit] + x_bits + [y_bit] + rest,
            flat_blocks(lower_send),
            flat_blocks(lower_keep),
        ),
    ]
    back_middle, back_branch, middle_sums, *back_heads = middle_back(
        scalars,
        order_after(back_upper, up_halves),
        up_weight,
        middle,
        second_gain,
        cotangent_turned,
        out_weight,
        seq_count,
        heads_here,
    )
    back_upper_half = route_upper(back_heads[-1])
    down_part, up_part, both_part = running
    out_shares = out_outer(
        scalars,
        attended_turned,
        order_after(back_branch, back_heads),
        3 * groups[0][1] * HEAD_PAD,
        seq_count,
        cell_count,
    )
    out_part = Reduction(
        "out",
        [("seq", 1)] + names,
        [("seq", 1)] + x_bits + [y_bit, z_bit] + rest,
        flat_blocks(out_shares[seq_count // 2 :]),
        flat_blocks(out_shares[: seq_count // 2]),
    )
    block_out = block_output(
        scalars, order_after(active, out_shares), down_turned, middle, down_bias
    )
    last = down_part.step(block_out)
    back_arrays, back_places = route_rest(
        back_heads[:-1], order_after(back_upper_half, last)
    )
    last = advance([up_part, both_part], last)
    mixed_back, mix_parts = [[], []], []
    back_normed, bias_backs, first_sums = [], [], []

    def mix_reductions(group, last):
        *halves, sums = mix_outer(
            scalars,
            normed,
            order_after(mixed_back[group], last),
            width,
            cell_count,
        )
        bias_backs.append(sums)
        label = ["first", "second"][group]
        return [
            Reduction(label + " upper", cell_bits, [y_bit, z_bit] + rest, *halves[:2]),
            Reduction(label + " lower", cell_bits, [z_bit, y_bit] + rest, *halves[2:]),
        ], halves[0]

    def attend_group(c, group, last):
        qkv, out = kept[c]
        back = attend_backward(
            scalars,
            c,
            qkv[group],
            out,
            order_after(back_arrays, last),
            back_places,
            groups[group][0],
            head_size,
        )
        mixed_back[group].append(back)
        return back

    def normed_reduction(c, last):
        *parts, sums = normed_back(
            weights_turned, [order_after(mixed_back[g][c], last) for g in range(2)], blocks[c]
        )
        first_sums.append(sums)
        back_normed.append(PositionSum(parts))
        return sums

    for c in range(cells_here):
        final = c == cells_here - 1
        last = attend_group(c, 0, last)
        if final:
            last = advance(running, last)
            last = out_part.step(last)
            for earlier in range(c):
                last = normed_reduction(earlier, last)
            parts, last = mix_reductions(0, last)
            mix_parts.append(parts)
        last = attend_group(c, 1, last)
        if c == 0:
            last = advance(running, last)
    for part in back_normed:
        last = part.step(last)
    while len(out_part.order) >= len(cell_bits):
        last = out_part.step(last)
    parts, last = mix_reductions(1, last)
    mix_parts.append(parts + [out_part])
    last = advance(mix_parts[0], last)
    done = [part.got for part in running if part.labels and not part.order]
    last = normed_reduction(cells_here - 1, (last, done))
    vectors = VectorSum(
        vector_blocks(
            scalars,
            order_after(first_sums, last),
            bias_backs,
            middle_sums,
            up_bias_back,
            heads_here,
            head_size,
            seq_count,
            cell_count,
        ),
        seq_count,
    )
    last = advance(mix_parts[1], (last, [part.got for part in back_normed[:-1]]))
    last = vectors.step(last)
    last = advance(mix_parts[0], last)
    last = back_normed[-1].step(last)
    last = vectors.step(last)
    last = advance(mix_parts[1], last)
    last = vectors.step(last)
    while any(part.bits for part in back_normed):
        for part in back_normed:
            last = part.step(last) if part.bits else last
    running += mix_parts[0] + mix_parts[1]
    running = [part for part in running if part.labels]
    while any(part.order for part in running):
        last = advance(running, last)
    while vectors.order:
        last = vectors.step(last)
    terms = [x for part in back_normed for x in part.terms()]
    tokens_gradient = tokens_back(
        tokens_turned, first_gain, back_middle, order_after(terms, last)
    )
    last = tokens_gradient
    joined = vectors.step(last)[0]
    vectors = [*(joined[n] for n in range(7)), joined[8:].reshape(-1), joined[7]]
    blocks = {}
    for part in running:
        blocks.update(part.finish(last))
    low = blocks["both"].shape[0] // 2

    def ungrouped(block, starts, share):
        pieces = jnp.split(block, len(starts), axis=1)
        cuts = [share * n - start for n, start in enumerate(starts)]
        return jnp.concatenate([p[c : c + share] for p, c in zip(pieces, cuts)])

    down_part = jnp.concatenate([blocks["down"], blocks["both"][:low]])
    down_share = width // seq_count
    down_starts, _ = row_cover(down_share, cell_count // seq_count)
    down_part = ungrouped(down_part, down_starts, down_share // len(down_starts))
    up_part = jnp.concatenate([blocks["up"], blocks["both"][low:]])
    mix_part = jnp.concatenate(
        [
            jnp.concatenate([blocks[g + " upper"], blocks[g + " lower"]])
            for g in ("first", "second")
        ],
        axis=1,
    )
    mix_part = mix_columns(
        scalars,
        gathered_blocks(mix_part.astype(jnp.bfloat16), seq_count),
        heads_here,
        head_size,
    )
    group = blocks["out"].shape[0]
    out_groups = blocks["out"].shape[1] * seq_count // width
    out_part = blocks["out"][:, : out_groups * (width // seq_count)]
    out_part = ungrouped(out_part, [group * n for n in range(out_groups)], group)

    def own_rows_of(part, unit=16):
        starts, _ = row_cover(width, cell_count, unit)
        share = width // cell_count
        shift = jnp.array([share * c - starts[c] for c in range(cell_count)])[me[1]]
        return lax.dynamic_slice_in_dim(part, shift, share, axis=0)

    matrices = (
        own_rows_of(mix_part),
        own_rows_of(out_part, 16 * out_groups),
        own_rows_of(up_part),
        down_part.T,
    )
    return (
        block_out.transpose(0, 2, 1),
        tokens_gradient.transpose(0, 2, 1),
        vectors[0],
        vectors[1],
        matrices[0],
        vectors[2],
        vectors[3],
        matrices[1],
        vectors[4],
        vectors[5],
        vectors[6],
        matrices[2],
        vectors[7],
        matrices[3],
        vectors[8],
    )


def solution(mesh):
    return jax.shard_map(
        on_device,
        mesh=mesh,
        in_specs=(
            P("cells", "seq", None),
            P(),
            P(),
            P(),
            P(),
            P(),
            P(),
            P(),
            P(),
            P(),
            P(),
            P(),
            P(),
            P(),
            P("cells", "seq", None),
            P("cells"),
            P("cells"),
            P("cells", "seq"),
        ),
        out_specs=(
            P("cells", "seq", None),
            P("cells", "seq", None),
            P("cells"),
            P("cells"),
            P("cells", "seq"),
            P("cells"),
            P("cells"),
            P("cells", "seq"),
            P("cells"),
            P("cells"),
            P("cells"),
            P("cells", "seq"),
            P("cells"),
            P("cells", "seq"),
            P("cells"),
        ),
        check_vma=False,
    )
```

```python
from functools import partial
import math

import jax
import jax.numpy as jnp
from jax import lax
from jax.experimental import pallas as pl
from jax.experimental.pallas import tpu as pltpu
from jax.sharding import PartitionSpec as P

HEADS = 20
LANES = 128
TILE = 256
HEAD_PAD = 64
MASKED = -1e30
ONE_ROW = 56
SPLIT_ROW = 57
VMEM_LIMIT = 20 * 1024 * 1024
SHORT = pl.CostEstimate(flops=1, bytes_accessed=1, transcendentals=0)


COSTS = {'widen': 3, 'attend_forward': 14, 'own_weights': 4}


def cost(name):
    return pl.CostEstimate(flops=COSTS.get(name, 0) * 10**9 + 1, bytes_accessed=1, transcendentals=0)


def bits_of(count):
    return [1 << b for b in range(count.bit_length() - 1)]


def swap_with(array, axis, bit):
    count = lax.axis_size(axis)
    return lax.ppermute(array, axis, [(i, i ^ bit) for i in range(count)])


def without_bit(index, bit):
    return (index // (2 * bit)) * bit + index % bit


def add_halves_kernel(count, *refs):
    for n in range(count):
        mine_away, got_away, mine_here, got_here = refs[4 * n : 4 * n + 4]
        first = sum(refs[4 * p].shape[1] for p in range(n))
        rows = slice(first, first + mine_away.shape[1])
        for mine, got, result in (
            (mine_away, got_away, refs[4 * count]),
            (mine_here, got_here, refs[4 * count + 1]),
        ):
            total = mine[...].astype(jnp.float32) + got[...].astype(jnp.float32)
            result[:, rows, :] = total.astype(jnp.bfloat16)


def add_halves(pairs, bit):
    count, _, width = pairs[0][0].shape
    rows = sum(mine.shape[1] for mine, _ in pairs)
    shape = jax.ShapeDtypeStruct((count // 2, rows, width), jnp.bfloat16)
    in_specs, inputs = [], []
    for mine, got in pairs:
        for value in (bit, 0):
            spec = pl.BlockSpec(
                (1,) + mine.shape[1:],
                lambda g, value=value: ((g // bit) * (2 * bit) + value + g % bit, 0, 0),
            )
            in_specs += [spec, spec]
            inputs += [mine, got]
    out = pl.BlockSpec((1, rows, width), lambda g: (g, 0, 0))
    return pl.pallas_call(
        partial(add_halves_kernel, len(pairs)),
        out_shape=(shape, shape),
        grid=(count // 2,),
        in_specs=in_specs,
        out_specs=(out, out),
        compiler_params=pltpu.CompilerParams(vmem_limit_bytes=VMEM_LIMIT),
        cost_estimate=SHORT,
        name="add_halves",
    )(*inputs)


class Reduction:
    def __init__(self, label, names, order, send, keep, kind=None):
        self.labels = [label]
        self.kind = kind
        self.names, self.order = list(names), list(order)
        self.keep = keep
        self.heights = [keep.shape[1]]
        self.leave(send)

    def leave(self, send):
        axis, bit = self.order.pop(0)
        self.names.remove((axis, bit))
        self.got = swap_with(send, axis, bit)

    def step(self, last, *others):
        place = self.names.index(self.order[0])
        bit = 1 << (len(self.names) - 1 - place)
        pairs = [order_after((p.keep, p.got), last) for p in (self,) + others]
        for other in others:
            assert (other.names, other.order) == (self.names, self.order)
            self.heights += other.heights
            self.labels += other.labels
            other.labels, other.order = [], []
        send, self.keep = add_halves(pairs, bit)
        self.leave(send)
        return self.keep

    def finish(self, last):
        while self.order:
            last = self.step(last)
        total = order_after(self.keep, last).astype(jnp.float32) + self.got.astype(jnp.float32)
        ends = [sum(self.heights[:n]) for n in range(len(self.heights) + 1)]
        return {label: total[0, a:b] for label, a, b in zip(self.labels, ends, ends[1:])}


def row_cover(rows, count, unit=16):
    share = rows // count
    starts = [share * c // 8 * 8 for c in range(count)]
    height = max(share * (c + 1) - starts[c] for c in range(count))
    height = -(-height // unit) * unit
    return [min(s, rows - height) for s in starts], height


def head_groups(heads):
    first = -(-heads * 3 // 5)
    return [(0, first, 0), (first, heads - first, 3 * first)]


def no_grid_call(body, out_shape, name, flops, inputs, scratch, scalars=1):
    in_specs = [pl.BlockSpec(memory_space=pltpu.SMEM)] * scalars
    in_specs += [pl.BlockSpec(memory_space=pltpu.VMEM)] * (len(inputs) - scalars)
    moved = sum(x.size * x.dtype.itemsize for x in inputs)
    moved += sum(math.prod(x.shape) * x.dtype.itemsize for x in jax.tree.leaves(out_shape))
    return pl.pallas_call(
        body,
        out_shape=out_shape,
        in_specs=in_specs,
        out_specs=jax.tree.map(lambda _: pl.BlockSpec(memory_space=pltpu.VMEM), out_shape),
        scratch_shapes=scratch,
        compiler_params=pltpu.CompilerParams(vmem_limit_bytes=VMEM_LIMIT),
        cost_estimate=cost(name),
        name=name,
    )(*inputs)


def make_diagonal(diag_ref, keys, tile, prefix):
    first = tile * TILE
    shape = (TILE, TILE)
    key_at = lax.broadcasted_iota(jnp.int32, shape, 0)
    row_at = lax.broadcasted_iota(jnp.int32, shape, 1)
    opened = keys[first : first + TILE, ONE_ROW : ONE_ROW + 1].astype(jnp.float32) > -1.0
    near = (key_at <= row_at) | (key_at + first < prefix)
    seen = (near & opened) | (key_at == row_at)
    diag_ref[tile] = jnp.where(seen, 0.0, MASKED)


def without_mask(keys):
    lane = lax.broadcasted_iota(jnp.int32, keys.shape, 1)
    return jnp.where(lane == ONE_ROW, 0.0, keys.astype(jnp.float32)).astype(jnp.bfloat16)


def turned_rows(columns):
    return columns.astype(jnp.float32).T.astype(jnp.bfloat16)


def split_rows(columns, value):
    row = lax.broadcasted_iota(jnp.int32, columns.shape, 0)
    result = columns.astype(jnp.float32)
    for place in range(3):
        part = value.astype(jnp.bfloat16).astype(jnp.float32)
        value = value - part
        result = jnp.where(row == SPLIT_ROW + place, part, result)
    return result.astype(jnp.bfloat16)


def forward_kernel(seq_count, cell, span, heads, head_size, rate, scalars, *refs):
    blocks, (weight, bias, gain, shift) = refs[:seq_count], refs[seq_count : seq_count + 4]
    groups = head_groups(heads)
    *qkv_groups, out, normed = refs[seq_count + 4 : seq_count + 6 + len(groups)]
    *parts, rows, diag, scores = refs[seq_count + 6 + len(groups) :]
    width = gain.shape[0]
    gain, shift = columns_of(gain, shift)
    me, prefix = scalars[0], scalars[2 + cell]
    length = span * seq_count
    tiles = length // TILE
    for r in range(seq_count):
        here = slice(r * span, (r + 1) * span)
        normal, _ = centred_columns(blocks[r][:width, :].astype(jnp.float32))
        normed[:width, here] = (normal * gain + shift).astype(jnp.bfloat16)
        normed[width:, here] = blocks[r][width:, :]
        mixed = jnp.dot(weight[...], normed[:, here], preferred_element_type=jnp.float32)
        mixed = (mixed + bias[...]).astype(jnp.bfloat16)
        place = pl.ds(pl.multiple_of((me ^ r) * span, LANES), span)
        mixed = mixed.reshape(3 * heads, HEAD_PAD, span)
        for (_, count, base), qkv in zip(groups, qkv_groups):
            qkv[:, :, place] = mixed[base : base + 3 * count]

    def turn(first, count, qkv, h, carry):
        rows[first + h] = turned_rows(qkv[count + h])
        return carry

    for (first, count, _), qkv in zip(groups, qkv_groups):
        lax.fori_loop(0, count, partial(turn, first, count, qkv), 0)
    for tile in range(tiles):
        make_diagonal(diag, rows.at[0], tile, prefix)

    def one_head(start, count, qkv, h, carry):
        for tile in range(tiles):
            across = slice(tile * TILE, (tile + 1) * TILE)
            query = qkv[h, :, across]
            tops = None
            for j in range(tile + 1):
                down = slice(j * TILE, (j + 1) * TILE)
                keys = rows[start + h, down, :]
                if j == tile:
                    keys = without_mask(keys)
                block = jnp.dot(keys, query, preferred_element_type=jnp.float32)
                if j == tile:
                    block = block + diag[tile]
                scores[down, :] = block
                top = jnp.max(block.reshape(TILE // 8, 8, TILE), axis=0)
                tops = top if tops is None else jnp.maximum(tops, top)
            top = jnp.max(tops, axis=0, keepdims=True)
            total = jnp.zeros((HEAD_PAD, TILE), jnp.float32)
            for j in range(tile + 1):
                down = slice(j * TILE, (j + 1) * TILE)
                probs = jnp.exp2((scores[down, :] - top) * rate).astype(jnp.bfloat16)
                total += jnp.dot(
                    qkv[2 * count + h, :, down], probs, preferred_element_type=jnp.float32
                )
            summed = total[ONE_ROW : ONE_ROW + 1]
            row = lax.broadcasted_iota(jnp.int32, total.shape, 0)
            log_sum = top * rate + jnp.log2(summed)
            out[start + h, :, across] = jnp.where(row == ONE_ROW, log_sum, total / summed)
        return carry

    for (first, count, _), qkv in zip(groups, qkv_groups):
        lax.fori_loop(0, count, partial(one_head, first, count, qkv), 0)
    for r in range(seq_count):
        place = pl.ds(pl.multiple_of((me ^ r) * span, LANES), span)
        piece = out[:, :head_size, place].reshape(heads * head_size, span)
        parts[r][...] = piece.astype(jnp.bfloat16)


def backward_kernel(seq_count, places, cell, span, first_head, heads, head_size, rate, scalars, *refs):
    qkv, out, *arrays, result = refs[:-6]
    back, query_rows, key_rows, value_rows, gathered, diag = refs[-6:]
    me, prefix = scalars[0], scalars[2 + cell]
    length = span * seq_count
    tiles = length // TILE
    scale = 1.0 / math.sqrt(head_size)
    for r in range(seq_count):
        place = pl.ds(pl.multiple_of((me ^ r) * span, LANES), span)
        gathered[:, :, place] = arrays[places[r][0]][
            places[r][1], cell, first_head : first_head + heads
        ]
    key_rows[...] = turned_rows(qkv[heads])
    for tile in range(tiles):
        make_diagonal(diag, key_rows, tile, prefix)

    def one_head(h, carry):
        key_rows[...] = turned_rows(qkv[heads + h])
        value_rows[...] = turned_rows(qkv[2 * heads + h])
        held = gathered[h]
        centre = jnp.sum(
            held[:head_size].astype(jnp.float32) * out[first_head + h, :head_size],
            axis=0,
            keepdims=True,
        )
        gathered[h] = split_rows(held, -centre)
        log_sum = out[first_head + h, ONE_ROW : ONE_ROW + 1, :]
        qkv_q = split_rows(qkv[h], -log_sum / rate)
        query_rows[...] = jnp.zeros_like(query_rows)
        for j in range(tiles):
            down = slice(j * TILE, (j + 1) * TILE)
            keys, values = key_rows[down, :], value_rows[down, :]
            keys_column = qkv[heads + h, :, down]
            keys_back = jnp.zeros((TILE, HEAD_PAD), jnp.float32)
            values_back = jnp.zeros((TILE, HEAD_PAD), jnp.float32)
            for i in range(j, tiles):
                across = slice(i * TILE, (i + 1) * TILE)
                query = qkv_q[:, across]
                back_out = gathered[h, :, across]
                if i == j:
                    block = jnp.dot(without_mask(keys), query, preferred_element_type=jnp.float32)
                    block = block + diag[i]
                else:
                    block = jnp.dot(keys, query, preferred_element_type=jnp.float32)
                probs = jnp.exp2(block * rate)
                back_probs = jnp.dot(values, back_out, preferred_element_type=jnp.float32)
                back_scores = (probs * back_probs).astype(jnp.bfloat16)
                probs = probs.astype(jnp.bfloat16)
                turned = (((1,), (1,)), ((), ()))
                values_back += lax.dot_general(
                    probs, back_out, turned, preferred_element_type=jnp.float32
                )
                keys_back += lax.dot_general(
                    back_scores, query, turned, preferred_element_type=jnp.float32
                )
                query_rows[:, across] += jnp.dot(
                    keys_column, back_scores, preferred_element_type=jnp.float32
                )
            back[heads + h, down, :] = (keys_back * scale).astype(jnp.bfloat16)
            back[2 * heads + h, down, :] = values_back.astype(jnp.bfloat16)
        back[h] = (query_rows[...] * scale).T.astype(jnp.bfloat16)
        return carry

    lax.fori_loop(0, heads, one_head, 0)
    for block in range(seq_count):
        here = slice(block * span, (block + 1) * span)
        there = pl.ds(pl.multiple_of((me ^ block) * span, LANES), span)
        for first in range(0, 3 * heads, 2):
            pieces = [back[p, here, :] for p in range(first, min(first + 2, 3 * heads))]
            joined = pieces[0] if len(pieces) == 1 else jnp.concatenate(pieces, axis=1)
            left = first * HEAD_PAD
            result[there, left : left + joined.shape[1]] = joined

def attend_forward(scalars, cell, blocks, weight, bias, gain, shift, heads, head_size):
    seq_count, span = len(blocks), blocks[0].shape[1]
    length = seq_count * span
    rate = math.log2(math.e) / math.sqrt(head_size)
    flops = 2 * weight.size * length + 4 * heads * HEAD_PAD * length * length
    return no_grid_call(
        partial(forward_kernel, seq_count, cell, span, heads, head_size, rate),
        tuple(
            jax.ShapeDtypeStruct((3 * count, HEAD_PAD, length), jnp.bfloat16)
            for _, count, _ in head_groups(heads)
        )
        + (
            jax.ShapeDtypeStruct((heads, HEAD_PAD, length), jnp.float32),
            jax.ShapeDtypeStruct((blocks[0].shape[0], length), jnp.bfloat16),
        )
        + (jax.ShapeDtypeStruct((heads * head_size, span), jnp.bfloat16),) * seq_count,
        "attend_forward",
        flops,
        [scalars, *blocks, weight, bias, gain, shift],
        [
            pltpu.VMEM((heads, length, HEAD_PAD), jnp.bfloat16),
            pltpu.VMEM((length // TILE, TILE, TILE), jnp.float32),
            pltpu.VMEM((length, TILE), jnp.float32),
        ],
    )


def attend_backward(scalars, cell, qkv, out, arrays, places, first_head, head_size):
    seq_count, span = len(places), arrays[0].shape[-1]
    heads = qkv.shape[0] // 3
    length = seq_count * span
    rate = math.log2(math.e) / math.sqrt(head_size)
    return no_grid_call(
        partial(
            backward_kernel, seq_count, places, cell, span, first_head, heads, head_size, rate
        ),
        jax.ShapeDtypeStruct((length, 3 * heads * HEAD_PAD), jnp.bfloat16),
        "attend_backward",
        1,
        [scalars, qkv, out, *arrays],
        [
            pltpu.VMEM((3 * heads, length, HEAD_PAD), jnp.bfloat16),
            pltpu.VMEM((HEAD_PAD, length), jnp.float32),
            pltpu.VMEM((length, HEAD_PAD), jnp.bfloat16),
            pltpu.VMEM((length, HEAD_PAD), jnp.bfloat16),
            pltpu.VMEM((heads, HEAD_PAD, length), jnp.bfloat16),
            pltpu.VMEM((length // TILE, TILE, TILE), jnp.float32),
        ],
    )


def normed_back_kernel(seq_count, count, *refs):
    weights, backs = refs[:count], refs[count : 2 * count]
    tokens, results = refs[2 * count : 2 * count + seq_count], refs[2 * count + seq_count : -1]
    sums = refs[-1]
    width, span = results[0].shape
    totals = [0.0] * 2
    for r in range(seq_count):
        rows = slice(r * span, (r + 1) * span)
        back = sum(dot_turned(w[...], part[rows, :]) for w, part in zip(weights, backs))
        results[r][...] = back.astype(jnp.bfloat16)
        normal, _ = centred_columns(tokens[r][:width, :].astype(jnp.float32))
        for n, term in enumerate((back * normal, back)):
            totals[n] = totals[n] + jnp.sum(term, axis=1, keepdims=True)
    sums[...] = lines_of(totals)


def normed_back(weights, backs, tokens):
    seq_count = len(tokens)
    span = backs[0].shape[0] // seq_count
    width = weights[0].shape[0]
    shape = jax.ShapeDtypeStruct((width, span), jnp.bfloat16)
    return no_grid_call(
        partial(normed_back_kernel, seq_count, len(backs)),
        (shape,) * seq_count + (jax.ShapeDtypeStruct((8, width), jnp.float32),),
        "normed_back",
        1,
        [*weights, *backs, *tokens],
        [],
        scalars=0,
    )


def mix_outer_kernel(cell_count, share, cuts, count, scalars, *refs):
    normed, backs, (*results, sums, whole_sum) = refs[:count], refs[count : 2 * count], refs[2 * count :]
    features, width = whole_sum.shape
    sums[...] = sum(
        jnp.sum(back[...].astype(jnp.float32), axis=0, keepdims=True) for back in backs
    )
    for first, last in chunks(width):
        whole_sum[:, first:last] = sum(
            dot(left[:features, :], back[:, first:last]) for left, back in zip(normed, backs)
        )
    for k in range(cell_count):
        c = k ^ scalars[1]
        start = jnp.minimum(lax.div(c * share, 8) * 8, features - cuts[-1])
        block = whole_sum[pl.ds(pl.multiple_of(start, 8), cuts[-1]), :].astype(jnp.bfloat16)
        for n, bit in enumerate((1, 2)):
            target = results[2 * n + (0 if k & bit else 1)]
            target[without_bit(k, bit)] = block[cuts[n] : cuts[n + 1]]


def mix_outer(scalars, normed, backs, features, cell_count):
    _, height = row_cover(features, cell_count)
    cuts = (0, -(-height // 2 // 16) * 16, height)
    width = backs[0].shape[1]
    halves = [(cell_count // 2, cuts[n + 1] - cuts[n], width) for n in (0, 0, 1, 1)]
    return no_grid_call(
        partial(mix_outer_kernel, cell_count, features // cell_count, cuts, len(backs)),
        tuple(jax.ShapeDtypeStruct(shape, jnp.bfloat16) for shape in halves)
        + (jax.ShapeDtypeStruct((1, width), jnp.float32),),
        "mix_outer",
        1,
        [scalars, *normed, *backs],
        [pltpu.VMEM((features, width), jnp.float32)],
    )


def gathered_blocks(block, seq_count):
    held = {0: block}
    for bit in list(reversed(bits_of(seq_count))):
        held.update({r | bit: swap_with(x, "seq", bit) for r, x in list(held.items())})
    return [held[r] for r in range(seq_count)]


class PositionSum:
    def __init__(self, blocks):
        self.held = dict(enumerate(blocks))
        self.bits = bits_of(len(blocks))
        self.leave()

    def leave(self):
        bit = self.bits.pop(0)
        self.got = {r: swap_with(self.held[r | bit], "seq", bit) for r in self.held if not r & bit}

    def step(self, last):
        held, got = order_after((self.held, self.got), last)
        self.held = {r: add_low(held[r], x) for r, x in got.items()}
        self.leave()
        return self.held[0]

    def terms(self):
        return [self.held[0], self.got[0]]


class VectorSum:
    def __init__(self, blocks, seq_count):
        cells = [("cells", bit) for bit in reversed(bits_of(blocks.shape[0]))]
        self.order = cells + [("seq", bit) for bit in bits_of(seq_count)]
        self.leave(blocks)

    def leave(self, blocks):
        axis, bit = self.order.pop(0)
        half = blocks.shape[0] // 2 if axis == "cells" else 0
        self.keep = blocks[:half] if half else blocks
        self.got = swap_with(blocks[half:], axis, bit)

    def step(self, last):
        keep, got = order_after((self.keep, self.got), last)
        self.keep = keep + got
        if self.order:
            self.leave(self.keep)
        return self.keep


def add_low(left, right):
    return (left.astype(jnp.float32) + right.astype(jnp.float32)).astype(jnp.bfloat16)


def route_upper(upper):
    return swap_with(upper, "seq", upper.shape[0])


def route_rest(lower, got):
    seq_count = 2 * len(lower)
    arrays = [x[None] for x in lower] + [got]
    held = {r: (r, 0) for r in range(len(lower))}
    held.update({len(lower) + r: (len(lower), r) for r in range(len(lower))})
    for bit in list(reversed(bits_of(seq_count)))[1:]:
        away = [r for r in held if r & bit]
        arrays.append(swap_with(jnp.stack([arrays[held[r][0]][held[r][1]] for r in away]), "seq", bit))
        held.update({r: (len(arrays) - 1, n) for n, r in enumerate(away)})
    return arrays, [held[r] for r in range(seq_count)]


def exchanged_blocks(blocks):
    return [blocks[0]] + [swap_with(blocks[r], "seq", r) for r in range(1, len(blocks))]


def chunks(width):
    return [(first, min(first + TILE, width)) for first in range(0, width, TILE)]


def dot(left, right):
    return jnp.dot(left, right, preferred_element_type=jnp.float32)


def dot_turned(left, right):
    return lax.dot_general(
        left, right, (((1,), (1,)), ((), ())), preferred_element_type=jnp.float32
    )


def centred_columns(values):
    centred = values - jnp.mean(values, axis=0, keepdims=True)
    spread = jnp.mean(centred * centred, axis=0, keepdims=True)
    rise = lax.rsqrt(spread + 1e-05)
    return centred * rise, rise


def norm_pull(normal, rise, back, gain):
    scaled = back * gain
    inner = scaled - jnp.mean(scaled, axis=0, keepdims=True)
    inner = inner - normal * jnp.mean(scaled * normal, axis=0, keepdims=True)
    return rise * inner


def columns_of(*vectors):
    rows = [vector[...].reshape(1, -1) for vector in vectors]
    rows += [jnp.zeros_like(rows[0])] * (8 - len(rows))
    turned = jnp.concatenate(rows, axis=0).T
    return [turned[:, n : n + 1] for n in range(len(vectors))]


def lines_of(columns):
    rows = columns[0].shape[0]
    room = [jnp.zeros((rows, 8 - len(columns)), jnp.float32)] if len(columns) < 8 else []
    return jnp.concatenate(list(columns) + room, axis=1).T


def widen_kernel(cell, cells, scalars, tokens, key_mask, result):
    width, span = tokens.shape[1:]
    place = lax.broadcasted_iota(jnp.int32, (1, span), 1) + scalars[0] * span
    result[:width, :] = tokens[0]
    seen = (key_mask[cell : cell + 1, :] == 1) & (place < scalars[2 + cells + cell])
    shape = (result.shape[0] - width, span)
    mark = lax.broadcasted_iota(jnp.int32, shape, 0) == 0
    hidden = jnp.where(seen, 0.0, MASKED)
    result[width:, :] = jnp.where(mark, hidden, 0.0).astype(jnp.bfloat16)


def widen(scalars, cell, tokens, key_mask, features):
    cells, width, span = tokens.shape
    return grid_call(
        partial(widen_kernel, cell, cells),
        (1,),
        [pl.BlockSpec((1, width, span), lambda g, me: (cell, 0, 0)), whole(key_mask)],
        pl.BlockSpec((features, span), lambda g, me: (0, 0)),
        jax.ShapeDtypeStruct((features, span), jnp.bfloat16),
        [],
        "widen",
        1,
        (scalars, tokens, key_mask),
        1,
    )


def second_norm_kernel(seq_count, scalars, weight, tokens, gain, shift, bias, *refs):
    parts = refs[:seq_count]
    middle, second, second_turned, attended, gather = refs[seq_count:]
    share = parts[0].shape[0]
    gain, shift, bias = columns_of(gain, shift, bias)
    for r in range(seq_count):
        place = pl.ds(pl.multiple_of((scalars[0] ^ r) * share, 8), share)
        gather[place, :] = parts[r][...].astype(jnp.float32)
    attended[...] = gather[: attended.shape[0], :].astype(jnp.bfloat16)
    total = dot(weight[...].T, attended[...])
    total = tokens[...].astype(jnp.float32) + (total + bias)
    middle[...] = total
    normal, _ = centred_columns(total)
    normed = (normal * gain + shift).astype(jnp.bfloat16)
    second_turned[...] = normed
    second[...] = normed.T


def second_norm(scalars, weight, tokens, vectors, parts):
    width, span = tokens.shape
    seq_count = len(parts)
    return no_grid_call(
        partial(second_norm_kernel, seq_count),
        (
            jax.ShapeDtypeStruct((width, span), jnp.float32),
            jax.ShapeDtypeStruct((span, width), jnp.bfloat16),
            jax.ShapeDtypeStruct((width, span), jnp.bfloat16),
            jax.ShapeDtypeStruct((width, span), jnp.bfloat16),
        ),
        "second_norm",
        2 * span * width * width,
        [scalars, weight, tokens, *vectors, *parts],
        [pltpu.VMEM((seq_count * parts[0].shape[0], span), jnp.float32)],
    )


def weights_kernel(seq_count, heads, head_size, scalars, mix, query, value, weight, bias, *turned):
    width = mix.shape[0]
    here = heads * head_size
    groups = head_groups(heads)
    weight[...] = jnp.zeros_like(weight)
    vectors = columns_of(query, value)
    row = lax.broadcasted_iota(jnp.int32, (HEAD_PAD, 1), 0)
    for _, count, base in groups:
        for p, least in ((0, (ONE_ROW, ONE_ROW + 1)), (1, (SPLIT_ROW, HEAD_PAD)), (2, (ONE_ROW, HEAD_PAD))):
            fill = jnp.where((row >= least[0]) & (row < least[1]), 1.0, 0.0)
            for n in range(count):
                place = (base + p * count + n) * HEAD_PAD
                bias[place : place + HEAD_PAD, :] = fill
    for s in range(seq_count):

        @pl.when(scalars[0] == s)
        def _():
            for p in range(3):
                first = s * here
                last = min(first + here, width)
                if last <= first:
                    continue
                start = (p * width + first) // LANES * LANES
                stop = min(-(-(p * width + last) // LANES) * LANES, mix.shape[1])
                block = mix[:, start:stop].astype(jnp.float32)
                block = block[:, p * width + first - start : p * width + last - start].T
                for group_first, count, base in groups:
                    for n in range(count):
                        h = group_first + n
                        if (h + 1) * head_size > last - first:
                            continue
                        place = (base + p * count + n) * HEAD_PAD
                        piece = block[h * head_size : (h + 1) * head_size]
                        room = jnp.zeros((HEAD_PAD - head_size, width), jnp.float32)
                        piece = jnp.concatenate([piece, room])
                        weight[place : place + HEAD_PAD, :width] = piece.astype(jnp.bfloat16)
                        if p != 1:
                            own = vectors[p // 2][first + h * head_size : first + (h + 1) * head_size]
                            bias[place : place + head_size, :] = own

    room = weight.shape[1] - width
    for (_, count, base), columns in zip(groups, turned):
        rows = slice(base * HEAD_PAD, (base + 3 * count) * HEAD_PAD)
        columns[...] = weight[rows, :width].T
        rows = slice((base + count) * HEAD_PAD, (base + 2 * count) * HEAD_PAD)
        row = lax.broadcasted_iota(jnp.int32, (count * HEAD_PAD, room), 0)
        lane = lax.broadcasted_iota(jnp.int32, (count * HEAD_PAD, room), 1)
        mark = (lane == 0) & (lax.rem(row, HEAD_PAD) == ONE_ROW)
        weight[rows, width:] = jnp.where(mark, 1.0, 0.0).astype(jnp.bfloat16)


def own_weights(scalars, mix, query, value, features, seq_count, heads, head_size):
    width = mix.shape[0]
    return no_grid_call(
        partial(weights_kernel, seq_count, heads, head_size),
        (
            jax.ShapeDtypeStruct((3 * heads * HEAD_PAD, features), jnp.bfloat16),
            jax.ShapeDtypeStruct((3 * heads * HEAD_PAD, 1), jnp.float32),
        )
        + tuple(
            jax.ShapeDtypeStruct((width, 3 * count * HEAD_PAD), jnp.bfloat16)
            for _, count, _ in head_groups(heads)
        ),
        "own_weights",
        1,
        [scalars, mix, query, value],
        [],
    )


def active_back_kernel(cotangent, down, result, rows):
    @pl.when(pl.program_id(0) == 0)
    def _():
        cells, _, span = cotangent.shape
        for c in range(cells):
            rows[c * span : (c + 1) * span, :] = cotangent[c].T

    for first, last in chunks(down.shape[1]):
        result[:, first:last] = dot(rows[...], down[:, first:last])


def active_back(scalars, cotangent, down):
    cells, width, span = cotangent.shape
    rows = cells * span
    tile = hidden_tile(down.shape[1])
    shape = jax.ShapeDtypeStruct((rows, down.shape[1]), jnp.float32)
    return grid_call(
        lambda me, *refs: active_back_kernel(*refs),
        (down.shape[1] // tile,),
        [whole(cotangent), pl.BlockSpec((width, tile), lambda g, me: (0, g))],
        pl.BlockSpec((rows, tile), lambda g, me: (0, g)),
        shape,
        [pltpu.VMEM((rows, width), jnp.bfloat16)],
        "active_back",
        1,
        (scalars, cotangent, down),
        1,
    )


def hidden_kernel(back_active, up, up_bias, *refs):
    *parts, active, back_upper, bias_back, second = refs

    @pl.when(pl.program_id(0) == 0)
    def _():
        for c, part in enumerate(parts):
            second[c * part.shape[0] : (c + 1) * part.shape[0], :] = part[...]

    inner = math.sqrt(2.0 / math.pi)
    for first, last in chunks(up.shape[1]):
        upper = dot(second[...], up[:, first:last]) + up_bias[:, first:last]
        back = back_active[:, first:last]
        square = upper * upper
        bend = jnp.tanh(inner * upper * (1.0 + 0.044715 * square))
        half = 0.5 + 0.5 * bend
        slope = half + 2.0 * half * (1.0 - half) * (inner * upper) * (1.0 + 0.134145 * square)
        active[:, first:last] = (upper * half).astype(jnp.bfloat16)
        back = (back * slope).astype(jnp.bfloat16)
        back_upper[:, first:last] = back
        bias_back[:, first:last] = jnp.sum(back.astype(jnp.float32), axis=0, keepdims=True)


def grid_call(
    body, grid, in_specs, out_specs, out_shape, scratch, name, flops, inputs, moved, aliases=None
):
    return pl.pallas_call(
        body,
        out_shape=out_shape,
        grid_spec=pltpu.PrefetchScalarGridSpec(
            num_scalar_prefetch=1,
            grid=grid,
            in_specs=in_specs,
            out_specs=out_specs,
            scratch_shapes=scratch,
        ),
        compiler_params=pltpu.CompilerParams(vmem_limit_bytes=VMEM_LIMIT),
        cost_estimate=cost(name),
        input_output_aliases=aliases or {},
        name=name,
    )(*inputs)


def whole(array):
    zeros = (0,) * array.ndim
    return pl.BlockSpec(array.shape, lambda g, me: zeros)


def hidden_tile(hidden):
    return max(t for t in range(LANES, 1024, LANES) if hidden % t == 0)


def hidden_layer(scalars, second, back_active, up, up_bias):
    rows = sum(part.shape[0] for part in second)
    width = up.shape[0]
    hidden = up.shape[1]
    tile = hidden_tile(hidden)
    weight = pl.BlockSpec((width, tile), lambda g, me: (0, g))
    out = pl.BlockSpec((rows, tile), lambda g, me: (0, g))
    line = pl.BlockSpec((1, tile), lambda g, me: (0, g))
    return grid_call(
        lambda me, *refs: hidden_kernel(*refs),
        (hidden // tile,),
        [out, weight, line] + [whole(part) for part in second],
        [out, out, line],
        (
            jax.ShapeDtypeStruct((rows, hidden), jnp.bfloat16),
            jax.ShapeDtypeStruct((rows, hidden), jnp.bfloat16),
            jax.ShapeDtypeStruct((1, hidden), jnp.float32),
        ),
        [pltpu.VMEM((rows, width), jnp.bfloat16)],
        "hidden_layer",
        4 * rows * up.size,
        (scalars, back_active, up, up_bias, *second),
        4 * up.size + 4 * rows * hidden,
    )


def middle_back_kernel(
    seq_count,
    cells,
    scalars,
    back_upper,
    up,
    gain,
    cotangent,
    weight,
    *refs,
):
    middle, (back_middle, back_branch, sums) = refs[:cells], refs[cells : cells + 3]
    *parts, total, back_heads = refs[cells + 3 :]
    half = seq_count // 2
    step = pl.program_id(0)

    @pl.when(step == 0)
    def _():
        total[...] = jnp.zeros_like(total)

    for first, last in chunks(total.shape[1]):
        total[:, first:last] += dot_turned(up[...], back_upper[first:last, :])

    @pl.when(step == pl.num_programs(0) - 1)
    def _():
        span = cotangent.shape[2]
        heads = parts[0].shape[1]
        head_size = back_heads.shape[0] // (seq_count * heads)
        (gain_column,) = columns_of(gain)
        totals = [0.0] * 4
        for c in range(cells):
            here = slice(c * span, (c + 1) * span)
            normal, rise = centred_columns(middle[c][...])
            back = total[:, here]
            back_out = cotangent[c].astype(jnp.float32)
            back_mid = back_out + norm_pull(normal, rise, back, gain_column)
            back_middle[:, here] = back_mid
            branch = back_mid.astype(jnp.bfloat16)
            back_branch[:, here] = branch
            for n, term in enumerate((back * normal, back, branch.astype(jnp.float32), back_out)):
                totals[n] = totals[n] + jnp.sum(term, axis=1, keepdims=True)
            back_heads[: weight.shape[0], :] = dot(weight[...], branch)
            if back_heads.shape[0] > weight.shape[0]:
                rest = back_heads.shape[0] - weight.shape[0]
                back_heads[weight.shape[0] :, :] = jnp.zeros((rest, span), jnp.float32)
            for r in range(seq_count):
                first = (scalars[0] ^ r) * heads * head_size
                part = back_heads[pl.ds(pl.multiple_of(first, 8), heads * head_size), :]
                room = jnp.zeros((heads, HEAD_PAD - head_size, span), jnp.float32)
                part = jnp.concatenate([part.reshape(heads, head_size, span), room], axis=1)
                target = parts[r].at[c] if r < half else parts[half].at[r - half, c]
                target[...] = part.astype(jnp.bfloat16)
        sums[...] = lines_of(totals)


def middle_back(scalars, back_upper, up, middle, gain, cotangent, weight, seq_count, heads):
    rows, hidden = back_upper.shape
    cells, width, span = cotangent.shape
    head_size = width // HEADS
    tile = hidden_tile(hidden)
    outs = [
        jax.ShapeDtypeStruct((width, rows), jnp.float32),
        jax.ShapeDtypeStruct((width, rows), jnp.bfloat16),
        jax.ShapeDtypeStruct((8, width), jnp.float32),
    ]
    block = (cells, heads, HEAD_PAD, span)
    outs += [jax.ShapeDtypeStruct(block, jnp.bfloat16)] * (seq_count // 2)
    outs += [jax.ShapeDtypeStruct((seq_count // 2,) + block, jnp.bfloat16)]
    return grid_call(
        partial(middle_back_kernel, seq_count, cells),
        (hidden // tile,),
        [
            pl.BlockSpec((rows, tile), lambda g, me: (0, g)),
            pl.BlockSpec((width, tile), lambda g, me: (0, g)),
            whole(gain),
            whole(cotangent),
            whole(weight),
        ]
        + [whole(m) for m in middle],
        [whole(o) for o in outs],
        outs,
        [
            pltpu.VMEM((width, rows), jnp.float32),
            pltpu.VMEM((seq_count * heads * head_size, span), jnp.float32),
        ],
        "middle_back",
        2 * rows * up.size + 2 * rows * width * width,
        (scalars, back_upper, up, gain, cotangent, weight, *middle),
        1,
    )


def block_out_kernel(active, down, bias, *refs):
    *middle, result, total = refs
    step = pl.program_id(0)

    @pl.when(step == 0)
    def _():
        (bias_column,) = columns_of(bias)
        for c, part in enumerate(middle):
            span = part.shape[1]
            total[:, c * span : (c + 1) * span] = part[...] + bias_column

    for first, last in chunks(total.shape[1]):
        total[:, first:last] += dot_turned(down[...], active[first:last, :])

    @pl.when(step == pl.num_programs(0) - 1)
    def _():
        cells, _, span = result.shape
        for c in range(cells):
            result[c] = total[:, c * span : (c + 1) * span].astype(jnp.bfloat16)


def block_output(scalars, active, down, middle, bias):
    rows, hidden = active.shape
    cells, width = len(middle), middle[0].shape[0]
    tile = hidden_tile(hidden)
    out = jax.ShapeDtypeStruct((cells, width, rows // cells), jnp.bfloat16)
    return grid_call(
        lambda me, *refs: block_out_kernel(*refs),
        (hidden // tile,),
        [
            pl.BlockSpec((rows, tile), lambda g, me: (0, g)),
            pl.BlockSpec((width, tile), lambda g, me: (0, g)),
            whole(bias),
        ]
        + [whole(m) for m in middle],
        whole(out),
        out,
        [pltpu.VMEM((width, rows), jnp.float32)],
        "block_output",
        2 * rows * down.size,
        (scalars, active, down, bias, *middle),
        1,
    )


def take_columns(piece, right, count, which):
    width = piece.shape[1]
    for s in range(count):

        @pl.when(which == s)
        def _():
            first = s * width // LANES * LANES
            last = min(-(-(s + 1) * width // LANES) * LANES, right.shape[1])
            block = right[:, first:last]
            piece[...] = block[:, s * width - first : (s + 1) * width - first]


def up_outer_kernel(seq_count, cells, share, cut, zbit, split, scalars, right, *refs):
    left, rest = refs[:cells], refs[cells:]
    got = rest[0] if split else None
    *results, total, piece, joined = rest[3 if split else 0 :]
    rows = left[0].shape[0]
    core = 0 if split else 1

    @pl.when(pl.program_id(0) == 0)
    def _():
        for c, part in enumerate(left):
            joined[:, c * part.shape[1] : (c + 1) * part.shape[1]] = part[...]

    take_columns(piece, right, seq_count, (2 * pl.program_id(0) + core) ^ scalars[0])
    for first, last in chunks(piece.shape[1]):
        total[:, first:last] = dot(joined[...], piece[:, first:last])
    cell_count = results[0].shape[1] * (2 if split else 1)
    height = results[0].shape[2] if not split else got.shape[2]
    for k in range(cell_count):
        c = k ^ scalars[1]
        start = jnp.minimum(lax.div(c * share, 8) * 8, rows - height)
        block = total[pl.ds(pl.multiple_of(start, 8), height), :]
        if split:
            block = block + got[0, k].astype(jnp.float32)
            for n, (bit, part) in enumerate(((1, block[:cut]), (zbit, block[cut:]))):
                target = results[2 * n + (0 if k & bit else 1)]
                target[0, without_bit(k, bit)] = part.astype(jnp.bfloat16)
        else:
            results[0][0, k] = block.astype(jnp.bfloat16)


def up_outer(scalars, left, right, seq_count, cell_count, got=None, lower=None):
    tokens, width = right.shape[0], right.shape[1] // seq_count
    rows = left[0].shape[0]
    _, height = row_cover(rows, cell_count)
    half = seq_count // 2
    split = got is not None
    cut = two_thirds(height)
    in_specs = [whole(right)] + [whole(part) for part in left]
    inputs = [scalars, right, *left]
    aliases = {}
    if split:
        in_specs.append(pl.BlockSpec((1,) + got.shape[1:], lambda g, me: (g, 0, 0, 0)))
        in_specs += [pl.BlockSpec(memory_space=pl.ANY)] * 2
        inputs += [got, *lower]
        aliases = {len(inputs) - 2: 2, len(inputs) - 1: 3}
        outs = [(half, cell_count // 2, cut, width)] * 2 + [lower[0].shape] * 2
        low = height - cut
        blocks = [pl.BlockSpec((1,) + outs[0][1:], lambda g, me: (g, 0, 0, 0))] * 2
        blocks += [
            pl.BlockSpec((1, cell_count // 2, low, width), lambda g, me: (g, 0, 1, 0))
        ] * 2
    else:
        outs = [(half, cell_count, height, width)]
        blocks = [pl.BlockSpec((1,) + outs[0][1:], lambda g, me: (g, 0, 0, 0))]
    return grid_call(
        partial(
            up_outer_kernel,
            seq_count,
            len(left),
            rows // cell_count,
            cut,
            cell_count // seq_count,
            split,
        ),
        (half,),
        in_specs,
        blocks,
        [jax.ShapeDtypeStruct(out, jnp.bfloat16) for out in outs],
        [
            pltpu.VMEM((rows, width), jnp.float32),
            pltpu.VMEM((tokens, width), jnp.bfloat16),
            pltpu.VMEM((rows, tokens), jnp.bfloat16),
        ],
        "up_outer",
        1,
        inputs,
        1,
        aliases,
    )


def two_thirds(height):
    return -(-height * 2 // 3 // 16) * 16


def down_outer_kernel(seq_count, inner, cut, split, scalars, left, right, *refs):
    got = refs[0] if split else None
    *results, total, piece, wide, own = refs[1 if split else 0 :]
    half = seq_count // 2
    share = own.shape[0] // half
    span = left.shape[2]
    width = piece.shape[1] // inner
    low = scalars[1] & (inner - 1)
    step = pl.program_id(0)
    core = 0 if split else 1
    starts, height = row_cover(share, inner)

    @pl.when(step == 0)
    def _():
        for c in range(left.shape[0]):
            wide[:, c * span : (c + 1) * span] = left[c].astype(jnp.float32)
        for x in range(half):
            for s in range(seq_count):

                @pl.when(((2 * x + core) ^ scalars[0]) == s)
                def _():
                    own[x * share : (x + 1) * share, :] = wide[s * share : (s + 1) * share, :]

    take_columns(piece, right, seq_count, step ^ lax.div(scalars[1], inner))
    for first, last in chunks(piece.shape[1]):
        total[:, first:last] = dot(own[...].astype(jnp.bfloat16), piece[:, first:last])
    for q in range(inner):
        for x in range(half):
            block = total[x * share : (x + 1) * share, q * width : (q + 1) * width]
            block = jnp.concatenate([block[s : s + height] for s in starts], axis=1)
            if split:
                block = block + got[x, q ^ low].astype(jnp.float32)
                away = 2 * x >= half
                target = results[0 if away else 1]
                target[x % (half // 2), q ^ low] = block[:cut].astype(jnp.bfloat16)
                rest = block[cut:].astype(jnp.bfloat16)

                @pl.when(step & 1 == 1)
                def _():
                    results[2][x, q ^ low] = rest

                @pl.when(step & 1 == 0)
                def _():
                    results[3][x, q ^ low] = rest

            else:
                results[0][x, q ^ low] = block.astype(jnp.bfloat16)


def down_outer(scalars, left, right, seq_count, cell_count, got=None):
    tokens, width = right.shape[0], right.shape[1] // seq_count
    half = seq_count // 2
    inner = cell_count // seq_count
    share = left.shape[1] // seq_count
    split = got is not None
    _, height = row_cover(share, inner)
    cut = two_thirds(height)
    in_specs = [whole(left), whole(right)]
    inputs = [scalars, left, right]
    if split:
        in_specs.append(pl.BlockSpec((half, inner) + got.shape[2:], lambda g, me: (0, g, 0, 0)))
        inputs.append(got)
        low = height - cut
        outs = [(half // 2, cell_count, cut, width)] * 2
        outs += [(half, cell_count // 2, 2 * low, width)] * 2
        blocks = [pl.BlockSpec((half // 2, inner, cut, width), lambda g, me: (0, g, 0, 0))] * 2
        blocks += [pl.BlockSpec((half, inner, low, width), lambda g, me: (0, g // 2, 0, 0))] * 2
    else:
        outs = [(half, cell_count, height, width)]
        blocks = [pl.BlockSpec((half, inner, height, width), lambda g, me: (0, g, 0, 0))]
    return grid_call(
        partial(down_outer_kernel, seq_count, inner, cut, split),
        (seq_count,),
        in_specs,
        blocks,
        [jax.ShapeDtypeStruct(out, jnp.bfloat16) for out in outs],
        [
            pltpu.VMEM((half * share, width), jnp.float32),
            pltpu.VMEM((tokens, width), jnp.bfloat16),
            pltpu.VMEM((left.shape[1], tokens), jnp.float32),
            pltpu.VMEM((half * share, tokens), jnp.float32),
        ],
        "down_outer",
        1,
        inputs,
        1,
    )


def out_outer_kernel(seq_count, cells, share, scalars, right, *refs):
    left, (result, total, joined) = refs[:cells], refs[cells:]
    for c, part in enumerate(left):
        joined[:, c * part.shape[1] : (c + 1) * part.shape[1]] = part[...]
    rows = total.shape[0]
    for first, last in chunks(total.shape[1]):
        total[:, first:last] = dot_turned(joined[...], right[first:last, :])
    width = total.shape[1] // seq_count
    _, cell_count, part, room = result.shape
    groups = room // width
    for k in range(cell_count):
        c = k ^ scalars[1]
        start = jnp.minimum(lax.div(c * share, 8) * 8, rows - groups * part)
        block = total[pl.ds(pl.multiple_of(start, 8), groups * part), :]
        for s in range(seq_count):
            piece = block[:, s * width : (s + 1) * width]
            pieces = [piece[i * part : (i + 1) * part] for i in range(groups)]
            pieces.append(jnp.zeros((part, room - groups * width), jnp.float32))
            place = s ^ scalars[0]
            place = (place & 1) * (seq_count // 2) + (place >> 1)
            result[place, k] = jnp.concatenate(pieces, axis=1).astype(jnp.bfloat16)


def out_outer(scalars, left, right, room, seq_count, cell_count):
    rows, tokens = right.shape
    groups = room * seq_count // rows
    _, height = row_cover(rows, cell_count, 16 * groups)
    shape = (seq_count, cell_count, height // groups, room)
    return no_grid_call(
        partial(out_outer_kernel, seq_count, len(left), rows // cell_count),
        jax.ShapeDtypeStruct(shape, jnp.bfloat16),
        "out_outer",
        1,
        [scalars, right, *left],
        [pltpu.VMEM((rows, rows), jnp.float32), pltpu.VMEM((rows, tokens), jnp.bfloat16)],
    )


def vector_kernel(cells, heads, head_size, seq_count, scalars, middle, hidden, *refs):
    first, sums, (result, own) = refs[:cells], refs[cells:-2], refs[-2:]
    own[...] = jnp.zeros_like(own)
    width = middle.shape[1]
    for s in range(seq_count):

        @pl.when(scalars[0] == s)
        def _():
            for (start, count, _), part in zip(head_groups(heads), sums):
                for n in range(count):
                    at = ((s * heads) + start + n) * head_size
                    if at >= width:
                        continue
                    for row, p in enumerate((0, 2)):
                        source = (p * count + n) * HEAD_PAD
                        own[row : row + 1, at : at + head_size] = part[
                            :, source : source + head_size
                        ]

    total = sum(part[0:2, :] for part in first)
    lines = [total[0:1], total[1:2], own[0:1, :], own[1:2, :]]
    lines += [middle[n : n + 1, :] for n in (2, 0, 1, 3)]
    count, rows, share = result.shape
    for c in range(count):
        place = c ^ scalars[1]
        for n, line in enumerate(lines):
            result[place, n : n + 1, :] = line[:, c * share : (c + 1) * share]
        for n in range(rows - 8):
            at = (c * (rows - 8) + n) * share
            result[place, 8 + n : 9 + n, :] = hidden[:, at : at + share]


def vector_blocks(
    scalars, first, sums, middle, hidden, heads, head_size, seq_count, cell_count
):
    share = middle.shape[1] // cell_count
    rows = 8 + hidden.shape[1] // middle.shape[1]
    return no_grid_call(
        partial(vector_kernel, len(first), heads, head_size, seq_count),
        jax.ShapeDtypeStruct((cell_count, rows, share), jnp.float32),
        "vector_blocks",
        1,
        [scalars, middle, hidden, *first, *sums],
        [pltpu.VMEM((8, middle.shape[1]), jnp.float32)],
    )


def mix_columns_kernel(heads, head_size, scalars, *refs):
    *blocks, result = refs
    places = {}
    for first, count, base in head_groups(heads):
        places.update({(p, first + n): base + p * count + n for p in range(3) for n in range(count)})
    seq_count = len(blocks)
    share = result.shape[1]
    width = HEADS * head_size
    for mine in range(seq_count):

        @pl.when(scalars[0] == mine)
        def _():
            for p in range(3):
                for head in range(HEADS):
                    first = p * width + head * head_size - mine * share
                    cut_left, cut_right = max(0, -first), min(head_size, share - first)
                    if cut_left >= cut_right:
                        continue
                    block = blocks[(head // heads) ^ mine]
                    source = places[p, head % heads] * HEAD_PAD
                    base = source // LANES * LANES
                    piece = block[:, base : min(base + LANES, block.shape[1])].astype(jnp.float32)
                    source -= base
                    result[:, first + cut_left : first + cut_right] = piece[
                        :, source + cut_left : source + cut_right
                    ]


def mix_columns(scalars, blocks, heads, head_size):
    rows = blocks[0].shape[0]
    return no_grid_call(
        partial(mix_columns_kernel, heads, head_size),
        jax.ShapeDtypeStruct((rows, 3 * HEADS * head_size // len(blocks)), jnp.float32),
        "mix_columns",
        1,
        [scalars, *blocks],
        [],
    )


def tokens_back_kernel(tokens, gain, back_middle, *refs):
    *terms, result = refs
    cells, _, span = tokens.shape
    (gain,) = columns_of(gain)
    for c in range(cells):
        normal, rise = centred_columns(tokens[c].astype(jnp.float32))
        back = terms[2 * c][...].astype(jnp.float32) + terms[2 * c + 1][...].astype(jnp.float32)
        back_in = back_middle[:, c * span : (c + 1) * span]
        back_in = back_in + norm_pull(normal, rise, back, gain)
        result[c] = back_in.astype(jnp.bfloat16)


def tokens_back(tokens, gain, back_middle, terms):
    return no_grid_call(
        tokens_back_kernel,
        jax.ShapeDtypeStruct(tokens.shape, jnp.bfloat16),
        "tokens_back",
        1,
        [tokens, gain, back_middle, *terms],
        [],
        scalars=0,
    )


def order_after(values, *earlier):
    values, _ = lax.optimization_barrier((values, earlier))
    return values


def advance(parts, last):
    groups = {}
    running = [part for part in parts if part.order]
    arrived = [part.got for part in running]
    for part in running:
        part.got = order_after(part.got, arrived)
        key = (part.kind, tuple(part.names), tuple(part.order), part.keep.shape[2])
        groups.setdefault(key, []).append(part)
    for first, *others in groups.values():
        last = first.step(last, *others)
    return last


def on_device(
    tokens,
    first_gain,
    first_shift,
    mix_weight,
    query_bias,
    value_bias,
    out_weight,
    out_bias,
    second_gain,
    second_shift,
    up_weight,
    up_bias,
    down_weight,
    down_bias,
    cotangent,
    prefix_lengths,
    gene_counts,
    key_mask,
):
    cells_here, span, width = tokens.shape
    head_size = width // HEADS
    length = span * lax.axis_size("seq")
    start = lax.axis_index("seq") * span
    seq_count, cell_count = lax.axis_size("seq"), lax.axis_size("cells")
    me = jnp.stack([lax.axis_index("seq"), lax.axis_index("cells")]).astype(jnp.int32)
    totals = prefix_lengths + gene_counts
    row_count = cells_here * span
    own_rows = start + jnp.arange(span)
    heads_here = -(-HEADS // seq_count)
    head_total = heads_here * seq_count
    features = -(-(width + 1) // LANES) * LANES
    scalars = jnp.concatenate([me, prefix_lengths, totals])

    def flat(array):
        return array.reshape(row_count, array.shape[-1])

    groups = head_groups(heads_here)
    tokens_turned = tokens.transpose(0, 2, 1)
    cotangent_turned = cotangent.transpose(0, 2, 1)
    down_turned = down_weight.T
    wide = []
    for c in range(cells_here):
        wide.append(widen(order_after(scalars, wide), c, tokens_turned, key_mask, features))
    weight, bias, *weights_turned = own_weights(
        order_after(scalars, wide),
        mix_weight,
        query_bias,
        value_bias,
        features,
        seq_count,
        heads_here,
        head_size,
    )
    x_bits = [b for b in reversed(bits_of(seq_count)) if b > 1]
    near = [swap_with(block, "seq", 1) for block in wide]
    back_active = active_back(scalars, order_after(cotangent_turned, weight), down_turned)
    held = [{0: wide[c]} for c in range(cells_here)]
    for c in range(cells_here):
        for bit in x_bits:
            for r, block in list(held[c].items()):
                after = (held[c - 1][x_bits[0]], back_active) if c > 0 else ()
                held[c][r | bit] = swap_with(order_after(block, *after), "seq", bit)

    attended, kept = [], []
    last = (back_active,)
    blocks, normed = [], []
    for c in range(cells_here):
        after = last
        for r, block in list(held[c].items()):
            held[c][r | 1] = near[c] if r == 0 else swap_with(order_after(block, *after), "seq", 1)
        blocks.append([held[c][r] for r in range(seq_count)])
        results = attend_forward(
            scalars,
            c,
            order_after(blocks[c], *last),
            weight,
            bias,
            first_gain,
            first_shift,
            heads_here,
            head_size,
        )
        qkv, (out, normed_cell, *parts) = results[: len(groups)], results[len(groups) :]
        last = (out,)
        kept.append((qkv, out))
        normed.append(normed_cell)
        attended.append(exchanged_blocks(parts))
    middle, second, second_turned, attended_turned = [], [], [], []
    for c in range(cells_here):
        results = second_norm(
            scalars,
            out_weight,
            tokens_turned[c],
            (second_gain, second_shift, out_bias),
            order_after(attended[c], *last),
        )
        last = (results[0],)
        for held, result in zip((middle, second, second_turned, attended_turned), results):
            held.append(result)
    active, back_upper, up_bias_back = hidden_layer(
        scalars, second, back_active, up_weight, up_bias.reshape(1, -1)
    )
    (down_send,) = down_outer(scalars, cotangent_turned, active, seq_count, cell_count)
    down_got = swap_with(down_send, "seq", 1)
    (up_send,) = up_outer(
        scalars, second_turned, order_after(back_upper, down_send), seq_count, cell_count
    )
    up_got = swap_with(up_send, "seq", 1)
    *down_halves, lower_send, lower_keep = down_outer(
        scalars, cotangent_turned, order_after(active, up_send), seq_count, cell_count, down_got
    )
    *up_halves, lower_send, lower_keep = up_outer(
        scalars,
        second_turned,
        order_after(back_upper, down_halves),
        seq_count,
        cell_count,
        up_got,
        (lower_send, lower_keep),
    )

    def flat_blocks(array):
        return array.reshape((-1,) + array.shape[-2:])

    x_bits = [("seq", b) for b in reversed(bits_of(seq_count)) if b > 1]
    cell_bits = [("cells", b) for b in reversed(bits_of(cell_count))]
    names = x_bits + cell_bits
    y_bit, z_bit = ("cells", 1), ("cells", cell_count // seq_count)
    rest = [n for n in reversed(cell_bits) if n not in (y_bit, z_bit)]
    running = [
        Reduction("down", names, x_bits + [y_bit, z_bit] + rest, *map(flat_blocks, down_halves)),
        Reduction("up", names, [y_bit, z_bit] + x_bits + rest, *map(flat_blocks, up_halves)),
        Reduction(
            "both",
            names,
            [z_bit] + x_bits + [y_bit] + rest,
            flat_blocks(lower_send),
            flat_blocks(lower_keep),
        ),
    ]
    back_middle, back_branch, middle_sums, *back_heads = middle_back(
        scalars,
        order_after(back_upper, up_halves),
        up_weight,
        middle,
        second_gain,
        cotangent_turned,
        out_weight,
        seq_count,
        heads_here,
    )
    back_upper_half = route_upper(back_heads[-1])
    down_part, up_part, both_part = running
    out_shares = out_outer(
        scalars,
        attended_turned,
        order_after(back_branch, back_heads),
        3 * groups[0][1] * HEAD_PAD,
        seq_count,
        cell_count,
    )
    out_part = Reduction(
        "out",
        [("seq", 1)] + names,
        [("seq", 1)] + x_bits + [y_bit, z_bit] + rest,
        flat_blocks(out_shares[seq_count // 2 :]),
        flat_blocks(out_shares[: seq_count // 2]),
    )
    block_out = block_output(
        scalars, order_after(active, out_shares), down_turned, middle, down_bias
    )
    last = down_part.step(block_out)
    back_arrays, back_places = route_rest(
        back_heads[:-1], order_after(back_upper_half, last)
    )
    last = advance([up_part, both_part], last)
    mixed_back, mix_parts = [[], []], []
    back_normed, bias_backs, first_sums = [], [], []

    def mix_reductions(group, last):
        *halves, sums = mix_outer(
            scalars,
            normed,
            order_after(mixed_back[group], last),
            width,
            cell_count,
        )
        bias_backs.append(sums)
        label = ["first", "second"][group]
        return [
            Reduction(label + " upper", cell_bits, [y_bit, z_bit] + rest, *halves[:2]),
            Reduction(label + " lower", cell_bits, [z_bit, y_bit] + rest, *halves[2:]),
        ], halves[0]

    def attend_group(c, group, last):
        qkv, out = kept[c]
        back = attend_backward(
            scalars,
            c,
            qkv[group],
            out,
            order_after(back_arrays, last),
            back_places,
            groups[group][0],
            head_size,
        )
        mixed_back[group].append(back)
        return back

    def normed_reduction(c, last):
        *parts, sums = normed_back(
            weights_turned, [order_after(mixed_back[g][c], last) for g in range(2)], blocks[c]
        )
        first_sums.append(sums)
        back_normed.append(PositionSum(parts))
        return sums

    for c in range(cells_here):
        final = c == cells_here - 1
        last = attend_group(c, 0, last)
        if final:
            last = advance(running, last)
            last = out_part.step(last)
            for earlier in range(c):
                last = normed_reduction(earlier, last)
            parts, last = mix_reductions(0, last)
            mix_parts.append(parts)
        last = attend_group(c, 1, last)
        if c == 0:
            last = advance(running, last)
    for part in back_normed:
        last = part.step(last)
    while len(out_part.order) >= len(cell_bits):
        last = out_part.step(last)
    parts, last = mix_reductions(1, last)
    mix_parts.append(parts + [out_part])
    last = advance(mix_parts[0], last)
    done = [part.got for part in running if part.labels and not part.order]
    last = normed_reduction(cells_here - 1, (last, done))
    vectors = VectorSum(
        vector_blocks(
            scalars,
            order_after(first_sums, last),
            bias_backs,
            middle_sums,
            up_bias_back,
            heads_here,
            head_size,
            seq_count,
            cell_count,
        ),
        seq_count,
    )
    last = advance(mix_parts[1], (last, [part.got for part in back_normed[:-1]]))
    last = vectors.step(last)
    last = advance(mix_parts[0], last)
    last = back_normed[-1].step(last)
    last = vectors.step(last)
    last = advance(mix_parts[1], last)
    last = vectors.step(last)
    while any(part.bits for part in back_normed):
        for part in back_normed:
            last = part.step(last) if part.bits else last
    running += mix_parts[0] + mix_parts[1]
    running = [part for part in running if part.labels]
    while any(part.order for part in running):
        last = advance(running, last)
    while vectors.order:
        last = vectors.step(last)
    terms = [x for part in back_normed for x in part.terms()]
    tokens_gradient = tokens_back(
        tokens_turned, first_gain, back_middle, order_after(terms, last)
    )
    last = tokens_gradient
    joined = vectors.step(last)[0]
    vectors = [*(joined[n] for n in range(7)), joined[8:].reshape(-1), joined[7]]
    blocks = {}
    for part in running:
        blocks.update(part.finish(last))
    low = blocks["both"].shape[0] // 2

    def ungrouped(block, starts, share):
        pieces = jnp.split(block, len(starts), axis=1)
        cuts = [share * n - start for n, start in enumerate(starts)]
        return jnp.concatenate([p[c : c + share] for p, c in zip(pieces, cuts)])

    down_part = jnp.concatenate([blocks["down"], blocks["both"][:low]])
    down_share = width // seq_count
    down_starts, _ = row_cover(down_share, cell_count // seq_count)
    down_part = ungrouped(down_part, down_starts, down_share // len(down_starts))
    up_part = jnp.concatenate([blocks["up"], blocks["both"][low:]])
    mix_part = jnp.concatenate(
        [
            jnp.concatenate([blocks[g + " upper"], blocks[g + " lower"]])
            for g in ("first", "second")
        ],
        axis=1,
    )
    mix_part = mix_columns(
        scalars,
        gathered_blocks(mix_part.astype(jnp.bfloat16), seq_count),
        heads_here,
        head_size,
    )
    group = blocks["out"].shape[0]
    out_groups = blocks["out"].shape[1] * seq_count // width
    out_part = blocks["out"][:, : out_groups * (width // seq_count)]
    out_part = ungrouped(out_part, [group * n for n in range(out_groups)], group)

    def own_rows_of(part, unit=16):
        starts, _ = row_cover(width, cell_count, unit)
        share = width // cell_count
        shift = jnp.array([share * c - starts[c] for c in range(cell_count)])[me[1]]
        return lax.dynamic_slice_in_dim(part, shift, share, axis=0)

    matrices = (
        own_rows_of(mix_part),
        own_rows_of(out_part, 16 * out_groups),
        own_rows_of(up_part),
        down_part.T,
    )
    return (
        block_out.transpose(0, 2, 1),
        tokens_gradient.transpose(0, 2, 1),
        vectors[0],
        vectors[1],
        matrices[0],
        vectors[2],
        vectors[3],
        matrices[1],
        vectors[4],
        vectors[5],
        vectors[6],
        matrices[2],
        vectors[7],
        matrices[3],
        vectors[8],
    )


def solution(mesh):
    return jax.shard_map(
        on_device,
        mesh=mesh,
        in_specs=(
            P("cells", "seq", None),
            P(),
            P(),
            P(),
            P(),
            P(),
            P(),
            P(),
            P(),
            P(),
            P(),
            P(),
            P(),
            P(),
            P("cells", "seq", None),
            P("cells"),
            P("cells"),
            P("cells", "seq"),
        ),
        out_specs=(
            P("cells", "seq", None),
            P("cells", "seq", None),
            P("cells"),
            P("cells"),
            P("cells", "seq"),
            P("cells"),
            P("cells"),
            P("cells", "seq"),
            P("cells"),
            P("cells"),
            P("cells"),
            P("cells", "seq"),
            P("cells"),
            P("cells", "seq"),
            P("cells"),
        ),
        check_vma=False,
    )
```
